32 devices in a mesh: dp: 16 (over z, y, core), tensor: 2 (over x).
Axes of the slice: x: 2, y: 2, z: 4, core: 2. Of those that a mesh axis runs over, the one named last changes fastest.
Arguments:
- tokens: bfloat16 [16384, 1024], P('dp'), may hold values from -6 to 6
- lengths: int32 [16, 23], P('dp'), may hold values from 0 to 197, as said below
- norm1_gain: float32 [1024], replicated, may hold values from 0.5 to 1.5
- norm1_bias: float32 [1024], replicated, may hold values from -1.5 to 1.5
- qkv_weight: bfloat16 [3, 1024, 1024], P(None, None, 'tensor'), may hold values from -0.1875 to 0.1875
- qv_bias: float32 [2, 16, 64], P(None, 'tensor'), may hold values from -2.5 to 2.5
- proj_weight: bfloat16 [1024, 1024], P('tensor'), may hold values from -0.75 to 0.75
- proj_bias: float32 [1024], replicated, may hold values from -2.5 to 2.5
- scale_attn: float32 [1024], replicated, may hold values from 0.5 to 2
- norm2_gain: float32 [1024], replicated, may hold values from 0.5 to 1.5
- norm2_bias: float32 [1024], replicated, may hold values from -1.5 to 1.5
- fc1_weight: bfloat16 [1024, 4096], P(None, 'tensor'), may hold values from -0.1875 to 0.1875
- fc1_bias: float32 [4096], P('tensor'), may hold values from -2.5 to 2.5
- fc2_weight: bfloat16 [4096, 1024], P('tensor'), may hold values from -0.125 to 0.125
- fc2_bias: float32 [1024], replicated, may hold values from -2.5 to 2.5
- scale_mlp: float32 [1024], replicated, may hold values from 0.5 to 2
- cotangent: bfloat16 [16384, 1024], P('dp'), may hold values from -6 to 6
Outputs:
- output: bfloat16 [16384, 1024], P('dp')
- grad_tokens: bfloat16 [16384, 1024], P('dp')
- norm1_gain_grad: float32 [1024], P(('dp', 'tensor'))
- norm1_bias_grad: float32 [1024], P(('dp', 'tensor'))
- qkv_weight_grad: float32 [3, 1024, 1024], P(None, 'dp', 'tensor')
- qv_bias_grad: float32 [2, 16, 64], P(None, 'tensor', 'dp')
- proj_weight_grad: float32 [1024, 1024], P('tensor', 'dp')
- proj_bias_grad: float32 [1024], P(('dp', 'tensor'))
- scale_attn_grad: float32 [1024], P(('dp', 'tensor'))
- norm2_gain_grad: float32 [1024], P(('dp', 'tensor'))
- norm2_bias_grad: float32 [1024], P(('dp', 'tensor'))
- fc1_weight_grad: float32 [1024, 4096], P('dp', 'tensor')
- fc1_bias_grad: float32 [64, 64], P('tensor', 'dp')
- fc2_weight_grad: float32 [4096, 1024], P('tensor', 'dp')
- fc2_bias_grad: float32 [1024], P(('dp', 'tensor'))
- scale_mlp_grad: float32 [1024], P(('dp', 'tensor'))
The draws below stay inside these ranges and needn't reach their ends.
Inputs may be any that keep to these rules, and one draw needn't show every extreme that they name: Each packed row's lengths are one or more 197, then zero or more 37, then zeros; a row's lengths add up to at most 1024.
All inputs are finite; a program needn't handle non-finite values.
Results may differ from the reference program's by a relative error of at most 0.02.
Values may be sent and summed in bfloat16 or wider, within the bound.
No kernel may reach another device: no remote copies, remote signals or barrier semaphores. Data moves between devices by JAX's collectives and lax.ppermute only.
A program may use at most 256 MiB of HBM per device.

```python
import math
import jax
import jax.numpy as jnp
from jax import lax

D = 1024
HEADS = 16
HEAD_DIM = 64
FF = 4096
PACK = 1024
GLOBAL_LEN = 197
LOCAL_LEN = 37
SLOTS = 23
PROWS = 16
TOKENS = 16384
N_TENSOR = 2


def draw_lengths(key, part):
    key = jax.random.fold_in(key, 7)
    key_global, key_local = jax.random.split(key)
    global_count = jax.random.randint(key_global, (PROWS, 1), 1, PACK // GLOBAL_LEN + 1)
    spare_room = (PACK - global_count * GLOBAL_LEN) // LOCAL_LEN
    raw_count = jax.random.randint(key_local, (PROWS, 1), 0, 1 << 20)
    local_count = raw_count % (spare_room + 1)
    slot_index = jnp.arange(SLOTS, dtype=jnp.int32)[None, :]
    lengths = jnp.where(slot_index < global_count, GLOBAL_LEN, jnp.where(slot_index < global_count + local_count, LOCAL_LEN, 0))
    return lengths.astype(jnp.int32)


def block_levels(key, dims, shards, smallest, top_value):
    level = 1.0
    for dim, parts in shards:
        steps = jax.random.uniform(jax.random.fold_in(jax.random.fold_in(key, 6), dim), (parts,), jnp.float32, smallest / len(shards), top_value / len(shards))
        level = level * jnp.repeat(jnp.exp(steps), dims[dim] // parts).reshape((-1,) + (1,) * (len(dims) - 1 - dim))
    return level


def centred(rng, dims, spread, most, shards=(), held_as=jnp.bfloat16):
    entries = jax.random.normal(rng, dims, jnp.float32) * spread
    if len(shards) > 0:
        entries = block_levels(rng, dims, shards, -0.22, 0.18) * entries
    return jnp.clip(entries, min=-most, max=most).astype(held_as)


def setup_inputs(seed: int = 0) -> dict:
    key_list = jax.random.split(jax.random.key(seed), 18)
    tokens = centred(key_list[0], (TOKENS, D), 1.0, 6.0, ((0, 16),))
    lengths = draw_lengths(jax.random.fold_in(key_list[17], 71), 0)
    norm1_gain = jnp.clip(1.0 + 0.1 * jax.random.normal(key_list[2], (D,), jnp.float32), 0.5, 1.5)
    norm1_bias = centred(key_list[3], (D,), 0.3, 1.5, (), jnp.float32)
    qkv_weight = centred(key_list[4], (3, D, D), D ** -0.5, 0.1875, ((2, 2),))
    qv_bias = centred(key_list[5], (2, HEADS, HEAD_DIM), 0.5, 2.5, ((1, 2),), jnp.float32)
    proj_weight = centred(key_list[6], (D, D), (D // 16) ** -0.5, 0.75, ((0, 2),))
    proj_bias = centred(key_list[7], (D,), 0.5, 2.5, (), jnp.float32)
    scale_attn = jnp.clip(jnp.exp(jax.random.uniform(key_list[8], (D,), jnp.float32, math.log(0.5), math.log(2.0))), 0.5, 2.0)
    norm2_gain = jnp.clip(1.0 + 0.1 * jax.random.normal(key_list[9], (D,), jnp.float32), 0.5, 1.5)
    norm2_bias = centred(key_list[10], (D,), 0.3, 1.5, (), jnp.float32)
    fc1_weight = centred(key_list[11], (D, FF), D ** -0.5, 0.1875, ((1, 2),))
    fc1_bias = centred(key_list[12], (FF,), 0.5, 2.5, ((0, 2),), jnp.float32)
    fc2_weight = centred(key_list[13], (FF, D), (FF // 2) ** -0.5, 0.125, ((0, 2),))
    fc2_bias = centred(key_list[14], (D,), 0.5, 2.5, (), jnp.float32)
    scale_mlp = jnp.clip(jnp.exp(jax.random.uniform(key_list[15], (D,), jnp.float32, math.log(0.5), math.log(2.0))), 0.5, 2.0)
    cotangent = centred(key_list[16], (TOKENS, D), 1.0, 6.0, ((0, 16),))
    return {"tokens": tokens, "lengths": lengths, "norm1_gain": norm1_gain, "norm1_bias": norm1_bias, "qkv_weight": qkv_weight, "qv_bias": qv_bias, "proj_weight": proj_weight, "proj_bias": proj_bias, "scale_attn": scale_attn, "norm2_gain": norm2_gain, "norm2_bias": norm2_bias, "fc1_weight": fc1_weight, "fc1_bias": fc1_bias, "fc2_weight": fc2_weight, "fc2_bias": fc2_bias, "scale_mlp": scale_mlp, "cotangent": cotangent}


HIGHEST = lax.Precision.HIGHEST
EPS = 1e-06
NEGATIVE = -1e+30

@jax.custom_vjp
def low(v):
    return lax.optimization_barrier(v.astype(jnp.bfloat16)).astype(jnp.float32)

@jax.custom_vjp
def low_back(v):
    return v

def low_keep(v):
    return (low(v), None)

def low_pass(kept, grad):
    return (grad,)

def back_keep(v):
    return (v, None)

def back_low(kept, grad):
    return (low(grad),)
low.defvjp(low_keep, low_pass)
low_back.defvjp(back_keep, back_low)

def layer_norm(values, gain, shift):
    average = lax.optimization_barrier(jnp.mean(values, axis=-1, keepdims=True))
    centered = values - average
    variance = lax.optimization_barrier(jnp.mean(centered * centered, axis=-1, keepdims=True))
    return centered * lax.rsqrt(variance + EPS) * gain + shift

def segment_row(lengths_row):
    finish = jnp.cumsum(lengths_row)
    places = jnp.arange(PACK, dtype=jnp.int32)
    labels = lax.optimization_barrier(jnp.sum((finish[None, :] <= places[:, None]).astype(jnp.int32), axis=1))
    return jnp.where(places < finish[-1], labels, -1).astype(jnp.int32)

def attend_row(row_items):
    queries, key_rows, values, labels = row_items
    block_rows = min(512, PACK)
    block_count = PACK // block_rows
    score_scale = HEAD_DIM ** (-0.5)

    def one_block(block_items):
        query_part, label_part = block_items
        scores = low_back(jnp.einsum('qhc,khc->hqk', query_part, key_rows, precision=HIGHEST) * score_scale)
        allowed = (label_part[:, None] == labels[None, :]) & (labels[None, :] >= 0)
        scores = jnp.where(allowed[None], scores, NEGATIVE)
        row_top = lax.optimization_barrier(jnp.max(scores, axis=-1, keepdims=True))
        weights = jnp.exp(scores - row_top)
        probability = weights / lax.optimization_barrier(jnp.sum(weights, axis=-1, keepdims=True))
        return jnp.einsum('hqk,khc->qhc', low(probability), values, precision=HIGHEST)
    mixed = lax.map(jax.checkpoint(one_block), (queries.reshape(block_count, block_rows, HEADS, HEAD_DIM), labels.reshape(block_count, block_rows)))
    return mixed.reshape(PACK, HEADS, HEAD_DIM)

def layer(params, inputs, labels, valid):
    norm1_gain, norm1_bias, qkv_weight, qv_bias, proj_weight, proj_bias, scale_attn, norm2_gain, norm2_bias, fc1_weight, fc1_bias, fc2_weight, fc2_bias, scale_mlp = params
    groups = N_TENSOR
    group_width = D // groups
    hidden_width = FF // groups
    row_count = inputs.shape[0]
    normed1 = low(layer_norm(inputs, norm1_gain, norm1_bias))
    copies1 = low_back(jnp.broadcast_to(normed1[None], (groups, row_count, D)))
    projected = jnp.einsum('gtd,sdgc->stgc', copies1, qkv_weight.reshape(3, D, groups, group_width), precision=HIGHEST)
    biases = qv_bias.reshape(2, groups, group_width)
    queries = low(low_back(projected[0]) + biases[0])
    key_rows = low(low_back(projected[1]))
    values = low(low_back(projected[2]) + biases[1])
    packed = row_count // PACK

    def shaped(array):
        return array.reshape(packed, PACK, HEADS, HEAD_DIM)
    mixed = lax.map(attend_row, (shaped(queries), shaped(key_rows), shaped(values), labels))
    mixed = low(low_back(mixed.reshape(row_count, groups, group_width)))
    attn_parts = jnp.einsum('tgc,gcd->gtd', mixed, proj_weight.reshape(groups, group_width, D), precision=HIGHEST)
    attn_out = low_back(lax.optimization_barrier(jnp.sum(low(attn_parts), axis=0))) + proj_bias
    middle = inputs + scale_attn * attn_out
    normed2 = low(layer_norm(middle, norm2_gain, norm2_bias))
    copies2 = low_back(jnp.broadcast_to(normed2[None], (groups, row_count, D)))
    hidden = jnp.einsum('gtd,dgf->tgf', copies2, fc1_weight.reshape(D, groups, hidden_width), precision=HIGHEST)
    hidden = low_back(hidden) + fc1_bias.reshape(groups, hidden_width)
    activated = low(jax.nn.gelu(hidden, approximate=False))
    mlp_parts = jnp.einsum('tgf,gfd->gtd', activated, fc2_weight.reshape(groups, hidden_width, D), precision=HIGHEST)
    mlp_out = low_back(lax.optimization_barrier(jnp.sum(low(mlp_parts), axis=0))) + fc2_bias
    return (middle + scale_mlp * mlp_out) * valid[:, None]

def reference(tokens, lengths, norm1_gain, norm1_bias, qkv_weight, qv_bias, proj_weight, proj_bias, scale_attn, norm2_gain, norm2_bias, fc1_weight, fc1_bias, fc2_weight, fc2_bias, scale_mlp, cotangent):
    params = tuple((array.astype(jnp.float32) for array in (norm1_gain, norm1_bias, qkv_weight, qv_bias, proj_weight, proj_bias, scale_attn, norm2_gain, norm2_bias, fc1_weight, fc1_bias, fc2_weight, fc2_bias, scale_mlp)))
    per_block = math.gcd(PROWS, max(1, 4096 // PACK))
    block_count = PROWS // per_block
    labels = jax.vmap(segment_row)(lengths)
    token_blocks = tokens.astype(jnp.float32).reshape(block_count, per_block * PACK, D)
    label_blocks = labels.reshape(block_count, per_block, PACK)
    grad_blocks = cotangent.astype(jnp.float32).reshape(block_count, per_block * PACK, D)

    def one_step(totals, step_items):
        block_tokens, block_labels, block_grad = step_items
        valid = (block_labels.reshape(-1) >= 0).astype(jnp.float32)
        result, backward = jax.vjp(lambda weights, inputs: layer(weights, inputs, block_labels, valid), params, block_tokens)
        grad_weights, grad_inputs = backward(block_grad)
        totals = jax.tree.map(jnp.add, totals, grad_weights)
        return (totals, (result.astype(jnp.bfloat16), grad_inputs.astype(jnp.bfloat16)))
    zeros = jax.tree.map(jnp.zeros_like, params)
    totals, (outputs, grad_inputs) = lax.scan(one_step, zeros, (token_blocks, label_blocks, grad_blocks))
    g_norm1_gain, g_norm1_bias, g_qkv, g_qv_bias, g_proj, g_proj_bias, g_scale_attn, g_norm2_gain, g_norm2_bias, g_fc1, g_fc1_bias, g_fc2, g_fc2_bias, g_scale_mlp = totals
    return (outputs.reshape(TOKENS, D), grad_inputs.reshape(TOKENS, D), g_norm1_gain, g_norm1_bias, g_qkv, g_qv_bias, g_proj, g_proj_bias, g_scale_attn, g_norm2_gain, g_norm2_bias, g_fc1, g_fc1_bias.reshape(FF // HEAD_DIM, HEAD_DIM), g_fc2, g_fc2_bias, g_scale_mlp)
```

```python
from functools import partial

import jax
import jax.numpy as jnp
from jax import lax
from jax.experimental import pallas as pl
from jax.experimental.pallas import tpu as pltpu
from jax.sharding import PartitionSpec as P

EPS = 1e-06
NEGATIVE = -1e30
GLOBAL_LEN = 197
LOCAL_LEN = 37
GROUP = GLOBAL_LEN // LOCAL_LEN
WINDOW = 224
BF16 = jnp.bfloat16
F32 = jnp.float32
MIB = 1 << 20


def dot_nn(a, b):
    return lax.dot_general(a, b, (((1,), (0,)), ((), ())), preferred_element_type=F32)


def dot_nt(a, b):
    return lax.dot_general(a, b, (((1,), (1,)), ((), ())), preferred_element_type=F32)


def dot_tn(a, b):
    return lax.dot_general(a, b, (((0,), (0,)), ((), ())), preferred_element_type=F32)


def norm_parts(values):
    average = jnp.mean(values, axis=-1, keepdims=True)
    centered = values - average
    inverse = lax.rsqrt(jnp.mean(centered * centered, axis=-1, keepdims=True) + EPS)
    return centered * inverse, inverse


def norm_back(grad_norm, scaled, inverse, gain):
    grad_hat = grad_norm * gain
    first_mean = jnp.mean(grad_hat, axis=-1, keepdims=True)
    second_mean = jnp.mean(grad_hat * scaled, axis=-1, keepdims=True)
    return inverse * (grad_hat - first_mean - scaled * second_mean)


def col_sum(values):
    return jnp.sum(values, axis=0, keepdims=True)


def call(kernel, name, grid, in_specs, out_specs, out_shape, args, flops, scratch=(), vmem=48, alias=None):
    moved = sum(a.size * a.dtype.itemsize for a in args) + sum(
        o.size * jnp.dtype(o.dtype).itemsize for o in jax.tree.leaves(out_shape)
    )
    return pl.pallas_call(
        kernel,
        grid=grid,
        in_specs=in_specs,
        out_specs=out_specs,
        out_shape=out_shape,
        scratch_shapes=scratch,
        input_output_aliases=alias or {},
        compiler_params=pltpu.CompilerParams(vmem_limit_bytes=vmem * MIB),
        cost_estimate=pl.CostEstimate(flops=int(flops), bytes_accessed=int(moved), transcendentals=0),
        name=name,
    )(*args)


def shape(dims, dtype):
    return jax.ShapeDtypeStruct(dims, dtype)


def whole(array):
    zeros = (0,) * array.ndim
    return pl.BlockSpec(array.shape, lambda *_: zeros)


SMEM = pl.BlockSpec(memory_space=pltpu.SMEM)


def row_total(lengths_ref):
    total = jnp.int32(0)
    for slot in range(lengths_ref.shape[1]):
        total = total + lengths_ref[0, slot]
    return total


def valid_rows(lengths_ref, first, rows):
    places = lax.broadcasted_iota(jnp.int32, (rows, 1), 0) + first
    return (places < row_total(lengths_ref)).astype(F32)


def project(tokens, gain, bias, weight, qv_bias, scale):
    count, width = tokens.shape
    local = weight.shape[2]
    rows = 256

    def kernel(x_ref, gain_ref, bias_ref, w_ref, qv_ref, q_ref, k_ref, v_ref, n_ref):
        scaled, _ = norm_parts(x_ref[...].astype(F32))
        normed = (scaled * gain_ref[...] + bias_ref[...]).astype(BF16)
        n_ref[...] = normed
        queries = (dot_nn(normed, w_ref[0]) + qv_ref[0:1]).astype(BF16)
        q_ref[...] = queries * BF16(scale)
        k_ref[...] = dot_nn(normed, w_ref[1]).astype(BF16)
        v_ref[...] = (dot_nn(normed, w_ref[2]) + qv_ref[1:2]).astype(BF16)

    by_row = pl.BlockSpec((rows, width), lambda i: (i, 0))
    by_row_local = pl.BlockSpec((rows, local), lambda i: (i, 0))
    part = shape((count, local), BF16)
    return call(
        kernel,
        "project",
        (count // rows,),
        [by_row, whole(gain), whole(bias), whole(weight), whole(qv_bias)],
        [by_row_local, by_row_local, by_row_local, by_row],
        [part, part, part, shape((count, width), BF16)],
        (tokens, gain, bias, weight, qv_bias),
        2 * count * width * 3 * local,
    )


def item_counts(lengths_ref):
    globals_ = jnp.int32(0)
    locals_ = jnp.int32(0)
    for slot in range(lengths_ref.shape[1]):
        value = lengths_ref[0, slot]
        globals_ = globals_ + jnp.where(value == GLOBAL_LEN, 1, 0)
        locals_ = locals_ + jnp.where(value == LOCAL_LEN, 1, 0)
    return globals_, locals_


def item_place(item, globals_, locals_, count):
    is_global = item < globals_
    group = item - globals_
    start = jnp.where(
        is_global, item * GLOBAL_LEN, globals_ * GLOBAL_LEN + group * (GROUP * LOCAL_LEN)
    )
    length = jnp.where(
        is_global, GLOBAL_LEN, jnp.minimum(locals_ - group * GROUP, GROUP) * LOCAL_LEN
    )
    crop = jnp.where(is_global, GLOBAL_LEN, LOCAL_LEN)
    first = jnp.minimum((start // 16) * 16, count - WINDOW)
    return pl.multiple_of(first, 16), start - first, length, crop


def crop_of(places, offset, length, crop, outside):
    inside = (places >= offset) & (places < offset + length)
    index = places - offset
    label = jnp.zeros_like(places)
    for step in range(1, GROUP):
        label = label + jnp.where(index >= step * crop, 1, 0)
    return jnp.where(inside, label, outside)


def item_total(globals_, locals_):
    return globals_ + (locals_ + GROUP - 1) // GROUP


def attend_forward(queries, keys, values, lengths):
    count, local = queries.shape
    head = 64
    pair = 2 * head

    def kernel(q_ref, k_ref, v_ref, lengths_ref, out_ref):
        globals_, locals_ = item_counts(lengths_ref)
        average = col_sum(v_ref[...].astype(F32)) * (1.0 / count)
        out_ref[...] = jnp.broadcast_to(average, (count, local)).astype(BF16)
        low_half = lax.broadcasted_iota(jnp.int32, (1, pair), 1) < head

        def step(item, carry):
            first, offset, length, crop = item_place(item, globals_, locals_, count)
            window = pl.ds(first, WINDOW)
            by_query = lax.broadcasted_iota(jnp.int32, (WINDOW, 1), 0)
            by_key = lax.broadcasted_iota(jnp.int32, (1, WINDOW), 1)
            query_crop = crop_of(by_query, offset, length, crop, -2)
            key_crop = crop_of(by_key, offset, length, crop, -1)
            mask = jnp.where(query_crop == key_crop, 0.0, NEGATIVE)
            inside = query_crop >= 0
            for index in range(local // pair):
                columns = slice(index * pair, (index + 1) * pair)
                q2 = q_ref[window, columns]
                k2 = k_ref[window, columns]
                v2 = v_ref[window, columns]
                out = None
                for keep in (low_half, jnp.logical_not(low_half)):
                    kept_k = jnp.where(keep, k2, BF16(0))
                    kept_v = jnp.where(keep, v2, BF16(0))
                    scores = dot_nt(q2, kept_k) + mask
                    weights = jnp.exp(scores - jnp.max(scores, axis=1, keepdims=True))
                    total = jnp.sum(weights, axis=1, keepdims=True)
                    low = (weights * (1.0 / total)).astype(BF16)
                    term = dot_nn(low, kept_v)
                    out = term if out is None else out + term
                out_ref[window, columns] = jnp.where(
                    inside, out, out_ref[window, columns].astype(F32)
                ).astype(BF16)
            return carry

        lax.fori_loop(0, item_total(globals_, locals_), step, 0)

    vm = pl.BlockSpec(memory_space=pltpu.VMEM)
    return call(
        kernel,
        "attend_forward",
        (),
        [vm, vm, vm, SMEM],
        vm,
        shape((count, local), BF16),
        (queries, keys, values, lengths),
        4 * count * local * WINDOW,
    )


def attend_backward(queries, keys, values, grad_mixed, lengths, scale):
    count, local = queries.shape
    head = 64
    pair = 2 * head

    def kernel(q_ref, k_ref, v_ref, g_ref, lengths_ref, out_ref, bias_ref, acc_ref):
        globals_, locals_ = item_counts(lengths_ref)
        acc_ref[...] = jnp.zeros_like(acc_ref)
        low_half = lax.broadcasted_iota(jnp.int32, (1, pair), 1) < head

        def step(item, carry):
            first, offset, length, crop = item_place(item, globals_, locals_, count)
            window = pl.ds(first, WINDOW)
            by_key = lax.broadcasted_iota(jnp.int32, (WINDOW, 1), 0)
            by_query = lax.broadcasted_iota(jnp.int32, (1, WINDOW), 1)
            query_crop = crop_of(by_query, offset, length, crop, -2)
            key_crop = crop_of(by_key, offset, length, crop, -1)
            mask = jnp.where(query_crop == key_crop, 0.0, NEGATIVE)
            inside = key_crop >= 0
            for index in range(local // pair):
                columns = slice(index * pair, (index + 1) * pair)
                q2 = q_ref[window, columns]
                k2 = k_ref[window, columns]
                v2 = v_ref[window, columns]
                g2 = jnp.where(inside, g_ref[window, columns], BF16(0))
                grad_q = grad_k = grad_v = None
                for keep in (low_half, jnp.logical_not(low_half)):
                    kept_k = jnp.where(keep, k2, BF16(0))
                    kept_v = jnp.where(keep, v2, BF16(0))
                    kept_q = jnp.where(keep, q2, BF16(0))
                    kept_g = jnp.where(keep, g2, BF16(0))
                    scores = dot_nt(kept_k, q2) + mask
                    weights = jnp.exp(scores - jnp.max(scores, axis=0, keepdims=True))
                    total = jnp.sum(weights, axis=0, keepdims=True)
                    probability = weights * (1.0 / total)
                    grad_probability = dot_nt(kept_v, g2)
                    delta = jnp.sum(probability * grad_probability, axis=0, keepdims=True)
                    grad_scores = (probability * (grad_probability - delta)).astype(BF16)
                    term_v = dot_nn(probability.astype(BF16), kept_g)
                    term_k = dot_nn(grad_scores, kept_q)
                    term_q = dot_tn(grad_scores, kept_k)
                    grad_v = term_v if grad_v is None else grad_v + term_v
                    grad_k = term_k if grad_k is None else grad_k + term_k
                    grad_q = term_q if grad_q is None else grad_q + term_q
                acc_ref[0, window, columns] += grad_q * scale
                acc_ref[1, window, columns] += grad_k
                acc_ref[2, window, columns] += grad_v
            return carry

        lax.fori_loop(0, item_total(globals_, locals_), step, 0)
        for part in range(3):
            out_ref[:, part * local : (part + 1) * local] = acc_ref[part].astype(BF16)
        bias_ref[0:1] = col_sum(acc_ref[0])
        bias_ref[1:2] = col_sum(acc_ref[2])

    vm = pl.BlockSpec(memory_space=pltpu.VMEM)
    return call(
        kernel,
        "attend_backward",
        (),
        [vm, vm, vm, vm, SMEM],
        [vm, vm],
        [shape((count, 3 * local), BF16), shape((2, local), F32)],
        (queries, keys, values, grad_mixed, lengths),
        10 * count * local * WINDOW,
        scratch=[pltpu.VMEM((3, count, local), F32)],
    )


def gelu_parts(value):
    size = jnp.abs(value)
    bell = jnp.exp(value * value * -0.5)
    t = 1.0 / (1.0 + size * (0.3275911 * 0.7071067811865476))
    poly = t * (
        0.254829592
        + t * (-0.284496736 + t * (1.421413741 + t * (-1.453152027 + t * 1.061405429)))
    )
    tail = 0.5 * poly * bell
    share = jnp.where(value >= 0, 1.0 - tail, tail)
    return value * share, share + value * (bell * 0.3989422804014327)


def feed_forward(chunk, rows, mixed, projs, tokens, cotangent, lengths, vectors, fc1, fc1_bias, fc2, kept):
    proj_bias, scale_attn, gain, bias, scale_mlp = vectors
    count, width = tokens.shape
    units = fc1.shape[1]
    step_units = min(512, units)
    steps = units // step_units
    parts = len(mixed)
    n_kept = 0 if kept is None else len(kept)

    def kernel(*refs):
        mixed_refs, refs = refs[:parts], refs[parts:]
        proj_refs, refs = refs[:parts], refs[parts:]
        x_ref, c_ref, lengths_ref, refs = refs[0], refs[1], refs[2], refs[3:]
        pb_ref, sa_ref, gain_ref, bias_ref, sm_ref, refs = *refs[:5], refs[5:]
        fc1_ref, fb_ref, fc2_ref, refs = refs[0], refs[1], refs[2], refs[3:]
        refs = refs[n_kept:]
        mid_ref, n2_ref, gm_ref, act_ref, gh_ref, fbg_ref, terms_ref, vec_ref, acc_ref = refs
        j = pl.program_id(0)

        @pl.when(j == 0)
        def _():
            attn = pb_ref[...]
            for m_ref, p_ref in zip(mixed_refs, proj_refs):
                attn = attn + dot_nn(m_ref[...], p_ref[...]).astype(BF16).astype(F32)
            middle = x_ref[...].astype(F32) + sa_ref[...] * attn
            mid_ref[...] = middle
            scaled, _ = norm_parts(middle)
            n2_ref[...] = (scaled * gain_ref[...] + bias_ref[...]).astype(BF16)
            grad = c_ref[...].astype(F32) * valid_rows(lengths_ref, chunk * rows, rows)
            gm_ref[...] = (grad * sm_ref[...]).astype(BF16)

        hidden = dot_nn(n2_ref[...], fc1_ref[...]) + fb_ref[...]
        activated, slope = gelu_parts(hidden)
        act_ref[...] = activated.astype(BF16)
        grad_hidden = dot_nt(gm_ref[...], fc2_ref[...]) * slope
        fbg_ref[...] = col_sum(grad_hidden)
        low = grad_hidden.astype(BF16)
        gh_ref[...] = low
        term = dot_nt(low, fc1_ref[...])

        @pl.when(j == 0)
        def _():
            acc_ref[...] = term

        @pl.when(j > 0)
        def _():
            acc_ref[...] += term

        @pl.when(j == steps - 1)
        def _():
            low_terms = acc_ref[...].astype(BF16)
            terms_ref[...] = low_terms
            wide = low_terms.astype(F32)
            scaled, _ = norm_parts(mid_ref[...])
            vec_ref[0:1] = col_sum(wide * scaled)
            vec_ref[1:2] = col_sum(wide)

    def of_chunk(w):
        return pl.BlockSpec((rows, w), lambda j: (chunk, 0))

    once = pl.BlockSpec((rows, mixed[0].shape[1]), lambda j: (0, 0))
    mixed_specs = [of_chunk(m.shape[1]) if m.shape[0] == count else once for m in mixed]
    row = pl.BlockSpec((1, width), lambda j: (0, 0))
    unit_block = pl.BlockSpec((rows, step_units), lambda j: (chunk, j))
    any_spec = pl.BlockSpec(memory_space=pl.ANY)
    args = (
        *mixed,
        *projs,
        tokens,
        cotangent,
        lengths,
        proj_bias,
        scale_attn,
        gain,
        bias,
        scale_mlp,
        fc1,
        fc1_bias,
        fc2,
    )
    alias = None
    if kept is not None:
        alias = {len(args) + i: i for i in range(n_kept)}
        args = args + tuple(kept)
    return call(
        kernel,
        "feed_forward",
        (steps,),
        mixed_specs
        + [whole(p) for p in projs]
        + [of_chunk(width), of_chunk(width), SMEM]
        + [row] * 5
        + [
            pl.BlockSpec((width, step_units), lambda j: (0, j)),
            pl.BlockSpec((1, step_units), lambda j: (0, j)),
            pl.BlockSpec((step_units, width), lambda j: (j, 0)),
        ]
        + [any_spec] * n_kept,
        [
            of_chunk(width),
            of_chunk(width),
            of_chunk(width),
            unit_block,
            unit_block,
            pl.BlockSpec((1, step_units), lambda j: (0, j)),
            pl.BlockSpec((rows, width), lambda j: (0, 0)),
            pl.BlockSpec((2, width), lambda j: (0, 0)),
        ],
        [
            shape((count, width), F32),
            shape((count, width), BF16),
            shape((count, width), BF16),
            shape((count, units), BF16),
            shape((count, units), BF16),
            shape((1, units), F32),
            shape((rows, width), BF16),
            shape((2, width), F32),
        ],
        args,
        2 * rows * width * (3 * units + parts * mixed[0].shape[1]),
        scratch=[pltpu.VMEM((rows, width), F32)],
        vmem=56,
        alias=alias,
    )


def second_projection(chunk, rows, activated, fc2, cotangent, lengths, scale_mlp):
    count, units = activated.shape
    width = fc2.shape[1]
    block = 256
    steps = rows // block

    def kernel(a_ref, w_ref, c_ref, lengths_ref, sm_ref, out_ref, vec_ref):
        i = pl.program_id(0)
        terms = dot_nn(a_ref[...], w_ref[...]).astype(BF16)
        out_ref[...] = terms
        grad = c_ref[...].astype(F32) * valid_rows(lengths_ref, chunk * rows + i * block, block)
        first = col_sum(grad * terms.astype(F32))
        second = col_sum(grad)

        @pl.when(i == 0)
        def _():
            vec_ref[0:1] = first
            vec_ref[1:2] = second

        @pl.when(i > 0)
        def _():
            vec_ref[0:1] += first
            vec_ref[1:2] += second

    return call(
        kernel,
        "second_projection",
        (steps,),
        [
            pl.BlockSpec((block, units), lambda i: (chunk * steps + i, 0)),
            whole(fc2),
            pl.BlockSpec((block, width), lambda i: (chunk * steps + i, 0)),
            SMEM,
            whole(scale_mlp),
        ],
        [
            pl.BlockSpec((block, width), lambda i: (i, 0)),
            pl.BlockSpec((2, width), lambda i: (0, 0)),
        ],
        [shape((rows, width), BF16), shape((2, width), F32)],
        (activated, fc2, cotangent, lengths, scale_mlp),
        2 * rows * width * units,
    )


def weight_grads(lefts, rights, step_columns, name):
    count, width = lefts[0].shape
    widths = [r.shape[1] for r in rights]
    step_columns = min([step_columns] + widths)
    starts, total = [], 0
    for w in widths:
        starts.append(total)
        total += w // step_columns
    pairs = len(lefts)

    def kernel(*refs):
        left_refs, right_refs = refs[:pairs], refs[pairs : 2 * pairs]
        out_ref = refs[2 * pairs]
        j = pl.program_id(0)
        for p in range(pairs):
            end = starts[p] + widths[p] // step_columns

            @pl.when((j >= starts[p]) & (j < end))
            def _(p=p):
                out_ref[...] = dot_tn(left_refs[p][...], right_refs[p][...]).astype(BF16)

    def right_spec(p):
        last = widths[p] // step_columns - 1
        return pl.BlockSpec(
            (count, step_columns), lambda j: (0, jnp.clip(j - starts[p], 0, last))
        )

    return call(
        kernel,
        name,
        (total,),
        [whole(l) for l in lefts] + [right_spec(p) for p in range(pairs)],
        pl.BlockSpec((width, step_columns), lambda j: (0, j)),
        shape((width, total * step_columns), BF16),
        (*lefts, *rights),
        2 * count * width * total * step_columns,
    )


def middle_back(terms, middle, tokens, cotangent, lengths, scale_attn, gain, proj):
    count, width = middle.shape
    local = proj.shape[0]
    block = 256
    parts = len(terms[0])
    chunks = len(terms)
    per = count // chunks // block
    flat = [t for group in terms for t in group]

    def kernel(*refs):
        term_refs, refs = refs[: len(flat)], refs[len(flat) :]
        mid_ref, x_ref, c_ref, lengths_ref, sa_ref, gain_ref, p_ref, refs = *refs[:7], refs[7:]
        gmid_ref, low_ref, gmix_ref, vec_ref = refs
        i = pl.program_id(0)
        for chunk in range(chunks):

            @pl.when(i // per == chunk)
            def _(chunk=chunk):
                grad_norm = None
                for part in range(parts):
                    term = term_refs[chunk * parts + part][...].astype(F32)
                    grad_norm = term if grad_norm is None else grad_norm + term
                gmid_ref[...] = grad_norm

        middle = mid_ref[...]
        scaled, inverse = norm_parts(middle)
        grad = c_ref[...].astype(F32) * valid_rows(lengths_ref, i * block, block)
        grad = grad + norm_back(gmid_ref[...], scaled, inverse, gain_ref[...])
        gmid_ref[...] = grad
        low = (sa_ref[...] * grad).astype(BF16)
        low_ref[...] = low
        gmix_ref[...] = dot_nt(low, p_ref[...]).astype(BF16)
        first = col_sum(grad * (middle - x_ref[...].astype(F32)))
        second = col_sum(grad)

        @pl.when(i == 0)
        def _():
            vec_ref[0:1] = first
            vec_ref[1:2] = second

        @pl.when(i > 0)
        def _():
            vec_ref[0:1] += first
            vec_ref[1:2] += second

    def term_spec(chunk):
        return pl.BlockSpec((block, width), lambda i: (jnp.clip(i - chunk * per, 0, per - 1), 0))

    by_row = pl.BlockSpec((block, width), lambda i: (i, 0))
    return call(
        kernel,
        "middle_back",
        (count // block,),
        [term_spec(c) for c in range(chunks) for _ in range(parts)]
        + [by_row, by_row, by_row, SMEM, whole(scale_attn), whole(gain), whole(proj)],
        [
            by_row,
            by_row,
            pl.BlockSpec((block, local), lambda i: (i, 0)),
            pl.BlockSpec((2, width), lambda i: (0, 0)),
        ],
        [
            shape((count, width), F32),
            shape((count, width), BF16),
            shape((count, local), BF16),
            shape((2, width), F32),
        ],
        (*flat, middle, tokens, cotangent, lengths, scale_attn, gain, proj),
        2 * count * width * local,
    )


def first_norm_terms(chunk, rows, grads, weight, tokens):
    count, width = tokens.shape
    local = weight.shape[2]
    block = 256
    steps = rows // block

    def kernel(g_ref, w_ref, x_ref, out_ref, vec_ref):
        i = pl.program_id(0)
        total = None
        for part in range(3):
            term = dot_nt(g_ref[:, part * local : (part + 1) * local], w_ref[part])
            total = term if total is None else total + term
        low = total.astype(BF16)
        out_ref[...] = low
        wide = low.astype(F32)
        scaled, _ = norm_parts(x_ref[...].astype(F32))
        first = col_sum(wide * scaled)
        second = col_sum(wide)

        @pl.when(i == 0)
        def _():
            vec_ref[0:1] = first
            vec_ref[1:2] = second

        @pl.when(i > 0)
        def _():
            vec_ref[0:1] += first
            vec_ref[1:2] += second

    return call(
        kernel,
        "first_norm_terms",
        (steps,),
        [
            pl.BlockSpec((block, 3 * local), lambda i: (chunk * steps + i, 0)),
            whole(weight),
            pl.BlockSpec((block, width), lambda i: (chunk * steps + i, 0)),
        ],
        [
            pl.BlockSpec((block, width), lambda i: (i, 0)),
            pl.BlockSpec((2, width), lambda i: (0, 0)),
        ],
        [shape((rows, width), BF16), shape((2, width), F32)],
        (grads, weight, tokens),
        2 * rows * width * 3 * local,
    )


def token_grads(chunk, rows, terms, grad_middle, tokens, gain, kept):
    count, width = tokens.shape
    block = 256
    steps = rows // block
    parts = len(terms)
    extra = 0 if kept is None else 1

    def kernel(*refs):
        term_refs, refs = refs[:parts], refs[parts:]
        gmid_ref, x_ref, gain_ref = refs[:3]
        out_ref = refs[3 + extra]
        grad_norm = None
        for ref in term_refs:
            term = ref[...].astype(F32)
            grad_norm = term if grad_norm is None else grad_norm + term
        scaled, inverse = norm_parts(x_ref[...].astype(F32))
        grad = gmid_ref[...] + norm_back(grad_norm, scaled, inverse, gain_ref[...])
        out_ref[...] = grad.astype(BF16)

    own = pl.BlockSpec((block, width), lambda i: (i, 0))
    by_row = pl.BlockSpec((block, width), lambda i: (chunk * steps + i, 0))
    args = (*terms, grad_middle, tokens, gain)
    alias = None
    if kept is not None:
        alias = {len(args): 0}
        args = args + (kept,)
    return call(
        kernel,
        "token_grads",
        (steps,),
        [own] * parts
        + [by_row, by_row, whole(gain)]
        + [pl.BlockSpec(memory_space=pl.ANY)] * extra,
        by_row,
        shape((count, width), BF16),
        args,
        0,
        alias=alias,
    )


def layer_output(chunk, rows, terms, middle, lengths, bias, scale, kept):
    count, width = middle.shape
    block = 256
    steps = rows // block
    parts = len(terms)
    extra = 0 if kept is None else 1

    def kernel(*refs):
        term_refs, refs = refs[:parts], refs[parts:]
        mid_ref, lengths_ref, bias_ref, scale_ref = refs[:4]
        out_ref = refs[4 + extra]
        i = pl.program_id(0)
        mlp = bias_ref[...]
        for ref in term_refs:
            mlp = mlp + ref[...].astype(F32)
        valid = valid_rows(lengths_ref, chunk * rows + i * block, block)
        out_ref[...] = (valid * (mid_ref[...] + scale_ref[...] * mlp)).astype(BF16)

    own = pl.BlockSpec((block, width), lambda i: (i, 0))
    by_row = pl.BlockSpec((block, width), lambda i: (chunk * steps + i, 0))
    args = (*terms, middle, lengths, bias, scale)
    alias = None
    if kept is not None:
        alias = {len(args): 0}
        args = args + (kept,)
    return call(
        kernel,
        "layer_output",
        (steps,),
        [own] * parts
        + [by_row, SMEM, whole(bias), whole(scale)]
        + [pl.BlockSpec(memory_space=pl.ANY)] * extra,
        by_row,
        shape((count, width), BF16),
        args,
        0,
        alias=alias,
    )


def from_peers(array):
    size = lax.axis_size("tensor")
    return [
        lax.ppermute(array, "tensor", [(i, (i + step) % size) for i in range(size)])
        for step in range(1, size)
    ]


def scatter_sum(array):
    size = lax.axis_size("dp")
    index = lax.axis_index("dp")
    stride = 1
    wide = None
    while stride < size:
        left = size // stride
        radix = 2 if stride == 1 and left % 2 == 0 else next(r for r in (2, 4, 3, left) if left % r == 0)
        if stride > 1 and left % 4 == 0 and left != 8:
            radix = 4
        rows = array.shape[0] // left
        view = array.reshape(left // radix, radix, rows, array.shape[1])
        place = (index // stride) % radix
        total = lax.dynamic_index_in_dim(view, place, 1, keepdims=False).astype(F32)
        for step in range(1, radix):
            to = lax.rem(place + step, radix)
            moves = []
            for i in range(size):
                at = (i // stride) % radix
                moves.append((i, i + ((at + step) % radix - at) * stride))
            sent = lax.dynamic_index_in_dim(view, to, 1, keepdims=False)
            total = total + lax.ppermute(sent, "dp", moves).astype(F32)
        stride *= radix
        wide = total.reshape(-1, array.shape[1])
        array = wide.astype(BF16)
    return wide


def body(
    tokens,
    lengths,
    norm1_gain,
    norm1_bias,
    qkv_weight,
    qv_bias,
    proj_weight,
    proj_bias,
    scale_attn,
    norm2_gain,
    norm2_bias,
    fc1_weight,
    fc1_bias,
    fc2_weight,
    fc2_bias,
    scale_mlp,
    cotangent,
):
    count, width = tokens.shape
    heads, head_size = qv_bias.shape[1:]
    local = heads * head_size
    units = fc1_weight.shape[1]
    tensor = lax.axis_size("tensor")
    dp = lax.axis_size("dp")
    chunks = 2
    rows = count // chunks
    scale = head_size**-0.5

    def flat(vector):
        return vector.reshape(1, -1)

    gain1, shift1, gain2, shift2 = map(flat, (norm1_gain, norm1_bias, norm2_gain, norm2_bias))
    bias_p, scale_a, bias_2, scale_m = map(flat, (proj_bias, scale_attn, fc2_bias, scale_mlp))

    projs = [proj_weight] + from_peers(proj_weight)
    queries, keys, values, normed1 = project(
        tokens, gain1, shift1, qkv_weight, qv_bias.reshape(2, local), scale
    )
    mixed = attend_forward(queries, keys, values, lengths)

    kept = None
    norm2_groups = []
    fc1_bias_sum = 0.0
    norm2_sums = 0.0
    for chunk in range(chunks):
        sent = lax.slice_in_dim(mixed, chunk * rows, (chunk + 1) * rows, axis=0)
        out = feed_forward(
            chunk,
            rows,
            [mixed] + from_peers(sent),
            projs,
            tokens,
            cotangent,
            lengths,
            (bias_p, scale_a, gain2, shift2, scale_m),
            fc1_weight,
            flat(fc1_bias),
            fc2_weight,
            kept,
        )
        kept = out[:5]
        fc1_bias_sum = fc1_bias_sum + out[5]
        norm2_sums = norm2_sums + out[7]
        norm2_groups.append([out[6]] + from_peers(out[6]))
    middle, normed2, grad_mlp, activated, grad_hidden = kept

    mlp_groups = []
    result_sums = 0.0
    for chunk in range(chunks):
        terms, sums = second_projection(
            chunk, rows, activated, fc2_weight, cotangent, lengths, scale_m
        )
        result_sums = result_sums + sums
        mlp_groups.append([terms] + from_peers(terms))

    fc_grads = weight_grads([normed2, grad_mlp], [grad_hidden, activated], 512, "fc_grads")
    fc_shares = lax.psum_scatter(fc_grads, "dp", scatter_dimension=0, tiled=True).astype(F32)

    grad_middle, grad_attn, grad_mixed, middle_sums = middle_back(
        norm2_groups, middle, tokens, cotangent, lengths, scale_a, gain2, proj_weight
    )
    grads, bias_sums = attend_backward(queries, keys, values, grad_mixed, lengths, scale)

    norm1_groups = []
    norm1_sums = 0.0
    for chunk in range(chunks):
        terms, sums = first_norm_terms(chunk, rows, grads, qkv_weight, tokens)
        norm1_sums = norm1_sums + sums
        norm1_groups.append([terms] + from_peers(terms))

    attn_grads = weight_grads([normed1, grad_attn], [grads, mixed], 512, "attn_grads")
    attn_shares = scatter_sum(attn_grads)

    output = None
    grad_tokens = None
    for chunk in range(chunks):
        output = layer_output(
            chunk, rows, mlp_groups[chunk], middle, lengths, bias_2, scale_m, output
        )
    for chunk in range(chunks):
        grad_tokens = token_grads(
            chunk, rows, norm1_groups[chunk], grad_middle, tokens, gain1, grad_tokens
        )

    once = 1.0 / tensor
    vectors = jnp.concatenate(
        [
            norm1_sums,
            middle_sums[0:1] / scale_a * once,
            middle_sums[1:2] * scale_a * once,
            norm2_sums,
            result_sums[0:1] + result_sums[1:2] * bias_2 * once,
            result_sums[1:2] * scale_m * once,
        ]
    )
    small = jnp.concatenate(
        [
            vectors.reshape(8, dp, -1).transpose(1, 0, 2).reshape(dp, -1),
            bias_sums.reshape(2 * heads, dp, -1).transpose(1, 0, 2).reshape(dp, -1),
            fc1_bias_sum.reshape(-1, dp, head_size // dp).transpose(1, 0, 2).reshape(dp, -1),
        ],
        axis=1,
    )
    small_share = scatter_sum(small)[0]
    first_end = 8 * width // dp
    second_end = first_end + 2 * local // dp
    vector_share = small_share[:first_end].reshape(8, width // dp)
    for other in from_peers(vector_share):
        vector_share = vector_share + other
    vector_share = lax.dynamic_slice_in_dim(
        vector_share, lax.axis_index("tensor") * (width // dp // tensor), width // dp // tensor, 1
    )
    bias_share = small_share[first_end:second_end].reshape(2, heads, -1)
    fc1_bias_share = small_share[second_end:].reshape(-1, head_size // dp)

    return (
        output,
        grad_tokens,
        vector_share[0],
        vector_share[1],
        jnp.stack([attn_shares[:, i * local : (i + 1) * local] for i in range(3)]),
        bias_share,
        attn_shares[:, 3 * local :].T,
        vector_share[3],
        vector_share[2],
        vector_share[4],
        vector_share[5],
        fc_shares[:, :units],
        fc1_bias_share,
        fc_shares[:, units:].T,
        vector_share[7],
        vector_share[6],
    )


def solution(mesh):
    in_specs = (
        P("dp", None),
        P("dp", None),
        P(),
        P(),
        P(None, None, "tensor"),
        P(None, "tensor", None),
        P("tensor", None),
        P(),
        P(),
        P(),
        P(),
        P(None, "tensor"),
        P("tensor"),
        P("tensor", None),
        P(),
        P(),
        P("dp", None),
    )
    out_specs = (
        P("dp", None),
        P("dp", None),
        P(("dp", "tensor")),
        P(("dp", "tensor")),
        P(None, "dp", "tensor"),
        P(None, "tensor", "dp"),
        P("tensor", "dp"),
        P(("dp", "tensor")),
        P(("dp", "tensor")),
        P(("dp", "tensor")),
        P(("dp", "tensor")),
        P("dp", "tensor"),
        P("tensor", "dp"),
        P("tensor", "dp"),
        P(("dp", "tensor")),
        P(("dp", "tensor")),
    )
    return jax.shard_map(body, mesh=mesh, in_specs=in_specs, out_specs=out_specs, check_vma=False)
```

```python
from functools import partial

import jax
import jax.numpy as jnp
from jax import lax
from jax.experimental import pallas as pl
from jax.experimental.pallas import tpu as pltpu
from jax.sharding import PartitionSpec as P

EPS = 1e-06
NEGATIVE = -1e30
GLOBAL_LEN = 197
LOCAL_LEN = 37
GROUP = GLOBAL_LEN // LOCAL_LEN
WINDOW = 224
BF16 = jnp.bfloat16
F32 = jnp.float32
MIB = 1 << 20
COST = 2300000000
COSTS = {"last_output": 46000000000, "first_norm_terms": 23000000000}


def dot_nn(a, b):
    return lax.dot_general(a, b, (((1,), (0,)), ((), ())), preferred_element_type=F32)


def dot_nt(a, b):
    return lax.dot_general(a, b, (((1,), (1,)), ((), ())), preferred_element_type=F32)


def dot_tn(a, b):
    return lax.dot_general(a, b, (((0,), (0,)), ((), ())), preferred_element_type=F32)


def norm_parts(values):
    average = jnp.mean(values, axis=-1, keepdims=True)
    centered = values - average
    inverse = lax.rsqrt(jnp.mean(centered * centered, axis=-1, keepdims=True) + EPS)
    return centered * inverse, inverse


def norm_back(grad_norm, scaled, inverse, gain):
    grad_hat = grad_norm * gain
    first_mean = jnp.mean(grad_hat, axis=-1, keepdims=True)
    second_mean = jnp.mean(grad_hat * scaled, axis=-1, keepdims=True)
    return inverse * (grad_hat - first_mean - scaled * second_mean)


def col_sum(values):
    return jnp.sum(values, axis=0, keepdims=True)


def call(kernel, name, grid, in_specs, out_specs, out_shape, args, after=None, scratch=(), vmem=60, alias=None):
    single = not isinstance(out_shape, list)
    if single:
        out_specs, out_shape = [out_specs], [out_shape]
    n_in, n_out = len(args), len(out_shape)
    n_after = 0 if after is None else 1

    def ordered(*refs):
        done = refs[n_in + n_after + n_out]
        done[...] = jnp.zeros_like(done)
        kernel(*refs[:n_in], *refs[n_in + n_after : n_in + n_after + n_out], *refs[n_in + n_after + n_out + 1 :])

    out = pl.pallas_call(
        ordered,
        grid=grid,
        in_specs=list(in_specs) + [pl.BlockSpec(memory_space=pl.ANY)] * n_after,
        out_specs=list(out_specs) + [pl.BlockSpec((8, 128), lambda *_: (0, 0))],
        out_shape=list(out_shape) + [shape((8, 128), F32)],
        scratch_shapes=scratch,
        input_output_aliases=alias or {},
        compiler_params=pltpu.CompilerParams(vmem_limit_bytes=vmem * MIB),
        cost_estimate=pl.CostEstimate(flops=COSTS.get(name, COST), bytes_accessed=COST, transcendentals=0),
        name=name,
    )(*args, *([after] if n_after else []))
    return (out[0] if single else out[:-1]), out[-1]


def shape(dims, dtype):
    return jax.ShapeDtypeStruct(dims, dtype)


def whole(array):
    zeros = (0,) * array.ndim
    return pl.BlockSpec(array.shape, lambda *_: zeros)


SMEM = pl.BlockSpec(memory_space=pltpu.SMEM)


def row_total(lengths_ref):
    total = jnp.int32(0)
    for slot in range(lengths_ref.shape[1]):
        total = total + lengths_ref[0, slot]
    return total


def valid_rows(lengths_ref, first, rows):
    places = lax.broadcasted_iota(jnp.int32, (rows, 1), 0) + first
    return (places < row_total(lengths_ref)).astype(F32)


def project(tokens, gain, bias, weight, qv_bias, scale, after=None):
    count, width = tokens.shape
    local = weight.shape[2]
    rows = 256

    def kernel(x_ref, gain_ref, bias_ref, w_ref, qv_ref, q_ref, k_ref, v_ref, n_ref):
        scaled, _ = norm_parts(x_ref[...].astype(F32))
        normed = (scaled * gain_ref[...] + bias_ref[...]).astype(BF16)
        n_ref[...] = normed
        queries = (dot_nn(normed, w_ref[0]) + qv_ref[0:1]).astype(BF16)
        q_ref[...] = queries * BF16(scale)
        k_ref[...] = dot_nn(normed, w_ref[1]).astype(BF16)
        v_ref[...] = (dot_nn(normed, w_ref[2]) + qv_ref[1:2]).astype(BF16)

    by_row = pl.BlockSpec((rows, width), lambda i: (i, 0))
    by_row_local = pl.BlockSpec((rows, local), lambda i: (i, 0))
    part = shape((count, local), BF16)
    return call(
        kernel,
        "project",
        (count // rows,),
        [by_row, whole(gain), whole(bias), whole(weight), whole(qv_bias)],
        [by_row_local, by_row_local, by_row_local, by_row],
        [part, part, part, shape((count, width), BF16)],
        (tokens, gain, bias, weight, qv_bias),
        after,
    )


def item_counts(lengths_ref):
    globals_ = jnp.int32(0)
    locals_ = jnp.int32(0)
    for slot in range(lengths_ref.shape[1]):
        value = lengths_ref[0, slot]
        globals_ = globals_ + jnp.where(value == GLOBAL_LEN, 1, 0)
        locals_ = locals_ + jnp.where(value == LOCAL_LEN, 1, 0)
    return globals_, locals_


def item_place(item, globals_, locals_, count):
    is_global = item < globals_
    group = item - globals_
    start = jnp.where(
        is_global, item * GLOBAL_LEN, globals_ * GLOBAL_LEN + group * (GROUP * LOCAL_LEN)
    )
    length = jnp.where(
        is_global, GLOBAL_LEN, jnp.minimum(locals_ - group * GROUP, GROUP) * LOCAL_LEN
    )
    crop = jnp.where(is_global, GLOBAL_LEN, LOCAL_LEN)
    first = jnp.minimum((start // 16) * 16, count - WINDOW)
    return pl.multiple_of(first, 16), start - first, length, crop


def crop_of(places, offset, length, crop, outside):
    inside = (places >= offset) & (places < offset + length)
    index = places - offset
    label = jnp.zeros_like(places)
    for step in range(1, GROUP):
        label = label + jnp.where(index >= step * crop, 1, 0)
    return jnp.where(inside, label, outside)


def item_total(globals_, locals_):
    return globals_ + (locals_ + GROUP - 1) // GROUP


def attend_forward(queries, keys, values, lengths, halves, after):
    count, local = queries.shape
    head = 64
    pair = 2 * head

    n_half = len(halves)

    def kernel(q_ref, k_ref, v_ref, lengths_ref, *refs):
        half_refs, out_ref, on_refs = refs[:n_half], refs[n_half], refs[n_half + 1 :]
        for half_ref, on_ref in zip(half_refs, on_refs):
            on_ref[...] = half_ref[...]
        globals_, locals_ = item_counts(lengths_ref)
        average = col_sum(v_ref[...].astype(F32)) * (1.0 / count)
        out_ref[...] = jnp.broadcast_to(average, (count, local)).astype(BF16)
        low_half = lax.broadcasted_iota(jnp.int32, (1, pair), 1) < head

        def step(item, carry):
            first, offset, length, crop = item_place(item, globals_, locals_, count)
            window = pl.ds(first, WINDOW)
            by_query = lax.broadcasted_iota(jnp.int32, (WINDOW, 1), 0)
            by_key = lax.broadcasted_iota(jnp.int32, (1, WINDOW), 1)
            query_crop = crop_of(by_query, offset, length, crop, -2)
            key_crop = crop_of(by_key, offset, length, crop, -1)
            mask = jnp.where(query_crop == key_crop, 0.0, NEGATIVE)
            inside = query_crop >= 0
            for index in range(local // pair):
                columns = slice(index * pair, (index + 1) * pair)
                q2 = q_ref[window, columns]
                k2 = k_ref[window, columns]
                v2 = v_ref[window, columns]
                out = None
                for keep in (low_half, jnp.logical_not(low_half)):
                    kept_k = jnp.where(keep, k2, BF16(0))
                    kept_v = jnp.where(keep, v2, BF16(0))
                    scores = dot_nt(q2, kept_k) + mask
                    weights = jnp.exp(scores - jnp.max(scores, axis=1, keepdims=True))
                    total = jnp.sum(weights, axis=1, keepdims=True)
                    low = (weights * (1.0 / total)).astype(BF16)
                    term = dot_nn(low, kept_v)
                    out = term if out is None else out + term
                out_ref[window, columns] = jnp.where(
                    inside, out, out_ref[window, columns].astype(F32)
                ).astype(BF16)
            return carry

        lax.fori_loop(0, item_total(globals_, locals_), step, 0)

    vm = pl.BlockSpec(memory_space=pltpu.VMEM)
    return call(
        kernel,
        "attend_forward",
        (),
        [vm, vm, vm, SMEM] + [vm] * n_half,
        [vm] + [vm] * n_half,
        [shape((count, local), BF16)] + [shape(h.shape, BF16) for h in halves],
        (queries, keys, values, lengths, *halves),
        after,
    )


def attend_backward(queries, keys, values, grad_mixed, lengths, scale, after):
    count, local = queries.shape
    head = 64
    pair = 2 * head

    def kernel(q_ref, k_ref, v_ref, g_ref, lengths_ref, out_ref, bias_ref, acc_ref):
        globals_, locals_ = item_counts(lengths_ref)
        acc_ref[...] = jnp.zeros_like(acc_ref)
        low_half = lax.broadcasted_iota(jnp.int32, (1, pair), 1) < head

        def step(item, carry):
            first, offset, length, crop = item_place(item, globals_, locals_, count)
            window = pl.ds(first, WINDOW)
            by_key = lax.broadcasted_iota(jnp.int32, (WINDOW, 1), 0)
            by_query = lax.broadcasted_iota(jnp.int32, (1, WINDOW), 1)
            query_crop = crop_of(by_query, offset, length, crop, -2)
            key_crop = crop_of(by_key, offset, length, crop, -1)
            mask = jnp.where(query_crop == key_crop, 0.0, NEGATIVE)
            inside = key_crop >= 0
            for index in range(local // pair):
                columns = slice(index * pair, (index + 1) * pair)
                q2 = q_ref[window, columns]
                k2 = k_ref[window, columns]
                v2 = v_ref[window, columns]
                g2 = jnp.where(inside, g_ref[window, columns], BF16(0))
                grad_q = grad_k = grad_v = None
                for keep in (low_half, jnp.logical_not(low_half)):
                    kept_k = jnp.where(keep, k2, BF16(0))
                    kept_v = jnp.where(keep, v2, BF16(0))
                    kept_q = jnp.where(keep, q2, BF16(0))
                    kept_g = jnp.where(keep, g2, BF16(0))
                    scores = dot_nt(kept_k, q2) + mask
                    weights = jnp.exp(scores - jnp.max(scores, axis=0, keepdims=True))
                    total = jnp.sum(weights, axis=0, keepdims=True)
                    probability = weights * (1.0 / total)
                    grad_probability = dot_nt(kept_v, g2)
                    delta = jnp.sum(probability * grad_probability, axis=0, keepdims=True)
                    grad_scores = (probability * (grad_probability - delta)).astype(BF16)
                    term_v = dot_nn(probability.astype(BF16), kept_g)
                    term_k = dot_nn(grad_scores, kept_q)
                    term_q = dot_tn(grad_scores, kept_k)
                    grad_v = term_v if grad_v is None else grad_v + term_v
                    grad_k = term_k if grad_k is None else grad_k + term_k
                    grad_q = term_q if grad_q is None else grad_q + term_q
                acc_ref[0, window, columns] += grad_q * scale
                acc_ref[1, window, columns] += grad_k
                acc_ref[2, window, columns] += grad_v
            return carry

        lax.fori_loop(0, item_total(globals_, locals_), step, 0)
        for part in range(3):
            out_ref[:, part * local : (part + 1) * local] = acc_ref[part].astype(BF16)
            bias_ref[part : part + 1] = col_sum(acc_ref[part])

    vm = pl.BlockSpec(memory_space=pltpu.VMEM)
    return call(
        kernel,
        "attend_backward",
        (),
        [vm, vm, vm, vm, SMEM],
        [vm, vm],
        [shape((count, 3 * local), BF16), shape((3, local), F32)],
        (queries, keys, values, grad_mixed, lengths),
        after,
        scratch=[pltpu.VMEM((3, count, local), F32)],
    )


def gelu_parts(value):
    size = jnp.abs(value)
    bell = jnp.exp(value * value * -0.5)
    t = 1.0 / (1.0 + size * (0.3275911 * 0.7071067811865476))
    poly = t * (
        0.254829592
        + t * (-0.284496736 + t * (1.421413741 + t * (-1.453152027 + t * 1.061405429)))
    )
    tail = 0.5 * poly * bell
    share = jnp.where(value >= 0, 1.0 - tail, tail)
    return value * share, share + value * (bell * 0.3989422804014327)


def hidden_cotangent(cotangent, lengths, scale_mlp, fc2, after):
    count, width = cotangent.shape
    units = fc2.shape[0]
    block = 256

    def kernel(c_ref, lengths_ref, sm_ref, w_ref, gm_ref, out_ref):
        grad = c_ref[...].astype(F32) * valid_rows(lengths_ref, pl.program_id(0) * block, block)
        low = (grad * sm_ref[...]).astype(BF16)
        gm_ref[...] = low
        out_ref[...] = dot_nt(low, w_ref[...]).astype(BF16)

    by_row = pl.BlockSpec((block, width), lambda i: (i, 0))
    return call(
        kernel,
        "hidden_cotangent",
        (count // block,),
        [by_row, SMEM, whole(scale_mlp), whole(fc2)],
        [by_row, pl.BlockSpec((block, units), lambda i: (i, 0))],
        [shape((count, width), BF16), shape((count, units), BF16)],
        (cotangent, lengths, scale_mlp, fc2),
        after,
    )


def feed_forward(chunk, rows, mixed, proj, halves, place, tokens, grad_act, vectors, fc1, fc1_bias, kept, after):
    proj_bias, scale_attn, gain, bias = vectors
    count, width = tokens.shape
    units = fc1.shape[1]
    step_units = min(512, units)
    steps = units // step_units
    parts = len(mixed)
    n_half = len(halves)
    depth = proj.shape[0] // 2
    n_kept = 0 if kept is None else len(kept)

    def kernel(*refs):
        mixed_refs, refs = refs[:parts], refs[parts:]
        p_ref, refs = refs[0], refs[1:]
        half_refs, refs = refs[:n_half], refs[n_half:]
        place_ref, refs = refs[0], refs[1:]
        x_ref, ga_ref, pb_ref, sa_ref, gain_ref, bias_ref, fc1_ref, fb_ref = refs[:8]
        mid_ref, n2_ref, act_ref, gh_ref, fbg_ref, terms_ref, vec_ref, acc_ref = refs[8 + n_kept :]
        j = pl.program_id(0)

        @pl.when(j == 0)
        def _():
            attn = pb_ref[...]
            attn = attn + dot_nn(mixed_refs[0][...], p_ref[...]).astype(BF16).astype(F32)
            for peer in range(parts - 1):
                m_ref = mixed_refs[peer + 1]
                if n_half == parts - 1:
                    term = dot_nn(m_ref[...], half_refs[peer][...])
                else:
                    first = pl.ds(pl.multiple_of(place_ref[0] * depth, depth), depth)
                    other = pl.ds(pl.multiple_of((1 - place_ref[0]) * depth, depth), depth)
                    term = dot_nn(m_ref[:, first], half_refs[2 * peer][...])
                    term = term + dot_nn(m_ref[:, other], half_refs[2 * peer + 1][...])
                attn = attn + term.astype(BF16).astype(F32)
            middle = x_ref[...].astype(F32) + sa_ref[...] * attn
            mid_ref[...] = middle
            scaled, _ = norm_parts(middle)
            n2_ref[...] = (scaled * gain_ref[...] + bias_ref[...]).astype(BF16)

        hidden = dot_nn(n2_ref[...], fc1_ref[...]) + fb_ref[...]
        activated, slope = gelu_parts(hidden)
        act_ref[...] = activated.astype(BF16)
        grad_hidden = ga_ref[...].astype(F32) * slope
        fbg_ref[...] = col_sum(grad_hidden)
        low = grad_hidden.astype(BF16)
        gh_ref[...] = low
        term = dot_nt(low, fc1_ref[...])

        @pl.when(j == 0)
        def _():
            acc_ref[...] = term

        @pl.when(j > 0)
        def _():
            acc_ref[...] += term

        @pl.when(j == steps - 1)
        def _():
            low_terms = acc_ref[...].astype(BF16)
            terms_ref[...] = low_terms
            wide = low_terms.astype(F32)
            scaled, _ = norm_parts(mid_ref[...])
            vec_ref[0:1] = col_sum(wide * scaled)
            vec_ref[1:2] = col_sum(wide)

    def of_chunk(w):
        return pl.BlockSpec((rows, w), lambda j: (chunk, 0))

    once = pl.BlockSpec((rows, mixed[0].shape[1]), lambda j: (0, 0))
    mixed_specs = [of_chunk(m.shape[1]) if m.shape[0] == count else once for m in mixed]
    row = pl.BlockSpec((1, width), lambda j: (0, 0))
    unit_block = pl.BlockSpec((rows, step_units), lambda j: (chunk, j))
    unit_row = pl.BlockSpec((1, step_units), lambda j: (0, j))
    any_spec = pl.BlockSpec(memory_space=pl.ANY)
    args = (*mixed, proj, *halves, place, tokens, grad_act, proj_bias, scale_attn, gain, bias, fc1, fc1_bias)
    alias = None
    if kept is not None:
        alias = {len(args) + i: i for i in range(n_kept)}
        args = args + tuple(kept)
    return call(
        kernel,
        "feed_forward",
        (steps,),
        mixed_specs
        + [whole(proj)]
        + [whole(h) for h in halves]
        + [SMEM, of_chunk(width), unit_block]
        + [row] * 4
        + [pl.BlockSpec((width, step_units), lambda j: (0, j)), unit_row]
        + [any_spec] * n_kept,
        [
            of_chunk(width),
            of_chunk(width),
            unit_block,
            unit_block,
            unit_row,
            pl.BlockSpec((rows, width), lambda j: (0, 0)),
            pl.BlockSpec((2, width), lambda j: (0, 0)),
        ],
        [
            shape((count, width), F32),
            shape((count, width), BF16),
            shape((count, units), BF16),
            shape((count, units), BF16),
            shape((1, units), F32),
            shape((rows, width), BF16),
            shape((2, width), F32),
        ],
        args,
        after,
        scratch=[pltpu.VMEM((rows, width), F32)],
        alias=alias,
    )


def second_projection(chunks, activated, fc2, cotangent, lengths, after):
    count, units = activated.shape
    width = fc2.shape[1]
    block = 256
    steps = count // block
    per = steps // chunks

    def kernel(a_ref, w_ref, c_ref, lengths_ref, *refs):
        out_refs, vec_ref = refs[:-1], refs[-1]
        i = pl.program_id(0)
        terms = dot_nn(a_ref[...], w_ref[...]).astype(BF16)
        for chunk in range(chunks):

            @pl.when(i // per == chunk)
            def _(chunk=chunk):
                out_refs[chunk][...] = terms

        grad = c_ref[...].astype(F32) * valid_rows(lengths_ref, i * block, block)
        first = col_sum(grad * terms.astype(F32))
        second = col_sum(grad)

        @pl.when(i == 0)
        def _():
            vec_ref[0:1] = first
            vec_ref[1:2] = second

        @pl.when(i > 0)
        def _():
            vec_ref[0:1] += first
            vec_ref[1:2] += second

    def chunk_spec(chunk):
        return pl.BlockSpec((block, width), lambda i: (jnp.clip(i - chunk * per, 0, per - 1), 0))

    return call(
        kernel,
        "second_projection",
        (steps,),
        [
            pl.BlockSpec((block, units), lambda i: (i, 0)),
            whole(fc2),
            pl.BlockSpec((block, width), lambda i: (i, 0)),
            SMEM,
        ],
        [chunk_spec(c) for c in range(chunks)] + [pl.BlockSpec((2, width), lambda i: (0, 0))],
        [shape((count // chunks, width), BF16)] * chunks + [shape((2, width), F32)],
        (activated, fc2, cotangent, lengths),
        after,
    )


def weight_grads(lefts, rights, step_columns, name, after):
    count, width = lefts[0].shape
    widths = [r.shape[1] for r in rights]
    step_columns = min([step_columns] + widths)
    starts, total = [], 0
    for w in widths:
        starts.append(total)
        total += w // step_columns
    pairs = len(lefts)

    def kernel(*refs):
        left_refs, right_refs = refs[:pairs], refs[pairs : 2 * pairs]
        out_ref = refs[2 * pairs]
        j = pl.program_id(0)
        for p in range(pairs):
            end = starts[p] + widths[p] // step_columns

            @pl.when((j >= starts[p]) & (j < end))
            def _(p=p):
                out_ref[...] = dot_tn(left_refs[p][...], right_refs[p][...]).astype(BF16)

    def right_spec(p):
        last = widths[p] // step_columns - 1
        return pl.BlockSpec(
            (count, step_columns), lambda j: (0, jnp.clip(j - starts[p], 0, last))
        )

    return call(
        kernel,
        name,
        (total,),
        [whole(l) for l in lefts] + [right_spec(p) for p in range(pairs)],
        pl.BlockSpec((width, step_columns), lambda j: (0, j)),
        shape((width, total * step_columns), BF16),
        (*lefts, *rights),
        after,
    )


def attention_grads(normed, grads, grad_attn, mixed, weight, sums, vectors, place, radix, shard, after):
    count, width = normed.shape
    block = max(256, radix * shard)
    wide, local = grads.shape[1], mixed.shape[1]
    extra = vectors.shape[0]
    total = wide + local + extra
    groups = block // (radix * shard)

    def kernel(n_ref, g_ref, a_ref, m_ref, w_ref, s_ref, v_ref, place_ref, *refs):
        out_refs, hold_ref = refs[:radix], refs[radix]
        columns = v_ref[...].T
        first = second = None
        product = dot_tn(n_ref[...], g_ref[...])
        for part in range(3):
            piece = product[:, part * local : (part + 1) * local]
            w = w_ref[part].astype(F32)
            one = jnp.sum(w * piece, axis=1, keepdims=True)
            two = jnp.sum(w * s_ref[part : part + 1], axis=1, keepdims=True)
            first = one if first is None else first + one
            second = two if second is None else second + two
        lane = lax.broadcasted_iota(jnp.int32, (block, extra), 1)
        gain_grad = (first - columns[:, 1:2] * second) / columns[:, 0:1]
        small = jnp.where(lane == 0, gain_grad, jnp.where(lane == 1, second, columns))
        hold_ref[:, :, :, :wide] = product.astype(BF16).reshape(groups, radix, shard, wide)
        hold_ref[:, :, :, wide : wide + local] = (
            dot_tn(a_ref[...], m_ref[...]).astype(BF16).reshape(groups, radix, shard, local)
        )
        hold_ref[:, :, :, wide + local :] = small.astype(BF16).reshape(groups, radix, shard, extra)
        for step in range(radix):
            out_refs[step][...] = hold_ref[:, lax.rem(place_ref[0] + step, radix)]

    by_column = pl.BlockSpec((count, block), lambda i: (0, i))
    return call(
        kernel,
        "attention_grads",
        (width // block,),
        [
            by_column,
            whole(grads),
            by_column,
            whole(mixed),
            pl.BlockSpec((3, block, local), lambda i: (0, i, 0)),
            whole(sums),
            pl.BlockSpec((extra, block), lambda i: (0, i)),
            SMEM,
        ],
        [pl.BlockSpec((groups, shard, total), lambda i: (i, 0, 0))] * radix,
        [shape((width // (radix * shard), shard, total), BF16)] * radix,
        (normed, grads, grad_attn, mixed, weight, sums, vectors, place),
        after,
        scratch=[pltpu.VMEM((groups, radix, shard, total), BF16)],
    )


def add_stage(parts, place, radix, after):
    left, shard, columns = parts[0].shape
    n_parts = len(parts)

    def kernel(*refs):
        part_refs, place_ref = refs[:n_parts], refs[n_parts]
        out_refs, hold_ref = refs[n_parts + 1 : n_parts + 1 + radix], refs[n_parts + 1 + radix]
        total = None
        for ref in part_refs:
            term = ref[...].astype(F32)
            total = term if total is None else total + term
        hold_ref[...] = total.astype(BF16)
        for step in range(radix):
            out_refs[step][...] = hold_ref[lax.rem(place_ref[0] + step, radix)][None]

    return call(
        kernel,
        "add_stage",
        (left // radix,),
        [pl.BlockSpec((radix, shard, columns), lambda i: (i, 0, 0))] * n_parts + [SMEM],
        [pl.BlockSpec((1, shard, columns), lambda i: (i, 0, 0))] * radix,
        [shape((left // radix, shard, columns), BF16)] * radix,
        (*parts, place),
        after,
        scratch=[pltpu.VMEM((radix, shard, columns), BF16)],
    )


def last_stage(parts, local, after):
    _, shard, columns = parts[0].shape
    n_parts = len(parts)
    extra = columns - 4 * local

    def kernel(*refs):
        part_refs, (qkv_ref, proj_ref, small_ref) = refs[:n_parts], refs[n_parts:]
        total = None
        for ref in part_refs:
            term = ref[0].astype(F32)
            total = term if total is None else total + term
        for part in range(3):
            qkv_ref[part] = total[:, part * local : (part + 1) * local]
        proj_ref[...] = total[:, 3 * local : 4 * local].T
        small_ref[...] = total[:, 4 * local :].T

    vm = pl.BlockSpec(memory_space=pltpu.VMEM)
    return call(
        kernel,
        "last_stage",
        (),
        [vm] * n_parts,
        [vm, vm, vm],
        [shape((3, shard, local), F32), shape((local, shard), F32), shape((extra, shard), F32)],
        tuple(parts),
        after,
    )


def middle_back(chunk, rows, terms, middle, tokens, cotangent, lengths, scale_attn, gain, proj, kept, after):
    count, width = middle.shape
    local = proj.shape[0]
    block = 256
    steps = rows // block
    parts = len(terms)
    n_kept = 0 if kept is None else len(kept)

    def kernel(*refs):
        term_refs, refs = refs[:parts], refs[parts:]
        mid_ref, x_ref, c_ref, lengths_ref, sa_ref, gain_ref, p_ref = refs[:7]
        gmid_ref, low_ref, gmix_ref, vec_ref = refs[7 + n_kept :]
        i = pl.program_id(0)
        grad_norm = None
        for ref in term_refs:
            term = ref[...].astype(F32)
            grad_norm = term if grad_norm is None else grad_norm + term
        middle = mid_ref[...]
        scaled, inverse = norm_parts(middle)
        grad = c_ref[...].astype(F32) * valid_rows(lengths_ref, chunk * rows + i * block, block)
        grad = grad + norm_back(grad_norm, scaled, inverse, gain_ref[...])
        gmid_ref[...] = grad
        low = (sa_ref[...] * grad).astype(BF16)
        low_ref[...] = low
        gmix_ref[...] = dot_nt(low, p_ref[...]).astype(BF16)
        first = col_sum(grad * (middle - x_ref[...].astype(F32)))
        second = col_sum(grad)

        @pl.when(i == 0)
        def _():
            vec_ref[0:1] = first
            vec_ref[1:2] = second

        @pl.when(i > 0)
        def _():
            vec_ref[0:1] += first
            vec_ref[1:2] += second

    own = pl.BlockSpec((block, width), lambda i: (i, 0))
    by_row = pl.BlockSpec((block, width), lambda i: (chunk * steps + i, 0))
    args = (*terms, middle, tokens, cotangent, lengths, scale_attn, gain, proj)
    alias = None
    if kept is not None:
        alias = {len(args) + i: i for i in range(n_kept)}
        args = args + tuple(kept)
    return call(
        kernel,
        "middle_back",
        (steps,),
        [own] * parts
        + [by_row, by_row, by_row, SMEM, whole(scale_attn), whole(gain), whole(proj)]
        + [pl.BlockSpec(memory_space=pl.ANY)] * n_kept,
        [
            by_row,
            by_row,
            pl.BlockSpec((block, local), lambda i: (chunk * steps + i, 0)),
            pl.BlockSpec((2, width), lambda i: (0, 0)),
        ],
        [
            shape((count, width), F32),
            shape((count, width), BF16),
            shape((count, local), BF16),
            shape((2, width), F32),
        ],
        args,
        after,
        alias=alias,
    )


def first_norm_terms(chunk, rows, grads, weight, after):
    width, local = weight.shape[1:]
    block = 256
    steps = rows // block

    def kernel(g_ref, w_ref, out_ref):
        total = None
        for part in range(3):
            term = dot_nt(g_ref[:, part * local : (part + 1) * local], w_ref[part])
            total = term if total is None else total + term
        out_ref[...] = total.astype(BF16)

    return call(
        kernel,
        "first_norm_terms",
        (steps,),
        [pl.BlockSpec((block, 3 * local), lambda i: (chunk * steps + i, 0)), whole(weight)],
        pl.BlockSpec((block, width), lambda i: (i, 0)),
        shape((rows, width), BF16),
        (grads, weight),
        after,
    )


def token_grads(chunk, rows, terms, grad_middle, tokens, gain, kept, after):
    count, width = tokens.shape
    block = 256
    steps = rows // block
    parts = len(terms)
    extra = 0 if kept is None else 1

    def kernel(*refs):
        term_refs, refs = refs[:parts], refs[parts:]
        gmid_ref, x_ref, gain_ref = refs[:3]
        out_ref = refs[3 + extra]
        grad_norm = None
        for ref in term_refs:
            term = ref[...].astype(F32)
            grad_norm = term if grad_norm is None else grad_norm + term
        scaled, inverse = norm_parts(x_ref[...].astype(F32))
        grad = gmid_ref[...] + norm_back(grad_norm, scaled, inverse, gain_ref[...])
        out_ref[...] = grad.astype(BF16)

    own = pl.BlockSpec((block, width), lambda i: (i, 0))
    by_row = pl.BlockSpec((block, width), lambda i: (chunk * steps + i, 0))
    args = (*terms, grad_middle, tokens, gain)
    alias = None
    if kept is not None:
        alias = {len(args): 0}
        args = args + (kept,)
    return call(
        kernel,
        "token_grads",
        (steps,),
        [own] * parts
        + [by_row, by_row, whole(gain)]
        + [pl.BlockSpec(memory_space=pl.ANY)] * extra,
        by_row,
        shape((count, width), BF16),
        args,
        after,
        alias=alias,
    )


def layer_output(chunk, rows, terms, middle, lengths, bias, scale, kept, after, name="layer_output"):
    count, width = middle.shape
    block = 256
    steps = rows // block
    parts = len(terms)
    extra = 0 if kept is None else 1

    def kernel(*refs):
        term_refs, refs = refs[:parts], refs[parts:]
        mid_ref, lengths_ref, bias_ref, scale_ref = refs[:4]
        out_ref = refs[4 + extra]
        i = pl.program_id(0)
        mlp = bias_ref[...]
        for ref in term_refs:
            mlp = mlp + ref[...].astype(F32)
        valid = valid_rows(lengths_ref, chunk * rows + i * block, block)
        out_ref[...] = (valid * (mid_ref[...] + scale_ref[...] * mlp)).astype(BF16)

    own = pl.BlockSpec((block, width), lambda i: (i, 0))
    by_row = pl.BlockSpec((block, width), lambda i: (chunk * steps + i, 0))
    args = (*terms, middle, lengths, bias, scale)
    alias = None
    if kept is not None:
        alias = {len(args): 0}
        args = args + (kept,)
    return call(
        kernel,
        name,
        (steps,),
        [own] * parts
        + [by_row, SMEM, whole(bias), whole(scale)]
        + [pl.BlockSpec(memory_space=pl.ANY)] * extra,
        by_row,
        shape((count, width), BF16),
        args,
        after,
        alias=alias,
    )


def from_peers(array):
    size = lax.axis_size("tensor")
    return [
        lax.ppermute(array, "tensor", [(i, (i + step) % size) for i in range(size)])
        for step in range(1, size)
    ]


def other_of_pair(array):
    return lax.ppermute(array, "dp", [(i, i ^ 1) for i in range(lax.axis_size("dp"))])


def radices(size):
    found = []
    if size % 2 == 0:
        found.append(2)
        size //= 2
    while size > 1:
        step = 2 if size % 4 and size % 2 == 0 or size == 8 else next((r for r in (4, 3) if size % r == 0), size)
        found.append(step)
        size //= step
    return found


def exchange(parts, stride, radix):
    size = lax.axis_size("dp")
    arrived = []
    for step in range(1, radix):
        moves = []
        for i in range(size):
            at = (i // stride) % radix
            moves.append((i, i + ((at + step) % radix - at) * stride))
        arrived.append(lax.ppermute(parts[step], "dp", moves))
    return [parts[0]] + arrived


def body(
    tokens,
    lengths,
    norm1_gain,
    norm1_bias,
    qkv_weight,
    qv_bias,
    proj_weight,
    proj_bias,
    scale_attn,
    norm2_gain,
    norm2_bias,
    fc1_weight,
    fc1_bias,
    fc2_weight,
    fc2_bias,
    scale_mlp,
    cotangent,
):
    count, width = tokens.shape
    heads, head_size = qv_bias.shape[1:]
    local = heads * head_size
    units = fc1_weight.shape[1]
    tensor = lax.axis_size("tensor")
    dp = lax.axis_size("dp")
    chunks = 2
    rows = count // chunks
    scale = head_size**-0.5

    def flat(vector):
        return vector.reshape(1, -1)

    gain1, shift1, gain2, shift2 = map(flat, (norm1_gain, norm1_bias, norm2_gain, norm2_bias))
    bias_p, scale_a, bias_2, scale_m = map(flat, (proj_bias, scale_attn, fc2_bias, scale_mlp))

    index = lax.axis_index("dp")
    steps = radices(dp)
    strides = [1]
    for step in steps:
        strides.append(strides[-1] * step)
    places = [((index // stride) % step).reshape(1) for stride, step in zip(strides, steps)]

    half_rows = local // 2
    paired = dp % 2 == 0 and half_rows % 128 == 0
    half_place = (index % 2).reshape(1)
    half = proj_weight
    if paired:
        half = lax.dynamic_slice_in_dim(proj_weight, half_place[0] * half_rows, half_rows, 0)
    halves = from_peers(half)
    (queries, keys, values, normed1), done = project(
        tokens, gain1, shift1, qkv_weight, qv_bias.reshape(2, local), scale
    )
    (mixed, *halves), done = attend_forward(queries, keys, values, lengths, halves, done)
    mixed_parts = [
        from_peers(lax.slice_in_dim(mixed, chunk * rows, (chunk + 1) * rows, axis=0))
        for chunk in range(chunks)
    ]
    if paired:
        halves = [part for half in halves for part in (half, other_of_pair(half))]
    (grad_mlp, grad_act), done = hidden_cotangent(cotangent, lengths, scale_m, fc2_weight, done)

    kept = None
    norm2_parts = []
    fc1_bias_sum = 0.0
    norm2_sums = 0.0
    for chunk in range(chunks):
        out, done = feed_forward(
            chunk,
            rows,
            [mixed] + mixed_parts[chunk],
            proj_weight,
            halves,
            half_place,
            tokens,
            grad_act,
            (bias_p, scale_a, gain2, shift2),
            fc1_weight,
            flat(fc1_bias),
            kept,
            done,
        )
        kept = out[:4]
        fc1_bias_sum = fc1_bias_sum + out[4]
        norm2_sums = norm2_sums + out[6]
        norm2_parts.append([out[5]] + from_peers(out[5]))
    middle, normed2, activated, grad_hidden = kept

    fc_grads, done = weight_grads(
        [normed2, grad_mlp], [grad_hidden, activated], 512, "fc_grads", done
    )
    fc_shares = lax.psum_scatter(fc_grads, "dp", scatter_dimension=0, tiled=True).astype(F32)

    (*mlp_terms, result_sums), done = second_projection(
        chunks, activated, fc2_weight, cotangent, lengths, done
    )
    mlp_parts = [[terms] + from_peers(terms) for terms in mlp_terms]

    kept = None
    middle_sums = 0.0
    for chunk in range(chunks):
        out, done = middle_back(
            chunk,
            rows,
            norm2_parts[chunk],
            middle,
            tokens,
            cotangent,
            lengths,
            scale_a,
            gain2,
            proj_weight,
            kept,
            done,
        )
        kept = out[:3]
        middle_sums = middle_sums + out[3]
    grad_middle, grad_attn, grad_mixed = kept
    (grads, grad_sums), done = attend_backward(
        queries, keys, values, grad_mixed, lengths, scale, done
    )

    once = 1.0 / tensor
    shard = width // dp

    def by_shard(array):
        entries = array.reshape(-1, dp, array.shape[-1] // dp).transpose(1, 0, 2).reshape(dp, -1)
        entries = jnp.pad(entries, ((0, 0), (0, -entries.shape[1] % shard)))
        return entries.reshape(dp, -1, shard).transpose(1, 0, 2).reshape(-1, width)

    bias_rows = by_shard(grad_sums.reshape(3, heads, head_size)[jnp.array([0, 2])])
    fc1_rows = by_shard(fc1_bias_sum.reshape(-1, head_size))
    vectors = jnp.concatenate(
        [
            gain1,
            shift1,
            middle_sums[0:1] / scale_a * once,
            middle_sums[1:2] * scale_a * once,
            norm2_sums,
            result_sums[0:1] + result_sums[1:2] * bias_2 * once,
            result_sums[1:2] * scale_m * once,
            bias_rows,
            fc1_rows,
        ]
    )
    vectors = jnp.pad(vectors, ((0, 128 - vectors.shape[0]), (0, 0)))
    parts, done = attention_grads(
        normed1, grads, grad_attn, mixed, qkv_weight, grad_sums, vectors, places[0], steps[0], shard, done
    )
    parts = exchange(parts, 1, steps[0])

    def norm1_terms(chunk, done):
        terms, done = first_norm_terms(chunk, rows, grads, qkv_weight, done)
        return [terms] + from_peers(terms), done

    output = grad_tokens = None
    stage = 1
    norm1_parts = []
    for chunk in range(chunks):
        if chunk < chunks - 1:
            output, done = layer_output(
                chunk, rows, mlp_parts[chunk], middle, lengths, bias_2, scale_m, output, done
            )
        terms, done = norm1_terms(chunk, done)
        norm1_parts.append(terms)
        if chunk == 0 and stage < len(steps):
            parts, done = add_stage(parts, places[stage], steps[stage], done)
            parts = exchange(parts, strides[stage], steps[stage])
            stage += 1
    for chunk in range(chunks):
        grad_tokens, done = token_grads(
            chunk, rows, norm1_parts[chunk], grad_middle, tokens, gain1, grad_tokens, done
        )
        if chunk == 0:
            while stage < len(steps):
                parts, done = add_stage(parts, places[stage], steps[stage], done)
                parts = exchange(parts, strides[stage], steps[stage])
                stage += 1
    (qkv_grad, proj_grad, small), done = last_stage(parts, local, done)
    output, done = layer_output(
        chunks - 1, rows, mlp_parts[-1], middle, lengths, bias_2, scale_m, output, done, "last_output"
    )

    vector_share = small[:8]
    for other in from_peers(vector_share):
        vector_share = vector_share + other
    own = shard // tensor
    vector_share = lax.dynamic_slice_in_dim(vector_share, lax.axis_index("tensor") * own, own, 1)
    end = 8 + bias_rows.shape[0]
    bias_share = small[8:end].reshape(-1)[: 2 * local // dp].reshape(2, heads, -1)
    fc1_share = small[end : end + fc1_rows.shape[0]].reshape(-1)[: units // dp].reshape(-1, head_size // dp)

    return (
        output,
        grad_tokens,
        vector_share[0],
        vector_share[1],
        qkv_grad,
        bias_share,
        proj_grad,
        vector_share[3],
        vector_share[2],
        vector_share[4],
        vector_share[5],
        fc_shares[:, :units],
        fc1_share,
        fc_shares[:, units:].T,
        vector_share[7],
        vector_share[6],
    )


def solution(mesh):
    in_specs = (
        P("dp", None),
        P("dp", None),
        P(),
        P(),
        P(None, None, "tensor"),
        P(None, "tensor", None),
        P("tensor", None),
        P(),
        P(),
        P(),
        P(),
        P(None, "tensor"),
        P("tensor"),
        P("tensor", None),
        P(),
        P(),
        P("dp", None),
    )
    out_specs = (
        P("dp", None),
        P("dp", None),
        P(("dp", "tensor")),
        P(("dp", "tensor")),
        P(None, "dp", "tensor"),
        P(None, "tensor", "dp"),
        P("tensor", "dp"),
        P(("dp", "tensor")),
        P(("dp", "tensor")),
        P(("dp", "tensor")),
        P(("dp", "tensor")),
        P("dp", "tensor"),
        P("tensor", "dp"),
        P("tensor", "dp"),
        P(("dp", "tensor")),
        P(("dp", "tensor")),
    )
    return jax.shard_map(body, mesh=mesh, in_specs=in_specs, out_specs=out_specs, check_vma=False)
```

```python
from functools import partial

import jax
import jax.numpy as jnp
from jax import lax
from jax.experimental import pallas as pl
from jax.experimental.pallas import tpu as pltpu
from jax.sharding import PartitionSpec as P

EPS = 1e-06
NEGATIVE = -1e30
GLOBAL_LEN = 197
LOCAL_LEN = 37
GROUP = GLOBAL_LEN // LOCAL_LEN
WINDOW = 224
BF16 = jnp.bfloat16
F32 = jnp.float32
MIB = 1 << 20
VMEM_MIB = 16
SPARE = 6
LIMITS = {
    "attend_forward": 14,
    "hidden_cotangent": 6,
    "feed_forward": 15,
    "weight_grads": 17,
    "second_projection": 18,
    "middle_back": 13,
    "attend_backward": 11,
    "attention_grads": 11,
    "layer_output": 13,
    "first_norm_terms": 5,
    "add_stage": 4,
    "token_grads": 9,
    "last_stage": 4,
    "last_far_stage": 6,
    "add_far_stage": 16,
}
COST = 2300000000
COSTS = {"middle_back_1": 46000000000, "add_far_stage_1": 23000000000}


def dot_nn(a, b):
    return lax.dot_general(a, b, (((1,), (0,)), ((), ())), preferred_element_type=F32)


def dot_nt(a, b):
    return lax.dot_general(a, b, (((1,), (1,)), ((), ())), preferred_element_type=F32)


def dot_tn(a, b):
    return lax.dot_general(a, b, (((0,), (0,)), ((), ())), preferred_element_type=F32)


def norm_parts(values):
    average = jnp.mean(values, axis=-1, keepdims=True)
    centered = values - average
    inverse = lax.rsqrt(jnp.mean(centered * centered, axis=-1, keepdims=True) + EPS)
    return centered * inverse, inverse


def norm_back(grad_norm, scaled, inverse, gain):
    grad_hat = grad_norm * gain
    first_mean = jnp.mean(grad_hat, axis=-1, keepdims=True)
    second_mean = jnp.mean(grad_hat * scaled, axis=-1, keepdims=True)
    return inverse * (grad_hat - first_mean - scaled * second_mean)


def col_sum(values):
    return jnp.sum(values, axis=0, keepdims=True)


def call(kernel, name, in_specs, out_specs, out_shape, args, after=None, scratch=(), vmem=VMEM_MIB, alias=None, bring=(), late=False):
    single = not isinstance(out_shape, list)
    if single:
        out_specs, out_shape = [out_specs], [out_shape]
    n_in, n_out, n_bring = len(args), len(out_shape), len(bring)
    n_after = 0 if after is None else 1
    args = [
        pltpu.with_memory_space_constraint(arg, pltpu.VMEM if spec is VMEM else pltpu.HBM)
        if spec is VMEM or spec is ANY
        else arg
        for arg, spec in zip(args, in_specs)
    ]
    args += [pltpu.with_memory_space_constraint(arg, pltpu.HBM) for arg in bring]
    out_shape = [
        pltpu.VMEM(o.shape, o.dtype) if spec is VMEM else o for o, spec in zip(out_shape, out_specs)
    ]

    def ordered(*refs):
        ins, refs = refs[:n_in], refs[n_in:]
        bring_hbm, refs = refs[:n_bring], refs[n_bring + n_after :]
        outs, refs = refs[:n_out], refs[n_out:]
        bring_refs, done, refs = refs[:n_bring], refs[n_bring], refs[n_bring + 1 :]
        done[...] = jnp.zeros_like(done)
        loads = []
        if n_bring:
            refs, sems = refs[:-1], refs[-1]

        def begin():
            for i in range(n_bring):
                loads.append(pltpu.make_async_copy(bring_hbm[i], bring_refs[i], sems.at[i]))
                loads[-1].start()

        if late:
            kernel(begin, *ins, *outs, *refs)
        else:
            begin()
            kernel(*ins, *outs, *refs)
        for load in loads:
            load.wait()

    out = pl.pallas_call(
        ordered,
        in_specs=list(in_specs) + [ANY] * (n_bring + n_after),
        out_specs=list(out_specs) + [VMEM] * (n_bring + 1),
        out_shape=list(out_shape) + [pltpu.VMEM(a.shape, a.dtype) for a in bring] + [pltpu.VMEM((8, 128), F32)],
        scratch_shapes=list(scratch) + ([pltpu.SemaphoreType.DMA((n_bring,))] if n_bring else []),
        input_output_aliases=alias or {},
        compiler_params=pltpu.CompilerParams(vmem_limit_bytes=(LIMITS.get(name.rstrip("_0123456789"), vmem) + SPARE) * MIB),
        cost_estimate=pl.CostEstimate(flops=COSTS.get(name, COST), bytes_accessed=COST, transcendentals=0),
        name=name,
    )(*args, *([after] if n_after else []))
    return (out[0] if single and not n_bring else out[:-1]), out[-1]


class Copies:
    def __init__(self, sems):
        self.sems = sems
        self.used = 0

    def start(self, source, target):
        copy = pltpu.make_async_copy(source, target, self.sems.at[self.used])
        self.used += 1
        copy.start()
        return copy


def shape(dims, dtype):
    return jax.ShapeDtypeStruct(dims, dtype)


SMEM = pl.BlockSpec(memory_space=pltpu.SMEM)
VMEM = pl.BlockSpec(memory_space=pltpu.VMEM)
ANY = pl.BlockSpec(memory_space=pl.ANY)
COPIED = pl.BlockSpec(memory_space=pltpu.VMEM)

GAIN1, SHIFT1, GAIN2, SHIFT2, PROJ_BIAS, SCALE_ATTN, FC2_BIAS, SCALE_MLP = range(8)


def row_total(lengths_ref):
    total = jnp.int32(0)
    for slot in range(lengths_ref.shape[1]):
        total = total + lengths_ref[0, slot]
    return total


def valid_rows(lengths_ref, first, rows):
    places = lax.broadcasted_iota(jnp.int32, (rows, 1), 0) + first
    return (places < row_total(lengths_ref)).astype(F32)


def item_counts(lengths_ref):
    globals_ = jnp.int32(0)
    locals_ = jnp.int32(0)
    for slot in range(lengths_ref.shape[1]):
        value = lengths_ref[0, slot]
        globals_ = globals_ + jnp.where(value == GLOBAL_LEN, 1, 0)
        locals_ = locals_ + jnp.where(value == LOCAL_LEN, 1, 0)
    return globals_, locals_


def item_place(item, globals_, locals_, count):
    is_global = item < globals_
    group = item - globals_
    start = jnp.where(
        is_global, item * GLOBAL_LEN, globals_ * GLOBAL_LEN + group * (GROUP * LOCAL_LEN)
    )
    length = jnp.where(
        is_global, GLOBAL_LEN, jnp.minimum(locals_ - group * GROUP, GROUP) * LOCAL_LEN
    )
    crop = jnp.where(is_global, GLOBAL_LEN, LOCAL_LEN)
    first = jnp.minimum((start // 16) * 16, count - WINDOW)
    return pl.multiple_of(first, 16), start - first, length, crop


def crop_of(places, offset, length, crop, outside):
    inside = (places >= offset) & (places < offset + length)
    index = places - offset
    label = jnp.zeros_like(places)
    for step in range(1, GROUP):
        label = label + jnp.where(index >= step * crop, 1, 0)
    return jnp.where(inside, label, outside)


def item_total(globals_, locals_):
    return globals_ + (locals_ + GROUP - 1) // GROUP


def attend_forward(tokens, lengths, vectors, weight, qv_bias, scale, chunks, later):
    count, width = tokens.shape
    local = weight.shape[2]
    head = 64
    pair = 2 * head
    block = 256
    blocks = count // block
    rows = count // chunks
    n_vec, n_later = len(vectors), len(later)

    def kernel(x_hbm, w_hbm, *refs):
        later_hbm, refs = refs[:n_later], refs[n_later:]
        vec_hbm, refs = refs[:n_vec], refs[n_vec:]
        qv_hbm, lengths_ref, refs = refs[0], refs[1], refs[2:]
        q_hbm, k_hbm, v_hbm, n_hbm, table_ref, refs = *refs[:5], refs[5:]
        later_refs, refs = refs[:n_later], refs[n_later:]
        mixed_refs, vec_refs, refs = refs[:chunks], refs[chunks : chunks + n_vec], refs[chunks + n_vec :]
        heads_ref, x_ref, w_ref, q_ref, k_ref, v_ref, n_ref, out_ref, sems = refs
        copies = Copies(sems)

        def part(ref, index):
            return ref.at[pl.ds(index * block, block)]

        loads = [copies.start(part(x_hbm, 0), part(x_ref, 0))]
        small_loads = [copies.start(hbm, ref) for hbm, ref in zip(vec_hbm, vec_refs)]
        small_loads.append(copies.start(qv_hbm, heads_ref))
        weight_loads = [copies.start(w_hbm.at[i], w_ref.at[i]) for i in range(3)]
        loads += [copies.start(part(x_hbm, i), part(x_ref, i)) for i in range(1, blocks)]
        later_loads = [copies.start(hbm, ref) for hbm, ref in zip(later_hbm, later_refs)]
        for load in small_loads:
            load.wait()
        for i in range(n_vec):
            table_ref[i : i + 1] = vec_refs[i][...]
        qv = [
            jnp.concatenate([heads_ref[i, h : h + 1] for h in range(local // head)], axis=1)
            for i in range(2)
        ]
        for i in range(blocks):
            loads[i].wait()
            rows_i = slice(i * block, (i + 1) * block)
            scaled, _ = norm_parts(x_ref[rows_i].astype(F32))
            normed = (scaled * vec_refs[GAIN1][...] + vec_refs[SHIFT1][...]).astype(BF16)
            n_ref[rows_i] = normed
            if i == 0:
                weight_loads[0].wait()
            queries = (dot_nn(normed, w_ref[0]) + qv[0]).astype(BF16)
            q_ref[rows_i] = queries * BF16(scale)
            if i == 0:
                weight_loads[1].wait()
            k_ref[rows_i] = dot_nn(normed, w_ref[1]).astype(BF16)
            if i == 0:
                weight_loads[2].wait()
            v_ref[rows_i] = (dot_nn(normed, w_ref[2]) + qv[1]).astype(BF16)
        stores = [
            copies.start(ref, hbm)
            for ref, hbm in ((q_ref, q_hbm), (k_ref, k_hbm), (v_ref, v_hbm), (n_ref, n_hbm))
        ]

        globals_, locals_ = item_counts(lengths_ref)
        average = col_sum(v_ref[...].astype(F32)) * (1.0 / count)
        out_ref[...] = jnp.broadcast_to(average, (count, local)).astype(BF16)
        low_half = lax.broadcasted_iota(jnp.int32, (1, pair), 1) < head

        def step(item, carry):
            first, offset, length, crop = item_place(item, globals_, locals_, count)
            window = pl.ds(first, WINDOW)
            by_query = lax.broadcasted_iota(jnp.int32, (WINDOW, 1), 0)
            by_key = lax.broadcasted_iota(jnp.int32, (1, WINDOW), 1)
            query_crop = crop_of(by_query, offset, length, crop, -2)
            key_crop = crop_of(by_key, offset, length, crop, -1)
            mask = jnp.where(query_crop == key_crop, 0.0, NEGATIVE)
            inside = query_crop >= 0
            for index in range(local // pair):
                columns = slice(index * pair, (index + 1) * pair)
                q2 = q_ref[window, columns]
                k2 = k_ref[window, columns]
                v2 = v_ref[window, columns]
                out = None
                for keep in (low_half, jnp.logical_not(low_half)):
                    kept_k = jnp.where(keep, k2, BF16(0))
                    kept_v = jnp.where(keep, v2, BF16(0))
                    scores = dot_nt(q2, kept_k) + mask
                    weights = jnp.exp(scores - jnp.max(scores, axis=1, keepdims=True))
                    total = jnp.sum(weights, axis=1, keepdims=True)
                    low = (weights * (1.0 / total)).astype(BF16)
                    term = dot_nn(low, kept_v)
                    out = term if out is None else out + term
                out_ref[window, columns] = jnp.where(
                    inside, out, out_ref[window, columns].astype(F32)
                ).astype(BF16)
            return carry

        lax.fori_loop(0, item_total(globals_, locals_), step, 0)
        for chunk in range(chunks):
            mixed_refs[chunk][...] = out_ref[chunk * rows : (chunk + 1) * rows]
        for copy in later_loads + stores:
            copy.wait()

    part = pltpu.HBM((count, local), BF16)
    wide = pltpu.HBM((count, width), BF16)
    hbm = (tokens, weight, *later)
    outs = [part, part, part, wide, shape((n_vec, width), F32)]
    outs = outs + [shape(a.shape, a.dtype) for a in later] + [shape((rows, local), BF16)] * chunks
    return call(
        kernel,
        "attend_forward",
        [ANY] * (len(hbm) + n_vec + 1) + [SMEM],
        [ANY] * 4 + [VMEM] * (len(outs) - 4),
        outs,
        (*hbm, *vectors, qv_bias, lengths),
        scratch=[pltpu.VMEM((1, width), F32)] * n_vec
        + [
            pltpu.VMEM(qv_bias.shape, F32),
            pltpu.VMEM((count, width), BF16),
            pltpu.VMEM(weight.shape, BF16),
            pltpu.VMEM((count, local), BF16),
            pltpu.VMEM((count, local), BF16),
            pltpu.VMEM((count, local), BF16),
            pltpu.VMEM((count, width), BF16),
            pltpu.VMEM((count, local), BF16),
            pltpu.SemaphoreType.DMA((blocks + 8 + n_later + n_vec,)),
        ],
    )


def attend_backward(queries, keys, values, grad_mixed, lengths, scale, after, bring):
    count, local = queries.shape
    head = 64
    pair = 2 * head

    chunks = len(grad_mixed)
    rows = count // chunks

    def kernel(q_ref, k_ref, v_ref, *refs):
        chunk_refs, refs = refs[:chunks], refs[chunks:]
        lengths_ref, out_ref, bias_ref, acc_ref, g_ref = refs
        for chunk in range(chunks):
            g_ref[chunk * rows : (chunk + 1) * rows] = chunk_refs[chunk][...]
        globals_, locals_ = item_counts(lengths_ref)
        acc_ref[...] = jnp.zeros_like(acc_ref)
        low_half = lax.broadcasted_iota(jnp.int32, (1, pair), 1) < head

        def step(item, carry):
            first, offset, length, crop = item_place(item, globals_, locals_, count)
            window = pl.ds(first, WINDOW)
            by_key = lax.broadcasted_iota(jnp.int32, (WINDOW, 1), 0)
            by_query = lax.broadcasted_iota(jnp.int32, (1, WINDOW), 1)
            query_crop = crop_of(by_query, offset, length, crop, -2)
            key_crop = crop_of(by_key, offset, length, crop, -1)
            mask = jnp.where(query_crop == key_crop, 0.0, NEGATIVE)
            inside = key_crop >= 0
            for index in range(local // pair):
                columns = slice(index * pair, (index + 1) * pair)
                q2 = q_ref[window, columns]
                k2 = k_ref[window, columns]
                v2 = v_ref[window, columns]
                g2 = jnp.where(inside, g_ref[window, columns], BF16(0))
                grad_q = grad_k = grad_v = None
                for keep in (low_half, jnp.logical_not(low_half)):
                    kept_k = jnp.where(keep, k2, BF16(0))
                    kept_v = jnp.where(keep, v2, BF16(0))
                    kept_q = jnp.where(keep, q2, BF16(0))
                    kept_g = jnp.where(keep, g2, BF16(0))
                    scores = dot_nt(kept_k, q2) + mask
                    weights = jnp.exp(scores - jnp.max(scores, axis=0, keepdims=True))
                    total = jnp.sum(weights, axis=0, keepdims=True)
                    probability = weights * (1.0 / total)
                    grad_probability = dot_nt(kept_v, g2)
                    delta = jnp.sum(probability * grad_probability, axis=0, keepdims=True)
                    grad_scores = (probability * (grad_probability - delta)).astype(BF16)
                    term_v = dot_nn(probability.astype(BF16), kept_g)
                    term_k = dot_nn(grad_scores, kept_q)
                    term_q = dot_tn(grad_scores, kept_k)
                    grad_v = term_v if grad_v is None else grad_v + term_v
                    grad_k = term_k if grad_k is None else grad_k + term_k
                    grad_q = term_q if grad_q is None else grad_q + term_q
                acc_ref[0, window, columns] += grad_q * scale
                acc_ref[1, window, columns] += grad_k
                acc_ref[2, window, columns] += grad_v
            return carry

        lax.fori_loop(0, item_total(globals_, locals_), step, 0)
        for part in range(3):
            out_ref[:, part * local : (part + 1) * local] = acc_ref[part].astype(BF16)
            bias_ref[part : part + 1] = col_sum(acc_ref[part])

    return call(
        kernel,
        "attend_backward",
        [VMEM, VMEM, VMEM] + [VMEM] * chunks + [SMEM],
        [VMEM, VMEM],
        [shape((count, 3 * local), BF16), shape((3, local), F32)],
        (queries, keys, values, *grad_mixed, lengths),
        after,
        scratch=[pltpu.VMEM((3, count, local), F32), pltpu.VMEM((count, local), BF16)],
        bring=bring,
    )


def gelu_parts(value):
    size = jnp.abs(value)
    bell = jnp.exp(value * value * -0.5)
    t = 1.0 / (1.0 + size * (0.3275911 * 0.7071067811865476))
    poly = t * (
        0.254829592
        + t * (-0.284496736 + t * (1.421413741 + t * (-1.453152027 + t * 1.061405429)))
    )
    tail = 0.5 * poly * bell
    share = jnp.where(value >= 0, 1.0 - tail, tail)
    return value * share, share + value * (bell * 0.3989422804014327)


def hidden_cotangent(cotangent, lengths, table, fc2, halves, chunks, after):
    count, width = cotangent.shape
    units = fc2.shape[0]
    rows = count // chunks
    n_half = len(halves)

    def kernel(c_ref, w_ref, table_ref, lengths_ref, *refs):
        half_refs, refs = refs[:n_half], refs[n_half:]
        gm_hbm, ga_refs, on_refs = refs[0], refs[1 : 1 + chunks], refs[1 + chunks : 1 + chunks + n_half]
        gm_ref, sems = refs[1 + chunks + n_half :]
        copies = Copies(sems)
        stores = []
        for half_ref, on_ref in zip(half_refs, on_refs):
            on_ref[...] = half_ref[...]
        for chunk in range(chunks):
            place = chunk * rows
            grad = c_ref[place : place + rows].astype(F32) * valid_rows(lengths_ref, place, rows)
            low = (grad * table_ref[SCALE_MLP : SCALE_MLP + 1]).astype(BF16)
            gm_ref[place : place + rows] = low
            own = pl.ds(place, rows)
            stores.append(copies.start(gm_ref.at[own], gm_hbm.at[own]))
            ga_refs[chunk][...] = dot_nt(low, w_ref[...]).astype(BF16)
        for copy in stores:
            copy.wait()

    return call(
        kernel,
        "hidden_cotangent",
        [VMEM, VMEM, VMEM, SMEM] + [VMEM] * n_half,
        [ANY] + [VMEM] * (chunks + n_half),
        [pltpu.HBM((count, width), BF16)]
        + [shape((rows, units), BF16)] * chunks
        + [shape(half.shape, BF16) for half in halves],
        (cotangent, fc2, table, lengths, *halves),
        after,
        scratch=[pltpu.VMEM((count, width), BF16), pltpu.SemaphoreType.DMA((chunks,))],
    )


def feed_forward(chunk, rows, mixed, proj, halves, place, tokens, grad_act, table, fc1, fc1_bias, after):
    width = tokens.shape[1]
    units = fc1.shape[1]
    step_units = min(512, units)
    steps = units // step_units
    parts = len(mixed)
    n_half = len(halves)
    depth = proj.shape[0] // 2

    def kernel(*refs):
        mixed_refs, p_ref, half_refs, refs = refs[:parts], refs[parts], refs[parts + 1 : parts + 1 + n_half], refs[parts + 1 + n_half :]
        place_ref, x_hbm, ga_ref, table_ref, fc1_ref, fb_ref = refs[:6]
        mid_hbm, n2_hbm, act_hbm, gh_hbm, fbg_ref, terms_ref, vec_ref, refs = *refs[6:13], refs[13:]
        mid_ref, n2_ref, act_ref, gh_ref, x_ref, sems = refs
        copies = Copies(sems)
        load = copies.start(x_hbm.at[pl.ds(chunk * rows, rows)], x_ref)

        def vector(row):
            return table_ref[row : row + 1]

        attn = vector(PROJ_BIAS) + dot_nn(mixed_refs[0][...], p_ref[...]).astype(BF16).astype(F32)
        for peer in range(parts - 1):
            m_ref = mixed_refs[peer + 1]
            if n_half == parts - 1:
                term = dot_nn(m_ref[...], half_refs[peer][...])
            else:
                first = pl.ds(pl.multiple_of(place_ref[0] * depth, depth), depth)
                other = pl.ds(pl.multiple_of((1 - place_ref[0]) * depth, depth), depth)
                term = dot_nn(m_ref[:, first], half_refs[2 * peer][...])
                term = term + dot_nn(m_ref[:, other], half_refs[2 * peer + 1][...])
            attn = attn + term.astype(BF16).astype(F32)
        load.wait()
        middle = x_ref[...].astype(F32) + vector(SCALE_ATTN) * attn
        mid_ref[...] = middle
        stores = [copies.start(mid_ref, mid_hbm)]
        scaled, _ = norm_parts(middle)
        n2_ref[...] = (scaled * vector(GAIN2) + vector(SHIFT2)).astype(BF16)
        stores.append(copies.start(n2_ref, n2_hbm))

        def hidden_of(j):
            units_j = slice(j * step_units, (j + 1) * step_units)
            return dot_nn(n2_ref[...], fc1_ref[:, units_j]) + fb_ref[:, units_j]

        total = None
        hidden = hidden_of(0)
        for j in range(steps):
            units_j = slice(j * step_units, (j + 1) * step_units)
            later = hidden_of(j + 1) if j + 1 < steps else None
            activated, slope = gelu_parts(hidden)
            own = pl.ds(j * step_units, step_units)
            act_ref[:, units_j] = activated.astype(BF16)
            stores.append(copies.start(act_ref.at[:, own], act_hbm.at[:, own]))
            grad_hidden = ga_ref[:, units_j].astype(F32) * slope
            fbg_ref[:, units_j] = col_sum(grad_hidden)
            low = grad_hidden.astype(BF16)
            gh_ref[:, units_j] = low
            stores.append(copies.start(gh_ref.at[:, own], gh_hbm.at[:, own]))
            term = dot_nt(low, fc1_ref[:, units_j])
            total = term if total is None else total + term
            hidden = later
        low_terms = total.astype(BF16)
        terms_ref[...] = low_terms
        wide = low_terms.astype(F32)
        scaled, _ = norm_parts(mid_ref[...])
        vec_ref[0:1] = col_sum(wide * scaled)
        vec_ref[1:2] = col_sum(wide)
        for copy in stores:
            copy.wait()

    args = (*mixed, proj, *halves, place, tokens, grad_act, table, fc1, fc1_bias)
    return call(
        kernel,
        "feed_forward",
        [VMEM] * (parts + 1 + n_half) + [SMEM, ANY] + [VMEM] * 3 + [COPIED],
        [ANY] * 4 + [VMEM] * 3,
        [
            pltpu.HBM((rows, width), F32),
            pltpu.HBM((rows, width), BF16),
            pltpu.HBM((rows, units), BF16),
            pltpu.HBM((rows, units), BF16),
            shape((1, units), F32),
            shape((rows, width), BF16),
            shape((2, width), F32),
        ],
        args,
        after,
        scratch=[
            pltpu.VMEM((rows, width), F32),
            pltpu.VMEM((rows, width), BF16),
            pltpu.VMEM((rows, units), BF16),
            pltpu.VMEM((rows, units), BF16),
            pltpu.VMEM((rows, width), BF16),
            pltpu.SemaphoreType.DMA((3 + 2 * steps,)),
        ],
    )


def second_projection(activated, fc2, cotangent, lengths, after, bring):
    units, width = fc2.shape
    chunks = len(activated)
    rows = activated[0].shape[0]
    block = min(512, units)
    steps = units // block

    def kernel(begin, *refs):
        a_hbm, refs = refs[:chunks], refs[chunks:]
        w_hbm, c_hbm, lengths_ref, refs = refs[0], refs[1], refs[2], refs[3:]
        out_ref, vec_ref, refs = refs[0], refs[1], refs[2:]
        a_refs, (w_ref, c_ref, sems) = refs[:chunks], refs[chunks:]
        copies = Copies(sems)
        loads = []
        for j in range(steps):
            own = pl.ds(j * block, block)
            loads.append([copies.start(w_hbm.at[own], w_ref.at[own])])
            loads[j].append(copies.start(a_hbm[0].at[:, own], a_refs[0].at[:, own]))
        late = [copies.start(hbm, ref) for hbm, ref in zip(a_hbm[1:], a_refs[1:])]
        late.append(copies.start(c_hbm, c_ref))
        begin()
        for chunk in range(chunks):
            total = None
            if chunk == 0:
                for j in range(steps):
                    for load in loads[j]:
                        load.wait()
                    place = slice(j * block, (j + 1) * block)
                    term = dot_nn(a_refs[0][:, place], w_ref[place])
                    total = term if total is None else total + term
                for load in late:
                    load.wait()
            else:
                total = dot_nn(a_refs[chunk][...], w_ref[...])
            terms = total.astype(BF16)
            place = slice(chunk * rows, (chunk + 1) * rows)
            out_ref[place] = terms
            grad = c_ref[place].astype(F32) * valid_rows(lengths_ref, chunk * rows, rows)
            first, second = col_sum(grad * terms.astype(F32)), col_sum(grad)
            vec_ref[0:1] = first if chunk == 0 else vec_ref[0:1] + first
            vec_ref[1:2] = second if chunk == 0 else vec_ref[1:2] + second

    return call(
        kernel,
        "second_projection",
        [ANY] * (chunks + 2) + [SMEM],
        [VMEM] * 2,
        [shape(cotangent.shape, BF16), shape((2, width), F32)],
        (*activated, fc2, cotangent, lengths),
        after,
        scratch=[pltpu.VMEM((rows, units), BF16)] * chunks
        + [
            pltpu.VMEM(fc2.shape, BF16),
            pltpu.VMEM(cotangent.shape, BF16),
            pltpu.SemaphoreType.DMA((2 * steps + chunks,)),
        ],
        bring=bring,
        late=True,
    )


def weight_grads(normed, grad_hidden, grad_mlp, activated, place, radix, shard, after):
    width = normed[0].shape[1]
    chunks = len(normed)
    rows = normed[0].shape[0]
    units = activated[0].shape[1]
    block = min(512, units)
    slots = 2
    steps = 2 * units // block
    half = steps // 2
    groups = width // (radix * shard)

    def kernel(*refs):
        n_hbm, h_hbm, a_hbm = refs[:chunks], refs[chunks : 2 * chunks], refs[2 * chunks : 3 * chunks]
        g_hbm, place_ref, refs = refs[3 * chunks], refs[3 * chunks + 1], refs[3 * chunks + 2 :]
        out_hbm, (n_ref, g_ref, right_ref, hold_ref, sems) = refs[:radix], refs[radix:]
        copies = Copies(sems)

        def rows_of(chunk):
            return pl.ds(chunk * rows, rows)

        loads = [[] for _ in range(steps)]
        for c in range(chunks):
            loads[0].append(copies.start(n_hbm[c], n_ref.at[rows_of(c)]))
        for step in range(steps):
            own = pl.ds(step % half * block, block)
            if step == half:
                loads[step].append(copies.start(g_hbm, g_ref))
            for c in range(chunks):
                source = (h_hbm if step < half else a_hbm)[c].at[:, own]
                loads[step].append(copies.start(source, right_ref.at[step, rows_of(c)]))
        flying = [[] for _ in range(slots)]
        for step in range(steps):
            for load in loads[step]:
                load.wait()
            total = dot_tn((n_ref if step < half else g_ref)[...], right_ref[step])
            slot = step % slots
            for copy in flying[slot]:
                copy.wait()
            hold_ref[slot] = total.astype(BF16).reshape(groups, radix, shard, block)
            columns = pl.ds(step * block, block)
            flying[slot] = [
                copies.start(
                    hold_ref.at[slot, :, lax.rem(place_ref[0] + part, radix)], out_hbm[part].at[:, :, columns]
                )
                for part in range(radix)
            ]
        for group in flying:
            for copy in group:
                copy.wait()

    return call(
        kernel,
        "weight_grads",
        [ANY] * (3 * chunks + 1) + [SMEM],
        [ANY] * radix,
        [pltpu.HBM((groups, shard, 2 * units), BF16)] * radix,
        (*normed, *grad_hidden, *activated, grad_mlp, place),
        after,
        scratch=[
            pltpu.VMEM((chunks * rows, width), BF16),
            pltpu.VMEM((chunks * rows, width), BF16),
            pltpu.VMEM((steps, chunks * rows, block), BF16),
            pltpu.VMEM((slots, groups, radix, shard, block), BF16),
            pltpu.SemaphoreType.DMA((chunks + 1 + (chunks + radix) * steps,)),
        ],
    )


def attention_grads(normed, grads, grad_attn, mixed, weight, sums, table, raw, share, place, radix, shard, after):
    count, width = normed.shape
    block = max(256, radix * shard)
    wide, local = grads.shape[1], mixed[0].shape[1]
    extra = 128
    total = wide + local + extra
    groups = block // (radix * shard)
    chunks = len(mixed)
    head = 64
    flat_raw = [part for group in raw for part in group]
    n_raw = len(flat_raw)
    units = raw[3][0].shape[1]

    def kernel(n_ref, g_ref, *refs):
        a_refs, m_refs, refs = refs[:chunks], refs[chunks : 2 * chunks], refs[2 * chunks :]
        raw_refs, refs = refs[:n_raw], refs[n_raw:]
        w_ref, s_ref, table_ref, place_ref = refs[:4]
        out_refs, hold_ref, v_ref = refs[4 : 4 + radix], refs[4 + radix], refs[5 + radix]

        def vector(row):
            return table_ref[row : row + 1]

        def both(group):
            first = sum(len(g) for g in raw[:group])
            return sum(ref[...] for ref in raw_refs[first : first + len(raw[group])])

        middle, norm2, result, hidden = both(0), both(1), both(2), both(3)
        v_ref[...] = jnp.zeros_like(v_ref)
        v_ref[0:1] = vector(GAIN1)
        v_ref[1:2] = vector(SHIFT1)
        v_ref[2:3] = middle[0:1] / vector(SCALE_ATTN) * share
        v_ref[3:4] = middle[1:2] * vector(SCALE_ATTN) * share
        v_ref[4:6] = norm2
        v_ref[6:7] = result[0:1] + result[1:2] * vector(FC2_BIAS) * share
        v_ref[7:8] = result[1:2] * vector(SCALE_MLP) * share

        def spread(flats, first):
            stack = [f[:, i * head : (i + 1) * head] for f in flats for i in range(f.shape[1] // head)]
            stack = jnp.concatenate(stack, axis=0)
            for group in range(head // shard):
                piece = stack[:, group * shard : (group + 1) * shard]
                repeat = max(1, 128 // shard)
                piece = jnp.concatenate([piece] * repeat, axis=1)
                piece = jnp.concatenate([piece] * (width // (repeat * shard)), axis=1)
                v_ref[first : first + stack.shape[0]] = piece
                first += stack.shape[0]
            return first

        spread([hidden], spread([s_ref[0:1], s_ref[2:3]], 8))
        lane = lax.broadcasted_iota(jnp.int32, (block, extra), 1)
        for i in range(width // block):
            blk = slice(i * block, (i + 1) * block)
            columns = v_ref[:, blk].T
            first = second = None
            product = dot_tn(n_ref[:, blk], g_ref[...])
            for part in range(3):
                piece = product[:, part * local : (part + 1) * local]
                w = w_ref[part, blk].astype(F32)
                one = jnp.sum(w * piece, axis=1, keepdims=True)
                two = jnp.sum(w * s_ref[part : part + 1], axis=1, keepdims=True)
                first = one if first is None else first + one
                second = two if second is None else second + two
            gain_grad = (first - columns[:, 1:2] * second) / columns[:, 0:1]
            small = jnp.where(lane == 0, gain_grad, jnp.where(lane == 1, second, columns))
            product_p = None
            for c in range(chunks):
                term = dot_tn(a_refs[c][:, blk], m_refs[c][...])
                product_p = term if product_p is None else product_p + term
            hold_ref[:, :, :, :wide] = product.astype(BF16).reshape(groups, radix, shard, wide)
            hold_ref[:, :, :, wide : wide + local] = product_p.astype(BF16).reshape(groups, radix, shard, local)
            hold_ref[:, :, :, wide + local :] = small.astype(BF16).reshape(groups, radix, shard, extra)
            for step in range(radix):
                out_refs[step][i * groups : (i + 1) * groups] = hold_ref[:, lax.rem(place_ref[0] + step, radix)]

    return call(
        kernel,
        "attention_grads",
        [VMEM, VMEM] + [VMEM] * (2 * chunks + n_raw) + [VMEM, VMEM, VMEM, SMEM],
        [VMEM] * radix,
        [shape((width // (radix * shard), shard, total), BF16)] * radix,
        (normed, grads, *grad_attn, *mixed, *flat_raw, weight, sums, table, place),
        after,
        scratch=[pltpu.VMEM((groups, radix, shard, total), BF16), pltpu.VMEM((extra, width), F32)],
    )


def add_stage(parts, place, radix, after):
    left, shard, columns = parts[0].shape
    n_parts = len(parts)

    def kernel(*refs):
        part_refs, place_ref, out_refs = refs[:n_parts], refs[n_parts], refs[n_parts + 1 :]
        for group in range(left // radix):
            for step in range(radix):
                source = group * radix + lax.rem(place_ref[0] + step, radix)
                total = None
                for ref in part_refs:
                    term = ref[source].astype(F32)
                    total = term if total is None else total + term
                out_refs[step][group] = total.astype(BF16)

    return call(
        kernel,
        "add_stage",
        [VMEM] * n_parts + [SMEM],
        [VMEM] * radix,
        [shape((left // radix, shard, columns), BF16)] * radix,
        (*parts, place),
        after,
    )


def add_far_stage(ways, after, name):
    sizes = [(len(way[0]), *way[0][0].shape[:2], way[2], way[3]) for way in ways]
    n_out = sum(size[4] for size in sizes)
    n_ways = len(ways)
    kept = [way[0][0] for way in ways]
    arrived = []
    for way in ways:
        arrived += [array for array in way[0][1:] if not any(array is other for other in arrived)]

    def kernel(*refs):
        hbm, refs = refs[:n_ways], refs[n_ways:]
        arrived_refs, place_refs, refs = refs[: len(arrived)], refs[len(arrived) :][:n_ways], refs[len(arrived) + n_ways :]
        out_hbm, refs = refs[:n_out], refs[n_out:]
        in_refs, out_refs, sems = refs[:n_ways], refs[n_ways : 2 * n_ways], refs[2 * n_ways]
        copies = Copies(sems)
        loads = []
        for w, (_, left, _, columns, radix) in enumerate(sizes):
            _, first, _, _, _, below = ways[w]
            span = radix * below
            loads.append(
                [
                    copies.start(
                        hbm[w].at[pl.ds(high * span, span), :, pl.ds(first, columns)],
                        in_refs[w].at[pl.ds(high * span, span)],
                    )
                    for high in range(left // span)
                ]
            )
        stores = []
        given = 0
        for w, (_, left, _, columns, radix) in enumerate(sizes):
            arrays, first, _, _, _, below = ways[w]
            others = [
                arrived_refs[next(i for i, other in enumerate(arrived) if other is array)] for array in arrays[1:]
            ]
            for group in range(left // radix):
                high, low = divmod(group, below)
                if low == 0:
                    loads[w][high].wait()
                for step in range(radix):
                    digit = lax.rem(place_refs[w][0] + step, radix)
                    source = (high * radix + digit) * below + low
                    total = in_refs[w][source].astype(F32)
                    for ref in others:
                        total = total + ref[source, :, first : first + columns].astype(F32)
                    out_refs[w][step, group] = total.astype(BF16)
                    stores.append(copies.start(out_refs[w].at[step, group], out_hbm[given + step].at[group]))
            given += radix
        for copy in stores:
            copy.wait()

    count = sum(left // (radix * way[5]) + left for (_, left, _, _, radix), way in zip(sizes, ways))
    out, done = call(
        kernel,
        name,
        [ANY] * n_ways + [VMEM] * len(arrived) + [SMEM] * n_ways,
        [ANY] * n_out,
        [pltpu.HBM((left // radix, rows, columns), BF16) for _, left, rows, columns, radix in sizes for _ in range(radix)],
        (*kept, *arrived, *[way[4] for way in ways]),
        after,
        scratch=[pltpu.VMEM((left, rows, columns), BF16) for _, left, rows, columns, _ in sizes]
        + [pltpu.VMEM((radix, left // radix, rows, columns), BF16) for _, left, rows, columns, radix in sizes]
        + [pltpu.SemaphoreType.DMA((count,))],
    )
    split = []
    for size in sizes:
        split.append(out[: size[4]])
        out = out[size[4] :]
    return split, done


def last_far_stage(firsts, seconds, after):
    _, shard, units = firsts[0].shape
    n_first = len(firsts)

    def total_of(refs):
        total = None
        for ref in refs:
            term = ref[0].astype(F32)
            total = term if total is None else total + term
        return total

    def kernel(*refs):
        first_ref, second_ref = refs[-2:]
        first_ref[...] = total_of(refs[:n_first])
        second_ref[...] = total_of(refs[n_first:-2]).T

    return call(
        kernel,
        "last_far_stage",
        [VMEM] * (n_first + len(seconds)),
        [COPIED] * 2,
        [shape((shard, units), F32), shape((units, shard), F32)],
        (*firsts, *seconds),
        after,
    )


def last_stage(parts, local, after):
    _, shard, columns = parts[0].shape
    n_parts = len(parts)
    extra = columns - 4 * local

    def kernel(*refs):
        part_refs, (qkv_ref, proj_ref, small_ref) = refs[:n_parts], refs[n_parts:]
        total = None
        for ref in part_refs:
            term = ref[0].astype(F32)
            total = term if total is None else total + term
        for part in range(3):
            qkv_ref[part] = total[:, part * local : (part + 1) * local]
        proj_ref[...] = total[:, 3 * local : 4 * local].T
        small_ref[...] = total[:, 4 * local :].T

    return call(
        kernel,
        "last_stage",
        [VMEM] * n_parts,
        [COPIED] * 3,
        [shape((3, shard, local), F32), shape((local, shard), F32), shape((extra, shard), F32)],
        tuple(parts),
        after,
    )


def middle_back(chunk, rows, terms, middle, tokens, cotangent, lengths, table, proj, after, bring):
    width = middle.shape[1]
    local = proj.shape[0]
    parts = len(terms)

    def kernel(*refs):
        term_refs, refs = refs[:parts], refs[parts:]
        mid_ref, x_hbm, c_hbm, lengths_ref, table_ref, p_ref = refs[:6]
        gmid_hbm, low_ref, gmix_ref, vec_ref, gmid_ref, x_ref, c_ref, sems = refs[6:]
        copies = Copies(sems)
        own = pl.ds(chunk * rows, rows)
        loads = [copies.start(c_hbm.at[own], c_ref), copies.start(x_hbm.at[own], x_ref)]
        grad_norm = None
        for ref in term_refs:
            term = ref[...].astype(F32)
            grad_norm = term if grad_norm is None else grad_norm + term
        middle = mid_ref[...]
        scaled, inverse = norm_parts(middle)
        back = norm_back(grad_norm, scaled, inverse, table_ref[GAIN2 : GAIN2 + 1])
        loads[0].wait()
        grad = c_ref[...].astype(F32) * valid_rows(lengths_ref, chunk * rows, rows) + back
        gmid_ref[...] = grad
        store = copies.start(gmid_ref, gmid_hbm)
        low = (table_ref[SCALE_ATTN : SCALE_ATTN + 1] * grad).astype(BF16)
        low_ref[...] = low
        gmix_ref[...] = dot_nt(low, p_ref[...]).astype(BF16)
        loads[1].wait()
        vec_ref[0:1] = col_sum(grad * (middle - x_ref[...].astype(F32)))
        vec_ref[1:2] = col_sum(grad)
        store.wait()

    return call(
        kernel,
        f"middle_back_{chunk}",
        [VMEM] * parts + [VMEM, ANY, ANY, SMEM, VMEM, VMEM],
        [ANY] + [VMEM] * 3,
        [
            pltpu.HBM((rows, width), F32),
            shape((rows, width), BF16),
            shape((rows, local), BF16),
            shape((2, width), F32),
        ],
        (*terms, middle, tokens, cotangent, lengths, table, proj),
        after,
        scratch=[
            pltpu.VMEM((rows, width), F32),
            pltpu.VMEM((rows, width), BF16),
            pltpu.VMEM((rows, width), BF16),
            pltpu.SemaphoreType.DMA((3,)),
        ],
        bring=bring,
    )


def first_norm_terms(chunk, rows, grads, weight, after):
    width, local = weight.shape[1:]

    def kernel(g_ref, w_ref, out_ref):
        place = slice(chunk * rows, (chunk + 1) * rows)
        total = None
        for part in range(3):
            term = dot_nt(g_ref[place, part * local : (part + 1) * local], w_ref[part])
            total = term if total is None else total + term
        out_ref[...] = total.astype(BF16)

    return call(
        kernel,
        "first_norm_terms",
        [VMEM, VMEM],
        VMEM,
        shape((rows, width), BF16),
        (grads, weight),
        after,
    )


def to_rows(chunk, rows, compute, args, specs, dims, kept, after, name, sources=()):
    extra = 0 if kept is None else 1
    blocks = 2
    block = rows // blocks
    n_args = len(args)
    n_source = len(sources)
    args, specs = args + tuple(array for array, _ in sources), specs + [ANY] * n_source

    def kernel(*refs):
        ins, refs = refs[:n_args], refs[n_args:]
        source_hbm, refs = refs[:n_source], refs[n_source:]
        out_hbm, hold_ref, sems = refs[extra : extra + 3]
        source_refs = refs[extra + 3 :]
        copies = Copies(sems)
        loads = [
            [
                copies.start(hbm.at[pl.ds(first + i * block, block)], ref.at[i])
                for hbm, ref, (_, first) in zip(source_hbm, source_refs, sources)
            ]
            for i in range(blocks)
        ]
        stores = []
        for i in range(blocks):
            for load in loads[i]:
                load.wait()
            hold_ref[i] = compute(i * block, block, *[ref[i] for ref in source_refs], *ins).astype(BF16)
            place = pl.ds(chunk * rows + i * block, block)
            stores.append(copies.start(hold_ref.at[i], out_hbm.at[place]))
        for copy in stores:
            copy.wait()

    alias = None
    if extra:
        alias = {len(args): 0}
        args = args + (kept,)
    scratch = [
        pltpu.VMEM((blocks, block, dims[1]), BF16),
        pltpu.SemaphoreType.DMA(((1 + n_source) * blocks,)),
        *[pltpu.VMEM((blocks, block, dims[1]), array.dtype) for array, _ in sources],
    ]
    return call(
        kernel,
        name,
        specs + [ANY] * extra,
        ANY,
        pltpu.HBM(dims, BF16),
        args,
        after,
        scratch=scratch,
        alias=alias,
    )


def token_grads(chunk, rows, terms, grad_middle, tokens, table, kept, after):
    parts = len(terms)

    def compute(first, block, x, grad, *refs):
        table_ref = refs[parts]
        place = slice(first, first + block)
        grad_norm = None
        for ref in refs[:parts]:
            term = ref[place].astype(F32)
            grad_norm = term if grad_norm is None else grad_norm + term
        scaled, inverse = norm_parts(x.astype(F32))
        return grad + norm_back(grad_norm, scaled, inverse, table_ref[GAIN1 : GAIN1 + 1])

    args = (*terms, table)
    specs = [VMEM] * (parts + 1)
    sources = ((tokens, chunk * rows), (grad_middle, 0))
    return to_rows(chunk, rows, compute, args, specs, tokens.shape, kept, after, "token_grads", sources)


def layer_output(terms, middle, lengths, table, after):
    parts = len(terms)
    count, width = terms[0].shape
    chunks = len(middle)
    rows = count // chunks
    blocks = 2
    block = rows // blocks

    def kernel(*refs):
        term_refs, mid_hbm, refs = refs[:parts], refs[parts : parts + chunks], refs[parts + chunks :]
        lengths_ref, table_ref, out_hbm, mid_ref, hold_ref, sems = refs
        copies = Copies(sems)
        loads = [
            copies.start(
                mid_hbm[i // blocks].at[pl.ds(i % blocks * block, block)], mid_ref.at[pl.ds(i * block, block)]
            )
            for i in range(chunks * blocks)
        ]
        stores = []
        for i in range(chunks * blocks):
            place = slice(i * block, (i + 1) * block)
            mlp = table_ref[FC2_BIAS : FC2_BIAS + 1]
            for ref in term_refs:
                mlp = mlp + ref[place].astype(F32)
            loads[i].wait()
            valid = valid_rows(lengths_ref, i * block, block)
            full = mid_ref[place] + table_ref[SCALE_MLP : SCALE_MLP + 1] * mlp
            hold_ref[place] = (valid * full).astype(BF16)
            own = pl.ds(i * block, block)
            stores.append(copies.start(hold_ref.at[own], out_hbm.at[own]))
        for copy in stores:
            copy.wait()

    return call(
        kernel,
        "layer_output",
        [VMEM] * parts + [ANY] * chunks + [SMEM, VMEM],
        ANY,
        pltpu.HBM((count, width), BF16),
        (*terms, *middle, lengths, table),
        after,
        scratch=[
            pltpu.VMEM((count, width), F32),
            pltpu.VMEM((count, width), BF16),
            pltpu.SemaphoreType.DMA((2 * chunks * blocks,)),
        ],
    )


def from_peers(array):
    size = lax.axis_size("tensor")
    return [
        lax.ppermute(array, "tensor", [(i, (i + step) % size) for i in range(size)])
        for step in range(1, size)
    ]


def other_of_pair(array):
    return lax.ppermute(array, "dp", [(i, i ^ 1) for i in range(lax.axis_size("dp"))])


def radices(size):
    found = []
    if size % 2 == 0:
        found.append(2)
        size //= 2
    while size > 1:
        step = 2 if size % 4 and size % 2 == 0 or size == 8 else next((r for r in (4, 3) if size % r == 0), size)
        found.append(step)
        size //= step
    return found


def small_digits(size, stride):
    digits = []
    while stride < size:
        left = size // stride
        radix = next(r for r in (2, 3, 5, left) if left % r == 0)
        digits.append((stride, radix))
        stride *= radix
    return digits


def exchange(parts, stride, radix):
    size = lax.axis_size("dp")
    arrived = []
    for step in range(1, radix):
        moves = []
        for i in range(size):
            at = (i // stride) % radix
            moves.append((i, i + ((at + step) % radix - at) * stride))
        arrived.append(lax.ppermute(parts[step], "dp", moves))
    return [parts[0]] + arrived


def body(
    tokens,
    lengths,
    norm1_gain,
    norm1_bias,
    qkv_weight,
    qv_bias,
    proj_weight,
    proj_bias,
    scale_attn,
    norm2_gain,
    norm2_bias,
    fc1_weight,
    fc1_bias,
    fc2_weight,
    fc2_bias,
    scale_mlp,
    cotangent,
):
    count, width = tokens.shape
    heads, head_size = qv_bias.shape[1:]
    local = heads * head_size
    units = fc1_weight.shape[1]
    tensor = lax.axis_size("tensor")
    dp = lax.axis_size("dp")
    chunks = 2
    rows = count // chunks
    scale = head_size**-0.5

    def flat(vector):
        return vector.reshape(1, -1)

    index = lax.axis_index("dp")
    steps = radices(dp)
    strides = [1]
    for step in steps:
        strides.append(strides[-1] * step)
    places = [((index // stride) % step).reshape(1) for stride, step in zip(strides, steps)]

    half_rows = local // 2
    paired = dp % 2 == 0 and half_rows % 128 == 0
    half_place = (index % 2).reshape(1)
    half = proj_weight
    if paired:
        half = lax.dynamic_slice_in_dim(proj_weight, half_place[0] * half_rows, half_rows, 0)
    halves = from_peers(half)
    vectors = (norm1_gain, norm1_bias, norm2_gain, norm2_bias, proj_bias, scale_attn, fc2_bias, scale_mlp)
    out, done = attend_forward(
        tokens,
        lengths,
        [flat(vector) for vector in vectors],
        qkv_weight,
        qv_bias,
        scale,
        chunks,
        (cotangent, fc2_weight, proj_weight, fc1_weight),
    )
    queries, keys, values, normed1, table, cotangent_near, fc2_near, proj_weight, fc1_weight = out[:9]
    mixed = out[9:]
    mixed_parts = [[part] + from_peers(part) for part in mixed]
    out, done = hidden_cotangent(cotangent_near, lengths, table, fc2_near, halves, chunks, done)
    grad_mlp, grad_act, halves = out[0], out[1 : 1 + chunks], out[1 + chunks :]
    if paired:
        halves = [part for half in halves for part in (half, other_of_pair(half))]

    middle, normed2, activated, grad_hidden, norm2_parts = [], [], [], [], []
    raw = [[], [], [], []]
    for chunk in range(chunks):
        out, done = feed_forward(
            chunk,
            rows,
            mixed_parts[chunk],
            proj_weight,
            halves,
            half_place,
            tokens,
            grad_act[chunk],
            table,
            fc1_weight,
            flat(fc1_bias),
            done,
        )
        for group, part in zip((middle, normed2, activated, grad_hidden), out[:4]):
            group.append(part)
        raw[3].append(out[4])
        raw[1].append(out[6])
        norm2_parts.append([out[5]] + from_peers(out[5]))

    shard = width // dp
    fc_parts, done = weight_grads(
        normed2, grad_hidden, grad_mlp, activated, places[0], steps[0], shard, done
    )
    fc_parts = exchange(fc_parts, 1, steps[0])

    def near_stage(parts, stage, done):
        parts, done = add_stage(parts, places[stage], steps[stage], done)
        return exchange(parts, strides[stage], steps[stage]), done

    out, done = second_projection(activated, fc2_weight, cotangent, lengths, done, middle)
    mlp_parts = [out[0]] + from_peers(out[0])
    raw[2].append(out[1])
    middle_near = out[2:]

    grad_middle, grad_attn, grad_mixed = [], [], []
    for chunk in range(chunks):
        out, done = middle_back(
            chunk,
            rows,
            norm2_parts[chunk],
            middle_near[chunk],
            tokens,
            cotangent,
            lengths,
            table,
            proj_weight,
            done,
            (queries, keys, values) if chunk == 0 else (),
        )
        if chunk == 0:
            queries, keys, values = out[4:]
        for group, part in zip((grad_middle, grad_attn, grad_mixed), out[:3]):
            group.append(part)
        raw[0].append(out[3])
    stages = len(steps)
    digits = small_digits(dp, strides[1])
    orders = [digits, digits[1:] + digits[:1]]

    def far_stage(at, firsts, seconds, start, done):
        ways = []
        for arrays, first, order in ((firsts, 0, orders[0]), (seconds, start, orders[1])):
            stride, radix = order[at]
            below = 1
            for other_stride, other_radix in order[at:]:
                below *= other_radix if other_stride < stride else 1
            place = ((index // stride) % radix).reshape(1)
            ways.append((arrays, first, units, radix, place, below))
        split, done = add_far_stage(ways, done, f"add_far_stage_{at}")
        return [exchange(parts, *order[at]) for parts, order in zip(split, orders)], done

    (firsts, seconds), done = far_stage(0, fc_parts, fc_parts, units, done)
    (grads, grad_sums, qkv_weight, normed1), done = attend_backward(
        queries, keys, values, grad_mixed, lengths, scale, done, (qkv_weight, normed1)
    )
    parts, done = attention_grads(
        normed1,
        grads,
        grad_attn,
        mixed,
        qkv_weight,
        grad_sums,
        table,
        raw,
        1.0 / tensor,
        places[0],
        steps[0],
        shard,
        done,
    )
    parts = exchange(parts, 1, steps[0])
    norm1_parts = []
    for chunk in range(chunks):
        terms, done = first_norm_terms(chunk, rows, grads, qkv_weight, done)
        norm1_parts.append([terms] + from_peers(terms))
    output, done = layer_output(mlp_parts, middle, lengths, table, done)
    at = 1
    if at < len(digits):
        (firsts, seconds), done = far_stage(at, firsts, seconds, 0, done)
        at += 1
    stage = 1
    if stage < stages:
        parts, done = near_stage(parts, stage, done)
        stage += 1
    grad_tokens = None
    for chunk in range(chunks - 1):
        grad_tokens, done = token_grads(
            chunk, rows, norm1_parts[chunk], grad_middle[chunk], tokens, table, grad_tokens, done
        )
    while at < len(digits):
        (firsts, seconds), done = far_stage(at, firsts, seconds, 0, done)
        at += 1
    while stage < stages:
        parts, done = near_stage(parts, stage, done)
        stage += 1
    grad_tokens, done = token_grads(
        chunks - 1, rows, norm1_parts[-1], grad_middle[-1], tokens, table, grad_tokens, done
    )
    (fc1_grad, fc2_grad), done = last_far_stage(firsts, seconds, done)
    (qkv_grad, proj_grad, small), done = last_stage(parts, local, done)

    vector_share = small[:8]
    for other in from_peers(vector_share):
        vector_share = vector_share + other
    own = shard // tensor
    vector_share = lax.dynamic_slice_in_dim(vector_share, lax.axis_index("tensor") * own, own, 1)

    def columns_of(first, heads_in):
        groups = head_size // shard
        pieces = [small[first + i * heads_in : first + (i + 1) * heads_in] for i in range(groups)]
        every = pieces[0] if groups == 1 else jnp.concatenate(pieces, axis=1)
        return lax.dynamic_slice_in_dim(every, index * (head_size // dp), head_size // dp, 1)

    bias_share = columns_of(8, 2 * heads).reshape(2, heads, -1)
    fc1_share = columns_of(8 + 2 * heads * (head_size // shard), units // head_size)

    return (
        output,
        grad_tokens,
        vector_share[0],
        vector_share[1],
        qkv_grad,
        bias_share,
        proj_grad,
        vector_share[3],
        vector_share[2],
        vector_share[4],
        vector_share[5],
        fc1_grad,
        fc1_share,
        fc2_grad,
        vector_share[7],
        vector_share[6],
    )


def solution(mesh):
    in_specs = (
        P("dp", None),
        P("dp", None),
        P(),
        P(),
        P(None, None, "tensor"),
        P(None, "tensor", None),
        P("tensor", None),
        P(),
        P(),
        P(),
        P(),
        P(None, "tensor"),
        P("tensor"),
        P("tensor", None),
        P(),
        P(),
        P("dp", None),
    )
    out_specs = (
        P("dp", None),
        P("dp", None),
        P(("dp", "tensor")),
        P(("dp", "tensor")),
        P(None, "dp", "tensor"),
        P(None, "tensor", "dp"),
        P("tensor", "dp"),
        P(("dp", "tensor")),
        P(("dp", "tensor")),
        P(("dp", "tensor")),
        P(("dp", "tensor")),
        P("dp", "tensor"),
        P("tensor", "dp"),
        P("tensor", "dp"),
        P(("dp", "tensor")),
        P(("dp", "tensor")),
    )
    return jax.shard_map(body, mesh=mesh, in_specs=in_specs, out_specs=out_specs, check_vma=False)
```

```python
from functools import partial

import jax
import jax.numpy as jnp
from jax import lax
from jax.experimental import pallas as pl
from jax.experimental.pallas import tpu as pltpu
from jax.sharding import PartitionSpec as P

EPS = 1e-06
NEGATIVE = -1e30
GLOBAL_LEN = 197
LOCAL_LEN = 37
GROUP = GLOBAL_LEN // LOCAL_LEN
WINDOW = 224
BF16 = jnp.bfloat16
F32 = jnp.float32
MIB = 1 << 20
VMEM_MIB = 16
SPARE = 6
LIMITS = {
    "attend_forward": 14,
    "attend_rest": 6,
    "hidden_cotangent": 6,
    "feed_forward": 15,
    "weight_grads": 17,
    "second_projection": 18,
    "middle_back": 13,
    "attend_backward": 11,
    "attention_grads": 14,
    "layer_output": 13,
    "first_norm_terms": 9,
    "add_stage": 8,
    "token_grads": 9,
    "last_stage": 8,
    "last_far_stage": 8,
    "wait_for": 1,
    "add_far_stage": 16,
}
COST = 2300000000
COSTS = {"middle_back_1": 46000000000, "wait_for": 16100000000, "token_grads_0": 13800000000}


def dot_nn(a, b):
    return lax.dot_general(a, b, (((1,), (0,)), ((), ())), preferred_element_type=F32)


def dot_nt(a, b):
    return lax.dot_general(a, b, (((1,), (1,)), ((), ())), preferred_element_type=F32)


def dot_tn(a, b):
    return lax.dot_general(a, b, (((0,), (0,)), ((), ())), preferred_element_type=F32)


def norm_parts(values):
    average = jnp.mean(values, axis=-1, keepdims=True)
    centered = values - average
    inverse = lax.rsqrt(jnp.mean(centered * centered, axis=-1, keepdims=True) + EPS)
    return centered * inverse, inverse


def norm_back(grad_norm, scaled, inverse, gain):
    grad_hat = grad_norm * gain
    first_mean = jnp.mean(grad_hat, axis=-1, keepdims=True)
    second_mean = jnp.mean(grad_hat * scaled, axis=-1, keepdims=True)
    return inverse * (grad_hat - first_mean - scaled * second_mean)


def col_sum(values):
    return jnp.sum(values, axis=0, keepdims=True)


def call(kernel, name, in_specs, out_specs, out_shape, args, after=None, scratch=(), vmem=VMEM_MIB, alias=None, bring=(), late=False, ties=()):
    single = not isinstance(out_shape, list)
    if single:
        out_specs, out_shape = [out_specs], [out_shape]
    n_in, n_out, n_bring = len(args), len(out_shape), len(bring)
    after = list(ties) if after is None else [after, *ties]
    n_after = len(after)
    args = [
        pltpu.with_memory_space_constraint(arg, pltpu.VMEM if spec is VMEM else pltpu.HBM)
        if spec is VMEM or spec is ANY
        else arg
        for arg, spec in zip(args, in_specs)
    ]
    args += [pltpu.with_memory_space_constraint(arg, pltpu.HBM) for arg in bring]
    out_shape = [
        pltpu.VMEM(o.shape, o.dtype) if spec is VMEM else o for o, spec in zip(out_shape, out_specs)
    ]

    def ordered(*refs):
        ins, refs = refs[:n_in], refs[n_in:]
        bring_hbm, refs = refs[:n_bring], refs[n_bring + n_after :]
        outs, refs = refs[:n_out], refs[n_out:]
        bring_refs, done, refs = refs[:n_bring], refs[n_bring], refs[n_bring + 1 :]
        done[...] = jnp.zeros_like(done)
        loads = []
        if n_bring:
            refs, sems = refs[:-1], refs[-1]

        def begin():
            for i in range(n_bring):
                loads.append(pltpu.make_async_copy(bring_hbm[i], bring_refs[i], sems.at[i]))
                loads[-1].start()

        if late:
            kernel(begin, *ins, *outs, *refs)
        else:
            begin()
            kernel(*ins, *outs, *refs)
        for load in loads:
            load.wait()

    out = pl.pallas_call(
        ordered,
        in_specs=list(in_specs) + [ANY] * (n_bring + n_after),
        out_specs=list(out_specs) + [VMEM] * (n_bring + 1),
        out_shape=list(out_shape) + [pltpu.VMEM(a.shape, a.dtype) for a in bring] + [pltpu.VMEM((8, 128), F32)],
        scratch_shapes=list(scratch) + ([pltpu.SemaphoreType.DMA((n_bring,))] if n_bring else []),
        input_output_aliases=alias or {},
        compiler_params=pltpu.CompilerParams(vmem_limit_bytes=(LIMITS.get(name.rstrip("_0123456789"), vmem) + SPARE) * MIB),
        cost_estimate=pl.CostEstimate(flops=COSTS.get(name, COST), bytes_accessed=COST, transcendentals=0),
        name=name,
    )(*args, *after)
    return (out[0] if single and not n_bring else out[:-1]), out[-1]


class Copies:
    def __init__(self, sems):
        self.sems = sems
        self.used = 0

    def start(self, source, target):
        copy = pltpu.make_async_copy(source, target, self.sems.at[self.used])
        self.used += 1
        copy.start()
        return copy


def shape(dims, dtype):
    return jax.ShapeDtypeStruct(dims, dtype)


SMEM = pl.BlockSpec(memory_space=pltpu.SMEM)
VMEM = pl.BlockSpec(memory_space=pltpu.VMEM)
ANY = pl.BlockSpec(memory_space=pl.ANY)
COPIED = pl.BlockSpec(memory_space=pltpu.VMEM)

GAIN1, SHIFT1, GAIN2, SHIFT2, PROJ_BIAS, SCALE_ATTN, FC2_BIAS, SCALE_MLP = range(8)


def row_total(lengths_ref):
    total = jnp.int32(0)
    for slot in range(lengths_ref.shape[1]):
        total = total + lengths_ref[0, slot]
    return total


def valid_rows(lengths_ref, first, rows):
    places = lax.broadcasted_iota(jnp.int32, (rows, 1), 0) + first
    return (places < row_total(lengths_ref)).astype(F32)


def item_counts(lengths_ref):
    globals_ = jnp.int32(0)
    locals_ = jnp.int32(0)
    for slot in range(lengths_ref.shape[1]):
        value = lengths_ref[0, slot]
        globals_ = globals_ + jnp.where(value == GLOBAL_LEN, 1, 0)
        locals_ = locals_ + jnp.where(value == LOCAL_LEN, 1, 0)
    return globals_, locals_


def item_place(item, globals_, locals_, count):
    is_global = item < globals_
    group = item - globals_
    start = jnp.where(
        is_global, item * GLOBAL_LEN, globals_ * GLOBAL_LEN + group * (GROUP * LOCAL_LEN)
    )
    length = jnp.where(
        is_global, GLOBAL_LEN, jnp.minimum(locals_ - group * GROUP, GROUP) * LOCAL_LEN
    )
    crop = jnp.where(is_global, GLOBAL_LEN, LOCAL_LEN)
    first = jnp.minimum((start // 16) * 16, count - WINDOW)
    return pl.multiple_of(first, 16), start - first, length, crop


def crop_of(places, offset, length, crop, outside):
    inside = (places >= offset) & (places < offset + length)
    index = places - offset
    label = jnp.zeros_like(places)
    for step in range(1, GROUP):
        label = label + jnp.where(index >= step * crop, 1, 0)
    return jnp.where(inside, label, outside)


def item_total(globals_, locals_):
    return globals_ + (locals_ + GROUP - 1) // GROUP


def attend_items(first_item, last_item, q_ref, k_ref, v_ref, out_ref, skipped, lengths_ref):
    count, local = q_ref.shape
    pair = 128
    pairs = local // pair
    globals_, locals_ = item_counts(lengths_ref)
    low_half = lax.broadcasted_iota(jnp.int32, (1, pair), 1) < pair // 2

    def step(item, carry):
        first, offset, length, crop = item_place(item, globals_, locals_, count)
        window = pl.ds(first, WINDOW)
        placed = pl.ds(pl.multiple_of(first - skipped, 16), WINDOW)
        by_key = lax.broadcasted_iota(jnp.int32, (WINDOW, 1), 0)
        by_query = lax.broadcasted_iota(jnp.int32, (1, WINDOW), 1)
        query_crop = crop_of(by_query, offset, length, crop, -2)
        key_crop = crop_of(by_key, offset, length, crop, -1)
        mask = jnp.where(query_crop == key_crop, 0.0, NEGATIVE)
        inside = key_crop >= 0

        def products(index):
            columns = slice(index * pair, (index + 1) * pair)
            return dot_nt(heads_apart(k_ref[window, columns], low_half), q_ref[window, columns])

        now = products(0)
        for index in range(pairs):
            columns = slice(index * pair, (index + 1) * pair)
            later = products(index + 1) if index + 1 < pairs else None
            scores = now.reshape(2, WINDOW, WINDOW) + mask
            weights = jnp.exp(scores - jnp.max(scores, axis=1, keepdims=True))
            total = jnp.sum(weights, axis=1, keepdims=True)
            low = (weights * (1.0 / total)).astype(BF16).reshape(2 * WINDOW, WINDOW)
            out = dot_tn(low, heads_apart(v_ref[window, columns], low_half))
            now = later
            kept = out_ref[placed, columns].astype(F32)
            out_ref[placed, columns] = jnp.where(inside, out, kept).astype(BF16)
        return carry

    lax.fori_loop(first_item, jnp.minimum(last_item, item_total(globals_, locals_)), step, 0)


def attend_forward(tokens, lengths, vectors, weight, qv_bias, scale, rows, later):
    count, width = tokens.shape
    local = weight.shape[2]
    head = 64
    block = 256
    blocks = count // block
    n_vec, n_later = len(vectors), len(later)

    def kernel(x_hbm, w_hbm, *refs):
        later_hbm, refs = refs[:n_later], refs[n_later:]
        vec_hbm, refs = refs[:n_vec], refs[n_vec:]
        qv_hbm, lengths_ref, refs = refs[0], refs[1], refs[2:]
        q_hbm, k_hbm, v_hbm, n_hbm, q_ref, k_ref, v_ref, table_ref, refs = *refs[:8], refs[8:]
        later_refs, (first_ref, rest_ref), refs = refs[:n_later], refs[n_later : n_later + 2], refs[n_later + 2 :]
        vec_refs, refs = refs[:n_vec], refs[n_vec:]
        heads_ref, x_ref, w_ref, n_ref, out_ref, sems = refs
        copies = Copies(sems)

        def part(ref, index):
            return ref.at[pl.ds(index * block, block)]

        loads = [copies.start(part(x_hbm, 0), part(x_ref, 0))]
        small_loads = [copies.start(hbm, ref) for hbm, ref in zip(vec_hbm[:2], vec_refs[:2])]
        weight_loads = [copies.start(w_hbm.at[0], w_ref.at[0])]
        small_loads.append(copies.start(qv_hbm, heads_ref))
        weight_loads += [copies.start(w_hbm.at[i], w_ref.at[i]) for i in range(1, 3)]
        loads += [copies.start(part(x_hbm, i), part(x_ref, i)) for i in range(1, blocks)]
        table_loads = [copies.start(hbm, ref) for hbm, ref in zip(vec_hbm[2:], vec_refs[2:])]
        later_loads = [copies.start(hbm, ref) for hbm, ref in zip(later_hbm, later_refs)]

        def scaled_of(i):
            loads[i].wait()
            return norm_parts(x_ref[i * block : (i + 1) * block].astype(F32))[0]

        def normed_of(i):
            return (scaled_of(i) * vec_refs[GAIN1][...] + vec_refs[SHIFT1][...]).astype(BF16)

        scaled = scaled_of(0)
        for load in small_loads:
            load.wait()
        qv = [
            jnp.concatenate([heads_ref[i, h : h + 1] for h in range(local // head)], axis=1)
            for i in range(2)
        ]
        now = (scaled * vec_refs[GAIN1][...] + vec_refs[SHIFT1][...]).astype(BF16)
        for i in range(blocks):
            rows_i = slice(i * block, (i + 1) * block)
            after = normed_of(i + 1) if i + 1 < blocks else None
            n_ref[rows_i] = now
            if i == 0:
                weight_loads[0].wait()
            queries = (dot_nn(now, w_ref[0]) + qv[0]).astype(BF16)
            q_ref[rows_i] = queries * BF16(scale)
            if i == 0:
                weight_loads[1].wait()
            k_ref[rows_i] = dot_nn(now, w_ref[1]).astype(BF16)
            if i == 0:
                weight_loads[2].wait()
            v_ref[rows_i] = (dot_nn(now, w_ref[2]) + qv[1]).astype(BF16)
            now = after
        stores = [
            copies.start(ref, hbm)
            for ref, hbm in ((q_ref, q_hbm), (k_ref, k_hbm), (v_ref, v_hbm), (n_ref, n_hbm))
        ]
        average = col_sum(v_ref[...].astype(F32)) * (1.0 / count)
        out_ref[...] = jnp.broadcast_to(average, (count, local)).astype(BF16)
        attend_items(0, first_items(rows), q_ref, k_ref, v_ref, out_ref, 0, lengths_ref)
        first_ref[...] = out_ref[:rows]
        rest_ref[...] = out_ref[rows:]
        for load in table_loads:
            load.wait()
        for i in range(n_vec):
            table_ref[i : i + 1] = vec_refs[i][...]
        for copy in later_loads + stores:
            copy.wait()

    part = pltpu.HBM((count, local), BF16)
    near = shape((count, local), BF16)
    outs = [part, part, part, pltpu.HBM((count, width), BF16), near, near, near, shape((n_vec, width), F32)]
    outs += [shape(a.shape, a.dtype) for a in later] + [shape((rows, local), BF16), shape((count - rows, local), BF16)]
    args = (tokens, weight, *later, *vectors, qv_bias, lengths)
    return call(
        kernel,
        "attend_forward",
        [ANY] * (len(args) - 1) + [SMEM],
        [ANY] * 4 + [VMEM] * (len(outs) - 4),
        outs,
        args,
        scratch=[pltpu.VMEM((1, width), F32)] * n_vec
        + [
            pltpu.VMEM(qv_bias.shape, F32),
            pltpu.VMEM((count, width), BF16),
            pltpu.VMEM(weight.shape, BF16),
            pltpu.VMEM((count, width), BF16),
            pltpu.VMEM((count, local), BF16),
            pltpu.SemaphoreType.DMA((blocks + 8 + n_later + n_vec,)),
        ],
    )


def first_items(rows):
    return -(-rows // (GROUP * LOCAL_LEN))


def attend_rest(queries, keys, values, rest, lengths, after):
    rows = queries.shape[0] - rest.shape[0]

    def kernel(q_ref, k_ref, v_ref, rest_ref, lengths_ref, out_ref):
        out_ref[...] = rest_ref[...]
        attend_items(first_items(rows), 1 << 20, q_ref, k_ref, v_ref, out_ref, rows, lengths_ref)

    return call(
        kernel,
        "attend_rest",
        [VMEM] * 4 + [SMEM],
        VMEM,
        shape(rest.shape, BF16),
        (queries, keys, values, rest, lengths),
        after,
    )


def heads_apart(both, low_half):
    return jnp.concatenate([jnp.where(low_half, both, BF16(0)), jnp.where(low_half, BF16(0), both)], axis=0)


def heads_together(apart, low_half):
    return jnp.where(low_half, apart[:WINDOW], apart[WINDOW:])


def attend_backward(queries, keys, values, grad_mixed, lengths, scale, after, bring):
    count, local = queries.shape
    head = 64
    pair = 2 * head

    chunks = len(grad_mixed)
    rows = count // chunks

    def kernel(q_ref, k_ref, v_ref, *refs):
        chunk_refs, refs = refs[:chunks], refs[chunks:]
        lengths_ref, out_ref, bias_ref, acc_ref, g_ref = refs
        for chunk in range(chunks):
            g_ref[chunk * rows : (chunk + 1) * rows] = chunk_refs[chunk][...]
        globals_, locals_ = item_counts(lengths_ref)
        acc_ref[...] = jnp.zeros_like(acc_ref)
        low_half = lax.broadcasted_iota(jnp.int32, (1, pair), 1) < head

        def step(item, carry):
            first, offset, length, crop = item_place(item, globals_, locals_, count)
            window = pl.ds(first, WINDOW)
            by_key = lax.broadcasted_iota(jnp.int32, (WINDOW, 1), 0)
            by_query = lax.broadcasted_iota(jnp.int32, (1, WINDOW), 1)
            query_crop = crop_of(by_query, offset, length, crop, -2)
            key_crop = crop_of(by_key, offset, length, crop, -1)
            mask = jnp.where(query_crop == key_crop, 0.0, NEGATIVE)
            inside = key_crop >= 0
            def products(index):
                columns = slice(index * pair, (index + 1) * pair)
                q2 = q_ref[window, columns]
                g2 = jnp.where(inside, g_ref[window, columns], BF16(0))
                both_k = heads_apart(k_ref[window, columns], low_half)
                both_v = heads_apart(v_ref[window, columns], low_half)
                return q2, g2, both_k, dot_nt(both_k, q2), dot_nt(both_v, g2)

            pairs = local // pair
            now = products(0)
            for index in range(pairs):
                columns = slice(index * pair, (index + 1) * pair)
                later = products(index + 1) if index + 1 < pairs else None
                q2, g2, both_k, scores, grad_probability = now
                now = later
                scores = scores.reshape(2, WINDOW, WINDOW) + mask
                weights = jnp.exp(scores - jnp.max(scores, axis=1, keepdims=True))
                total = jnp.sum(weights, axis=1, keepdims=True)
                probability = weights * (1.0 / total)
                grad_probability = grad_probability.reshape(2, WINDOW, WINDOW)
                delta = jnp.sum(probability * grad_probability, axis=1, keepdims=True)
                grad_scores = (probability * (grad_probability - delta)).astype(BF16)
                grad_scores = grad_scores.reshape(2 * WINDOW, WINDOW)
                low = probability.astype(BF16).reshape(2 * WINDOW, WINDOW)
                grad_v = heads_together(dot_nn(low, g2), low_half)
                grad_k = heads_together(dot_nn(grad_scores, q2), low_half)
                grad_q = dot_tn(grad_scores, both_k)
                acc_ref[0, window, columns] += grad_q * scale
                acc_ref[1, window, columns] += grad_k
                acc_ref[2, window, columns] += grad_v
            return carry

        lax.fori_loop(0, item_total(globals_, locals_), step, 0)
        for part in range(3):
            out_ref[:, part * local : (part + 1) * local] = acc_ref[part].astype(BF16)
            bias_ref[part : part + 1] = col_sum(acc_ref[part])

    return call(
        kernel,
        "attend_backward",
        [VMEM, VMEM, VMEM] + [VMEM] * chunks + [SMEM],
        [VMEM, VMEM],
        [shape((count, 3 * local), BF16), shape((3, local), F32)],
        (queries, keys, values, *grad_mixed, lengths),
        after,
        scratch=[pltpu.VMEM((3, count, local), F32), pltpu.VMEM((count, local), BF16)],
        bring=bring,
    )


def gelu_parts(value):
    size = jnp.abs(value)
    bell = jnp.exp(value * value * -0.5)
    t = 1.0 / (1.0 + size * (0.3275911 * 0.7071067811865476))
    poly = t * (
        0.254829592
        + t * (-0.284496736 + t * (1.421413741 + t * (-1.453152027 + t * 1.061405429)))
    )
    tail = 0.5 * poly * bell
    share = jnp.where(value >= 0, 1.0 - tail, tail)
    return value * share, share + value * (bell * 0.3989422804014327)


def hidden_cotangent(cotangent, lengths, table, fc2, halves, chunks, after):
    count, width = cotangent.shape
    units = fc2.shape[0]
    rows = count // chunks
    n_half = len(halves)

    def kernel(c_ref, w_ref, table_ref, lengths_ref, *refs):
        half_refs, refs = refs[:n_half], refs[n_half:]
        gm_hbm, ga_refs, on_refs = refs[0], refs[1 : 1 + chunks], refs[1 + chunks : 1 + chunks + n_half]
        gm_ref, sems = refs[1 + chunks + n_half :]
        copies = Copies(sems)
        stores = []
        for half_ref, on_ref in zip(half_refs, on_refs):
            on_ref[...] = half_ref[...]
        for chunk in range(chunks):
            place = chunk * rows
            grad = c_ref[place : place + rows].astype(F32) * valid_rows(lengths_ref, place, rows)
            low = (grad * table_ref[SCALE_MLP : SCALE_MLP + 1]).astype(BF16)
            gm_ref[place : place + rows] = low
            own = pl.ds(place, rows)
            stores.append(copies.start(gm_ref.at[own], gm_hbm.at[own]))
            ga_refs[chunk][...] = dot_nt(low, w_ref[...]).astype(BF16)
        for copy in stores:
            copy.wait()

    return call(
        kernel,
        "hidden_cotangent",
        [VMEM, VMEM, VMEM, SMEM] + [VMEM] * n_half,
        [ANY] + [VMEM] * (chunks + n_half),
        [pltpu.HBM((count, width), BF16)]
        + [shape((rows, units), BF16)] * chunks
        + [shape(half.shape, BF16) for half in halves],
        (cotangent, fc2, table, lengths, *halves),
        after,
        scratch=[pltpu.VMEM((count, width), BF16), pltpu.SemaphoreType.DMA((chunks,))],
    )


def feed_forward(chunk, rows, mixed, proj, halves, place, tokens, grad_act, table, fc1, fc1_bias, after):
    width = tokens.shape[1]
    units = fc1.shape[1]
    step_units = min(512, units)
    steps = units // step_units
    parts = len(mixed)
    n_half = len(halves)
    depth = proj.shape[0] // 2

    def kernel(*refs):
        mixed_refs, p_ref, half_refs, refs = refs[:parts], refs[parts], refs[parts + 1 : parts + 1 + n_half], refs[parts + 1 + n_half :]
        place_ref, x_hbm, ga_ref, table_ref, fc1_ref, fb_ref = refs[:6]
        mid_hbm, n2_hbm, act_hbm, gh_hbm, fbg_ref, terms_ref, vec_ref, refs = *refs[6:13], refs[13:]
        mid_ref, n2_ref, act_ref, gh_ref, x_ref, sems = refs
        copies = Copies(sems)
        load = copies.start(x_hbm.at[pl.ds(chunk * rows, rows)], x_ref)

        def vector(row):
            return table_ref[row : row + 1]

        attn = vector(PROJ_BIAS) + dot_nn(mixed_refs[0][...], p_ref[...]).astype(BF16).astype(F32)
        for peer in range(parts - 1):
            m_ref = mixed_refs[peer + 1]
            if n_half == parts - 1:
                term = dot_nn(m_ref[...], half_refs[peer][...])
            else:
                first = pl.ds(pl.multiple_of(place_ref[0] * depth, depth), depth)
                other = pl.ds(pl.multiple_of((1 - place_ref[0]) * depth, depth), depth)
                term = dot_nn(m_ref[:, first], half_refs[2 * peer][...])
                term = term + dot_nn(m_ref[:, other], half_refs[2 * peer + 1][...])
            attn = attn + term.astype(BF16).astype(F32)
        load.wait()
        middle = x_ref[...].astype(F32) + vector(SCALE_ATTN) * attn
        mid_ref[...] = middle
        stores = [copies.start(mid_ref, mid_hbm)]
        scaled, _ = norm_parts(middle)
        n2_ref[...] = (scaled * vector(GAIN2) + vector(SHIFT2)).astype(BF16)
        stores.append(copies.start(n2_ref, n2_hbm))

        def hidden_of(j):
            units_j = slice(j * step_units, (j + 1) * step_units)
            return dot_nn(n2_ref[...], fc1_ref[:, units_j]) + fb_ref[:, units_j]

        total = None
        hidden = hidden_of(0)
        for j in range(steps):
            units_j = slice(j * step_units, (j + 1) * step_units)
            later = hidden_of(j + 1) if j + 1 < steps else None
            activated, slope = gelu_parts(hidden)
            own = pl.ds(j * step_units, step_units)
            act_ref[:, units_j] = activated.astype(BF16)
            stores.append(copies.start(act_ref.at[:, own], act_hbm.at[:, own]))
            grad_hidden = ga_ref[:, units_j].astype(F32) * slope
            fbg_ref[:, units_j] = col_sum(grad_hidden)
            low = grad_hidden.astype(BF16)
            gh_ref[:, units_j] = low
            stores.append(copies.start(gh_ref.at[:, own], gh_hbm.at[:, own]))
            term = dot_nt(low, fc1_ref[:, units_j])
            total = term if total is None else total + term
            hidden = later
        low_terms = total.astype(BF16)
        terms_ref[...] = low_terms
        wide = low_terms.astype(F32)
        scaled, _ = norm_parts(mid_ref[...])
        vec_ref[0:1] = col_sum(wide * scaled)
        vec_ref[1:2] = col_sum(wide)
        for copy in stores:
            copy.wait()

    args = (*mixed, proj, *halves, place, tokens, grad_act, table, fc1, fc1_bias)
    return call(
        kernel,
        "feed_forward",
        [VMEM] * (parts + 1 + n_half) + [SMEM, ANY] + [VMEM] * 3 + [COPIED],
        [ANY] * 4 + [VMEM] * 3,
        [
            pltpu.HBM((rows, width), F32),
            pltpu.HBM((rows, width), BF16),
            pltpu.HBM((rows, units), BF16),
            pltpu.HBM((rows, units), BF16),
            shape((1, units), F32),
            shape((rows, width), BF16),
            shape((2, width), F32),
        ],
        args,
        after,
        scratch=[
            pltpu.VMEM((rows, width), F32),
            pltpu.VMEM((rows, width), BF16),
            pltpu.VMEM((rows, units), BF16),
            pltpu.VMEM((rows, units), BF16),
            pltpu.VMEM((rows, width), BF16),
            pltpu.SemaphoreType.DMA((3 + 2 * steps,)),
        ],
    )


def second_projection(activated, fc2, cotangent, lengths, after, bring):
    units, width = fc2.shape
    chunks = len(activated)
    rows = activated[0].shape[0]
    block = min(512, units)
    steps = units // block

    def kernel(begin, *refs):
        a_hbm, refs = refs[:chunks], refs[chunks:]
        w_hbm, c_hbm, lengths_ref, refs = refs[0], refs[1], refs[2], refs[3:]
        out_hbm, vec_ref, refs = refs[:chunks], refs[chunks], refs[chunks + 1 :]
        a_refs, (w_ref, c_ref, out_ref, sems) = refs[:chunks], refs[chunks:]
        stores = []
        copies = Copies(sems)
        loads = []
        for j in range(steps):
            own = pl.ds(j * block, block)
            loads.append([copies.start(w_hbm.at[own], w_ref.at[own])])
            loads[j].append(copies.start(a_hbm[0].at[:, own], a_refs[0].at[:, own]))
        late = [copies.start(hbm, ref) for hbm, ref in zip(a_hbm[1:], a_refs[1:])]
        late.append(copies.start(c_hbm, c_ref))
        begin()
        for chunk in range(chunks):
            total = None
            if chunk == 0:
                for j in range(steps):
                    for load in loads[j]:
                        load.wait()
                    place = slice(j * block, (j + 1) * block)
                    term = dot_nn(a_refs[0][:, place], w_ref[place])
                    total = term if total is None else total + term
                for load in late:
                    load.wait()
            else:
                total = dot_nn(a_refs[chunk][...], w_ref[...])
            terms = total.astype(BF16)
            place = slice(chunk * rows, (chunk + 1) * rows)
            out_ref[place] = terms
            stores.append(copies.start(out_ref.at[pl.ds(chunk * rows, rows)], out_hbm[chunk]))
            grad = c_ref[place].astype(F32) * valid_rows(lengths_ref, chunk * rows, rows)
            first, second = col_sum(grad * terms.astype(F32)), col_sum(grad)
            vec_ref[0:1] = first if chunk == 0 else vec_ref[0:1] + first
            vec_ref[1:2] = second if chunk == 0 else vec_ref[1:2] + second
        for copy in stores:
            copy.wait()

    return call(
        kernel,
        "second_projection",
        [ANY] * (chunks + 2) + [SMEM],
        [ANY] * chunks + [VMEM],
        [pltpu.HBM((rows, width), BF16)] * chunks + [shape((2, width), F32)],
        (*activated, fc2, cotangent, lengths),
        after,
        scratch=[pltpu.VMEM((rows, units), BF16)] * chunks
        + [
            pltpu.VMEM(fc2.shape, BF16),
            pltpu.VMEM(cotangent.shape, BF16),
            pltpu.VMEM(cotangent.shape, BF16),
            pltpu.SemaphoreType.DMA((2 * steps + 2 * chunks,)),
        ],
        bring=bring,
        late=True,
    )


def weight_grads(normed, grad_hidden, grad_mlp, activated, place, radix, shard, after):
    width = normed[0].shape[1]
    chunks = len(normed)
    rows = normed[0].shape[0]
    units = activated[0].shape[1]
    block = min(512, units)
    slots = 2
    steps = 2 * units // block
    half = steps // 2
    groups = width // (radix * shard)

    def kernel(*refs):
        n_hbm, h_hbm, a_hbm = refs[:chunks], refs[chunks : 2 * chunks], refs[2 * chunks : 3 * chunks]
        g_hbm, place_ref, refs = refs[3 * chunks], refs[3 * chunks + 1], refs[3 * chunks + 2 :]
        out_hbm, (n_ref, g_ref, right_ref, hold_ref, sems) = refs[:radix], refs[radix:]
        copies = Copies(sems)

        def rows_of(chunk):
            return pl.ds(chunk * rows, rows)

        loads = [[] for _ in range(steps)]
        for c in range(chunks):
            loads[0].append(copies.start(n_hbm[c], n_ref.at[rows_of(c)]))
        for step in range(steps):
            own = pl.ds(step % half * block, block)
            if step == half:
                loads[step].append(copies.start(g_hbm, g_ref))
            for c in range(chunks):
                source = (h_hbm if step < half else a_hbm)[c].at[:, own]
                loads[step].append(copies.start(source, right_ref.at[step, rows_of(c)]))
        flying = [[] for _ in range(slots)]
        for step in range(steps):
            for load in loads[step]:
                load.wait()
            total = dot_tn((n_ref if step < half else g_ref)[...], right_ref[step])
            slot = step % slots
            for copy in flying[slot]:
                copy.wait()
            hold_ref[slot] = total.astype(BF16).reshape(groups, radix, shard, block)
            columns = pl.ds(step * block, block)
            flying[slot] = [
                copies.start(
                    hold_ref.at[slot, :, lax.rem(place_ref[0] + part, radix)], out_hbm[part].at[:, :, columns]
                )
                for part in range(radix)
            ]
        for group in flying:
            for copy in group:
                copy.wait()

    return call(
        kernel,
        "weight_grads",
        [ANY] * (3 * chunks + 1) + [SMEM],
        [ANY] * radix,
        [pltpu.HBM((groups, shard, 2 * units), BF16)] * radix,
        (*normed, *grad_hidden, *activated, grad_mlp, place),
        after,
        scratch=[
            pltpu.VMEM((chunks * rows, width), BF16),
            pltpu.VMEM((chunks * rows, width), BF16),
            pltpu.VMEM((steps, chunks * rows, block), BF16),
            pltpu.VMEM((slots, groups, radix, shard, block), BF16),
            pltpu.SemaphoreType.DMA((chunks + 1 + (chunks + radix) * steps,)),
        ],
    )


def attention_grads(normed, grads, grad_attn, mixed, weight, sums, table, raw, share, place, radix, shard, after, ties, bring):
    count, width = normed.shape
    block = max(256, radix * shard)
    wide, local = grads.shape[1], mixed[0].shape[1]
    extra = 128
    total = wide + local + extra
    groups = block // (radix * shard)
    chunks = len(mixed)
    head = 64
    flat_raw = [part for group in raw for part in group]
    n_raw = len(flat_raw)
    units = raw[3][0].shape[1]

    def kernel(n_ref, g_ref, *refs):
        a_refs, m_refs, refs = refs[:chunks], refs[chunks : 2 * chunks], refs[2 * chunks :]
        raw_refs, refs = refs[:n_raw], refs[n_raw:]
        w_ref, s_ref, table_ref, place_ref = refs[:4]
        out_hbm, (hold_ref, v_ref, sems) = refs[4 : 4 + radix], refs[4 + radix :]
        copies = Copies(sems)
        stores = []

        def vector(row):
            return table_ref[row : row + 1]

        def both(group):
            first = sum(len(g) for g in raw[:group])
            return sum(ref[...] for ref in raw_refs[first : first + len(raw[group])])

        middle, norm2, result, hidden = both(0), both(1), both(2), both(3)
        v_ref[...] = jnp.zeros_like(v_ref)
        v_ref[0:1] = vector(GAIN1)
        v_ref[1:2] = vector(SHIFT1)
        v_ref[2:3] = middle[0:1] / vector(SCALE_ATTN) * share
        v_ref[3:4] = middle[1:2] * vector(SCALE_ATTN) * share
        v_ref[4:6] = norm2
        v_ref[6:7] = result[0:1] + result[1:2] * vector(FC2_BIAS) * share
        v_ref[7:8] = result[1:2] * vector(SCALE_MLP) * share

        def spread(flats, first):
            stack = [f[:, i * head : (i + 1) * head] for f in flats for i in range(f.shape[1] // head)]
            stack = jnp.concatenate(stack, axis=0)
            for group in range(head // shard):
                piece = stack[:, group * shard : (group + 1) * shard]
                repeat = max(1, 128 // shard)
                piece = jnp.concatenate([piece] * repeat, axis=1)
                piece = jnp.concatenate([piece] * (width // (repeat * shard)), axis=1)
                v_ref[first : first + stack.shape[0]] = piece
                first += stack.shape[0]
            return first

        spread([hidden], spread([s_ref[0:1], s_ref[2:3]], 8))
        lane = lax.broadcasted_iota(jnp.int32, (block, extra), 1)
        for i in range(width // block):
            blk = slice(i * block, (i + 1) * block)
            columns = v_ref[:, blk].T
            first = second = None
            product = dot_tn(n_ref[:, blk], g_ref[...])
            for part in range(3):
                piece = product[:, part * local : (part + 1) * local]
                w = w_ref[part, blk].astype(F32)
                one = jnp.sum(w * piece, axis=1, keepdims=True)
                two = jnp.sum(w * s_ref[part : part + 1], axis=1, keepdims=True)
                first = one if first is None else first + one
                second = two if second is None else second + two
            gain_grad = (first - columns[:, 1:2] * second) / columns[:, 0:1]
            small = jnp.where(lane == 0, gain_grad, jnp.where(lane == 1, second, columns))
            product_p = None
            for c in range(chunks):
                term = dot_tn(a_refs[c][:, blk], m_refs[c][...])
                product_p = term if product_p is None else product_p + term
            for copy in stores[(i - 2) * radix : (i - 1) * radix] if i >= 2 else ():
                copy.wait()
            hold_ref[i % 2, :, :, :, :wide] = product.astype(BF16).reshape(groups, radix, shard, wide)
            hold_ref[i % 2, :, :, :, wide : wide + local] = product_p.astype(BF16).reshape(groups, radix, shard, local)
            hold_ref[i % 2, :, :, :, wide + local :] = small.astype(BF16).reshape(groups, radix, shard, extra)
            for step in range(radix):
                source = hold_ref.at[i % 2, :, lax.rem(place_ref[0] + step, radix)]
                stores.append(copies.start(source, out_hbm[step].at[pl.ds(i * groups, groups)]))
        for copy in stores[-2 * radix :]:
            copy.wait()

    return call(
        kernel,
        "attention_grads",
        [VMEM, VMEM] + [VMEM] * (2 * chunks + n_raw) + [VMEM, VMEM, VMEM, SMEM],
        [ANY] * radix,
        [pltpu.HBM((width // (radix * shard), shard, total), BF16)] * radix,
        (normed, grads, *grad_attn, *mixed, *flat_raw, weight, sums, table, place),
        after,
        scratch=[
            pltpu.VMEM((2, groups, radix, shard, total), BF16),
            pltpu.VMEM((extra, width), F32),
            pltpu.SemaphoreType.DMA((width // block * radix,)),
        ],
        ties=ties,
        bring=bring,
    )


def add_far_stage(ways, after, name, ties=()):
    sizes = [(len(way[0]), *way[0][0].shape[:2], way[2], way[3]) for way in ways]
    n_out = sum(size[4] for size in sizes)
    n_ways = len(ways)
    kept = [way[0][0] for way in ways]
    arrived = []
    for way in ways:
        arrived += [array for array in way[0][1:] if not any(array is other for other in arrived)]

    def kernel(*refs):
        hbm, refs = refs[:n_ways], refs[n_ways:]
        arrived_refs, place_refs, refs = refs[: len(arrived)], refs[len(arrived) :][:n_ways], refs[len(arrived) + n_ways :]
        out_hbm, refs = refs[:n_out], refs[n_out:]
        in_refs, out_refs, sems = refs[:n_ways], refs[n_ways : 2 * n_ways], refs[2 * n_ways]
        copies = Copies(sems)
        loads = []
        for w, (_, left, _, columns, radix) in enumerate(sizes):
            _, first, _, _, _, below = ways[w]
            span = radix * below
            loads.append(
                [
                    copies.start(
                        hbm[w].at[pl.ds(high * span, span), :, pl.ds(first, columns)],
                        in_refs[w].at[pl.ds(high * span, span)],
                    )
                    for high in range(left // span)
                ]
            )
        stores = []
        given = 0
        for w, (_, left, _, columns, radix) in enumerate(sizes):
            arrays, first, _, _, _, below = ways[w]
            others = [
                arrived_refs[next(i for i, other in enumerate(arrived) if other is array)] for array in arrays[1:]
            ]
            for group in range(left // radix):
                high, low = divmod(group, below)
                if low == 0:
                    loads[w][high].wait()
                for step in range(radix):
                    digit = lax.rem(place_refs[w][0] + step, radix)
                    source = (high * radix + digit) * below + low
                    total = in_refs[w][source].astype(F32)
                    for ref in others:
                        total = total + ref[source, :, first : first + columns].astype(F32)
                    out_refs[w][step, group] = total.astype(BF16)
                    stores.append(copies.start(out_refs[w].at[step, group], out_hbm[given + step].at[group]))
            given += radix
        for copy in stores:
            copy.wait()

    count = sum(left // (radix * way[5]) + left for (_, left, _, _, radix), way in zip(sizes, ways))
    out, done = call(
        kernel,
        name,
        [ANY] * n_ways + [VMEM] * len(arrived) + [SMEM] * n_ways,
        [ANY] * n_out,
        [pltpu.HBM((left // radix, rows, columns), BF16) for _, left, rows, columns, radix in sizes for _ in range(radix)],
        (*kept, *arrived, *[way[4] for way in ways]),
        after,
        scratch=[pltpu.VMEM((left, rows, columns), BF16) for _, left, rows, columns, _ in sizes]
        + [pltpu.VMEM((radix, left // radix, rows, columns), BF16) for _, left, rows, columns, radix in sizes]
        + [pltpu.SemaphoreType.DMA((count,))],
        ties=ties,
    )
    split = []
    for size in sizes:
        split.append(out[: size[4]])
        out = out[size[4] :]
    return split, done


def total_of(refs):
    total = None
    for ref in refs:
        term = ref[0].astype(F32)
        total = term if total is None else total + term
    return total


def last_stage(parts, local, after):
    _, shard, columns = parts[0].shape

    def kernel(*refs):
        part_refs, (qkv_ref, proj_ref, small_ref) = refs[:-3], refs[-3:]
        total = total_of(part_refs)
        for part in range(3):
            qkv_ref[part] = total[:, part * local : (part + 1) * local]
        proj_ref[...] = total[:, 3 * local : 4 * local]
        small_ref[...] = total[:, 4 * local :].T

    return call(
        kernel,
        "last_stage",
        [COPIED] + [VMEM] * (len(parts) - 1),
        [COPIED, COPIED, VMEM],
        [shape((3, shard, local), F32), shape((shard, local), F32), shape((columns - 4 * local, shard), F32)],
        tuple(parts),
        after,
    )


def last_far_stage(firsts, seconds, after):
    _, shard, units = firsts[0].shape
    n_first = len(firsts)

    def kernel(*refs):
        first_ref, second_ref = refs[-2:]
        first_ref[...] = total_of(refs[:n_first])
        second_ref[...] = total_of(refs[n_first:-2])

    return call(
        kernel,
        "last_far_stage",
        [COPIED] + [VMEM] * (n_first - 1) + [COPIED] + [VMEM] * (len(seconds) - 1),
        [COPIED] * 2,
        [shape((shard, units), F32), shape((shard, units), F32)],
        (*firsts, *seconds),
        after,
    )


def wait_for(arrays, after):
    def kernel():
        pass

    _, done = call(kernel, "wait_for", [], [], [], (), after, ties=arrays)
    return done


def middle_back(chunk, rows, terms, middle, tokens, cotangent, lengths, table, proj, after, bring):
    width = middle.shape[1]
    local = proj.shape[0]
    parts = len(terms)

    def kernel(*refs):
        term_refs, refs = refs[:parts], refs[parts:]
        mid_ref, x_hbm, c_hbm, lengths_ref, table_ref, p_ref = refs[:6]
        gmid_hbm, low_ref, gmix_ref, vec_ref, gmid_ref, x_ref, c_ref, sems = refs[6:]
        copies = Copies(sems)
        own = pl.ds(chunk * rows, rows)
        loads = [copies.start(c_hbm.at[own], c_ref), copies.start(x_hbm.at[own], x_ref)]
        grad_norm = None
        for ref in term_refs:
            term = ref[...].astype(F32)
            grad_norm = term if grad_norm is None else grad_norm + term
        middle = mid_ref[...]
        scaled, inverse = norm_parts(middle)
        back = norm_back(grad_norm, scaled, inverse, table_ref[GAIN2 : GAIN2 + 1])
        loads[0].wait()
        grad = c_ref[...].astype(F32) * valid_rows(lengths_ref, chunk * rows, rows) + back
        gmid_ref[...] = grad
        store = copies.start(gmid_ref, gmid_hbm)
        low = (table_ref[SCALE_ATTN : SCALE_ATTN + 1] * grad).astype(BF16)
        low_ref[...] = low
        gmix_ref[...] = dot_nt(low, p_ref[...]).astype(BF16)
        loads[1].wait()
        vec_ref[0:1] = col_sum(grad * (middle - x_ref[...].astype(F32)))
        vec_ref[1:2] = col_sum(grad)
        store.wait()

    return call(
        kernel,
        f"middle_back_{chunk}",
        [VMEM] * parts + [VMEM, ANY, ANY, SMEM, VMEM, VMEM],
        [ANY] + [VMEM] * 3,
        [
            pltpu.HBM((rows, width), F32),
            shape((rows, width), BF16),
            shape((rows, local), BF16),
            shape((2, width), F32),
        ],
        (*terms, middle, tokens, cotangent, lengths, table, proj),
        after,
        scratch=[
            pltpu.VMEM((rows, width), F32),
            pltpu.VMEM((rows, width), BF16),
            pltpu.VMEM((rows, width), BF16),
            pltpu.SemaphoreType.DMA((3,)),
        ],
        bring=bring,
    )


def first_norm_terms(chunks, grads, weight, after):
    width, local = weight.shape[1:]
    rows = grads.shape[0] // chunks

    def kernel(g_ref, w_hbm, *refs):
        out_refs, (w_ref, sems) = refs[:chunks], refs[chunks:]
        copies = Copies(sems)
        loads = [copies.start(w_hbm.at[part], w_ref.at[part]) for part in range(3)]
        for chunk in range(chunks):
            place = slice(chunk * rows, (chunk + 1) * rows)
            total = None
            for part in range(3):
                if chunk == 0:
                    loads[part].wait()
                term = dot_nt(g_ref[place, part * local : (part + 1) * local], w_ref[part])
                total = term if total is None else total + term
            out_refs[chunk][...] = total.astype(BF16)

    return call(
        kernel,
        "first_norm_terms",
        [VMEM, ANY],
        [VMEM] * chunks,
        [shape((rows, width), BF16)] * chunks,
        (grads, weight),
        after,
        scratch=[pltpu.VMEM(weight.shape, BF16), pltpu.SemaphoreType.DMA((3,))],
    )


def to_rows(chunk, rows, compute, args, specs, dims, kept, after, name, sources=(), ties=()):
    extra = 0 if kept is None else 1
    blocks = 2
    block = rows // blocks
    n_args = len(args)
    n_source = len(sources)
    args, specs = args + tuple(array for array, _ in sources), specs + [ANY] * n_source

    def kernel(*refs):
        ins, refs = refs[:n_args], refs[n_args:]
        source_hbm, refs = refs[:n_source], refs[n_source:]
        out_hbm, hold_ref, sems = refs[extra : extra + 3]
        source_refs = refs[extra + 3 :]
        copies = Copies(sems)
        loads = [
            [
                copies.start(hbm.at[pl.ds(first + i * block, block)], ref.at[i])
                for hbm, ref, (_, first) in zip(source_hbm, source_refs, sources)
            ]
            for i in range(blocks)
        ]
        stores = []
        for i in range(blocks):
            for load in loads[i]:
                load.wait()
            hold_ref[i] = compute(i * block, block, *[ref[i] for ref in source_refs], *ins).astype(BF16)
            place = pl.ds(chunk * rows + i * block, block)
            stores.append(copies.start(hold_ref.at[i], out_hbm.at[place]))
        for copy in stores:
            copy.wait()

    alias = None
    if extra:
        alias = {len(args): 0}
        args = args + (kept,)
    scratch = [
        pltpu.VMEM((blocks, block, dims[1]), BF16),
        pltpu.SemaphoreType.DMA(((1 + n_source) * blocks,)),
        *[pltpu.VMEM((blocks, block, dims[1]), array.dtype) for array, _ in sources],
    ]
    return call(
        kernel,
        name,
        specs + [ANY] * extra,
        ANY,
        pltpu.HBM(dims, BF16),
        args,
        after,
        scratch=scratch,
        alias=alias,
        ties=ties,
    )


def token_grads(chunk, rows, terms, grad_middle, tokens, table, kept, after):
    parts = len(terms)

    def compute(first, block, x, grad, *refs):
        table_ref = refs[parts]
        place = slice(first, first + block)
        grad_norm = None
        for ref in refs[:parts]:
            term = ref[place].astype(F32)
            grad_norm = term if grad_norm is None else grad_norm + term
        scaled, inverse = norm_parts(x.astype(F32))
        return grad + norm_back(grad_norm, scaled, inverse, table_ref[GAIN1 : GAIN1 + 1])

    args = (*terms, table)
    specs = [VMEM] * (parts + 1)
    sources = ((tokens, chunk * rows), (grad_middle, 0))
    return to_rows(chunk, rows, compute, args, specs, tokens.shape, kept, after, f"token_grads_{chunk}", sources)


def layer_output(chunk, rows, terms, middle, lengths, table, dims, kept, after):
    parts = len(terms)

    def compute(first, block, mid, *refs):
        lengths_ref, table_ref = refs[parts:]
        mlp = table_ref[FC2_BIAS : FC2_BIAS + 1]
        for term in refs[:parts]:
            mlp = mlp + term.astype(F32)
        valid = valid_rows(lengths_ref, chunk * rows + first, block)
        return valid * (mid + table_ref[SCALE_MLP : SCALE_MLP + 1] * mlp)

    sources = ((middle, 0), *((term, 0) for term in terms))
    name = f"layer_output_{chunk}"
    return to_rows(chunk, rows, compute, (lengths, table), [SMEM, VMEM], dims, kept, after, name, sources)


def from_peers(array):
    size = lax.axis_size("tensor")
    return [
        lax.ppermute(array, "tensor", [(i, (i + step) % size) for i in range(size)])
        for step in range(1, size)
    ]


def other_of_pair(array):
    return lax.ppermute(array, "dp", [(i, i ^ 1) for i in range(lax.axis_size("dp"))])


def radices(size):
    found = []
    if size % 2 == 0:
        found.append(2)
        size //= 2
    while size > 1:
        step = 2 if size % 4 and size % 2 == 0 or size == 8 else next((r for r in (4, 3) if size % r == 0), size)
        found.append(step)
        size //= step
    return found


def small_digits(size, stride):
    digits = []
    while stride < size:
        left = size // stride
        radix = next(r for r in (2, 3, 5, left) if left % r == 0)
        digits.append((stride, radix))
        stride *= radix
    return digits


def exchange(parts, stride, radix):
    size = lax.axis_size("dp")
    arrived = []
    for step in range(1, radix):
        moves = []
        for i in range(size):
            at = (i // stride) % radix
            moves.append((i, i + ((at + step) % radix - at) * stride))
        arrived.append(lax.ppermute(parts[step], "dp", moves))
    return [parts[0]] + arrived


def body(
    tokens,
    lengths,
    norm1_gain,
    norm1_bias,
    qkv_weight,
    qv_bias,
    proj_weight,
    proj_bias,
    scale_attn,
    norm2_gain,
    norm2_bias,
    fc1_weight,
    fc1_bias,
    fc2_weight,
    fc2_bias,
    scale_mlp,
    cotangent,
):
    count, width = tokens.shape
    heads, head_size = qv_bias.shape[1:]
    local = heads * head_size
    units = fc1_weight.shape[1]
    tensor = lax.axis_size("tensor")
    dp = lax.axis_size("dp")
    chunks = 2
    rows = count // chunks
    scale = head_size**-0.5

    def flat(vector):
        return vector.reshape(1, -1)

    index = lax.axis_index("dp")
    steps = radices(dp)
    strides = [1]
    for step in steps:
        strides.append(strides[-1] * step)
    places = [((index // stride) % step).reshape(1) for stride, step in zip(strides, steps)]

    half_rows = local // 2
    paired = dp % 2 == 0 and half_rows % 128 == 0
    half_place = (index % 2).reshape(1)
    half = proj_weight
    if paired:
        half = lax.dynamic_slice_in_dim(proj_weight, half_place[0] * half_rows, half_rows, 0)
    halves = from_peers(half)
    vectors = (norm1_gain, norm1_bias, norm2_gain, norm2_bias, proj_bias, scale_attn, fc2_bias, scale_mlp)
    out, done = attend_forward(
        tokens,
        lengths,
        [flat(vector) for vector in vectors],
        qkv_weight,
        qv_bias,
        scale,
        rows,
        (cotangent, fc2_weight, proj_weight, fc1_weight),
    )
    queries, keys, values, normed1, *near, table, cotangent_near, fc2_near, proj_weight, fc1_weight = out[:12]
    first, rest = out[12:]
    mixed_parts = [[first] + from_peers(first)]
    rest, done = attend_rest(*near, rest, lengths, done)
    mixed_parts.append([rest] + from_peers(rest))
    mixed = [first, rest]
    out, done = hidden_cotangent(cotangent_near, lengths, table, fc2_near, halves, chunks, done)
    grad_mlp, grad_act, halves = out[0], out[1 : 1 + chunks], out[1 + chunks :]
    if paired:
        halves = [part for half in halves for part in (half, other_of_pair(half))]

    middle, normed2, activated, grad_hidden, norm2_parts = [], [], [], [], []
    raw = [[], [], [], []]
    for chunk in range(chunks):
        out, done = feed_forward(
            chunk,
            rows,
            mixed_parts[chunk],
            proj_weight,
            halves,
            half_place,
            tokens,
            grad_act[chunk],
            table,
            fc1_weight,
            flat(fc1_bias),
            done,
        )
        for group, part in zip((middle, normed2, activated, grad_hidden), out[:4]):
            group.append(part)
        raw[3].append(out[4])
        raw[1].append(out[6])
        norm2_parts.append([out[5]] + from_peers(out[5]))

    shard = width // dp
    fc_parts, done = weight_grads(
        normed2, grad_hidden, grad_mlp, activated, places[0], steps[0], shard, done
    )
    fc_parts = exchange(fc_parts, 1, steps[0])

    def near_stage(parts, stage, done):
        way = (parts, 0, parts[0].shape[2], steps[stage], places[stage], 1)
        (parts,), done = add_far_stage([way], done, f"add_stage_{stage}")
        return exchange(parts, strides[stage], steps[stage]), done

    out, done = second_projection(activated, fc2_weight, cotangent, lengths, done, middle)
    mlp_parts = [[terms] + from_peers(terms) for terms in out[:chunks]]
    raw[2].append(out[chunks])
    middle_near = out[chunks + 1 :]

    grad_middle, grad_attn, grad_mixed = [], [], []
    for chunk in range(chunks):
        out, done = middle_back(
            chunk,
            rows,
            norm2_parts[chunk],
            middle_near[chunk],
            tokens,
            cotangent,
            lengths,
            table,
            proj_weight,
            done,
            (queries, keys, values) if chunk == 0 else (),
        )
        if chunk == 0:
            queries, keys, values = out[4:]
        for group, part in zip((grad_middle, grad_attn, grad_mixed), out[:3]):
            group.append(part)
        raw[0].append(out[3])
    stages = len(steps)
    digits = small_digits(dp, strides[1])
    orders = [digits, digits[1:] + digits[:1]]

    def far_stage(at, firsts, seconds, start, done, ties=()):
        ways = []
        for arrays, first, order in ((firsts, 0, orders[0]), (seconds, start, orders[1])):
            stride, radix = order[at]
            below = 1
            for other_stride, other_radix in order[at:]:
                below *= other_radix if other_stride < stride else 1
            place = ((index // stride) % radix).reshape(1)
            ways.append((arrays, first, units, radix, place, below))
        split, done = add_far_stage(ways, done, f"add_far_stage_{at}", ties)
        return [exchange(parts, *order[at]) for parts, order in zip(split, orders)], done

    (firsts, seconds), done = far_stage(0, fc_parts, fc_parts, units, done)
    (grads, grad_sums, qkv_near, normed1), done = attend_backward(
        queries, keys, values, grad_mixed, lengths, scale, done, (qkv_weight, normed1)
    )
    parts, done = attention_grads(
        normed1,
        grads,
        grad_attn,
        mixed,
        qkv_near,
        grad_sums,
        table,
        raw,
        1.0 / tensor,
        places[0],
        steps[0],
        shard,
        done,
        mlp_parts[0][1:],
        (),
    )
    parts = exchange(parts, 1, steps[0])
    terms, done = first_norm_terms(chunks, grads, qkv_weight, done)
    norm1_parts = [[part] + from_peers(part) for part in terms]
    if len(digits) > 1:
        (firsts, seconds), done = far_stage(1, firsts, seconds, 0, done)
    done = wait_for([part for group in mlp_parts[1:] for part in group[1:]], done)
    if stages > 1:
        parts, done = near_stage(parts, 1, done)
    output = None
    for chunk in range(chunks):
        output, done = layer_output(
            chunk, rows, mlp_parts[chunk], middle[chunk], lengths, table, tokens.shape, output, done
        )
    for at in range(2, len(digits)):
        (firsts, seconds), done = far_stage(at, firsts, seconds, 0, done)
    grad_tokens = None
    for chunk in range(chunks - 1):
        grad_tokens, done = token_grads(
            chunk, rows, norm1_parts[chunk], grad_middle[chunk], tokens, table, grad_tokens, done
        )
    for stage in range(2, stages):
        parts, done = near_stage(parts, stage, done)
    (fc1_grad, fc2_grad), done = last_far_stage(firsts, seconds, done)
    grad_tokens, done = token_grads(
        chunks - 1, rows, norm1_parts[-1], grad_middle[-1], tokens, table, grad_tokens, done
    )
    (qkv_grad, proj_grad, small), done = last_stage(parts, local, done)

    vector_share = small[:8]
    for other in from_peers(vector_share):
        vector_share = vector_share + other
    own = shard // tensor
    vector_share = lax.dynamic_slice_in_dim(vector_share, lax.axis_index("tensor") * own, own, 1)

    def columns_of(first, heads_in):
        groups = head_size // shard
        pieces = [small[first + i * heads_in : first + (i + 1) * heads_in] for i in range(groups)]
        every = pieces[0] if groups == 1 else jnp.concatenate(pieces, axis=1)
        return lax.dynamic_slice_in_dim(every, index * (head_size // dp), head_size // dp, 1)

    bias_share = columns_of(8, 2 * heads).reshape(2, heads, -1)
    fc1_share = columns_of(8 + 2 * heads * (head_size // shard), units // head_size)

    return (
        output,
        grad_tokens,
        vector_share[0],
        vector_share[1],
        qkv_grad,
        bias_share,
        proj_grad.T,
        vector_share[3],
        vector_share[2],
        vector_share[4],
        vector_share[5],
        fc1_grad,
        fc1_share,
        fc2_grad.T,
        vector_share[7],
        vector_share[6],
    )


def solution(mesh):
    in_specs = (
        P("dp", None),
        P("dp", None),
        P(),
        P(),
        P(None, None, "tensor"),
        P(None, "tensor", None),
        P("tensor", None),
        P(),
        P(),
        P(),
        P(),
        P(None, "tensor"),
        P("tensor"),
        P("tensor", None),
        P(),
        P(),
        P("dp", None),
    )
    out_specs = (
        P("dp", None),
        P("dp", None),
        P(("dp", "tensor")),
        P(("dp", "tensor")),
        P(None, "dp", "tensor"),
        P(None, "tensor", "dp"),
        P("tensor", "dp"),
        P(("dp", "tensor")),
        P(("dp", "tensor")),
        P(("dp", "tensor")),
        P(("dp", "tensor")),
        P("dp", "tensor"),
        P("tensor", "dp"),
        P("tensor", "dp"),
        P(("dp", "tensor")),
        P(("dp", "tensor")),
    )
    return jax.shard_map(body, mesh=mesh, in_specs=in_specs, out_specs=out_specs, check_vma=False)
```

```python
from functools import partial

import jax
import jax.numpy as jnp
from jax import lax
from jax.experimental import pallas as pl
from jax.experimental.pallas import tpu as pltpu
from jax.sharding import PartitionSpec as P

EPS = 1e-06
NEGATIVE = -1e30
GLOBAL_LEN = 197
LOCAL_LEN = 37
GROUP = GLOBAL_LEN // LOCAL_LEN
WINDOW = 224
BF16 = jnp.bfloat16
F32 = jnp.float32
MIB = 1 << 20
VMEM_MIB = 16
SPARE = 6
LIMITS = {
    "attend_forward": 14,
    "attend_rest": 6,
    "hidden_cotangent": 6,
    "feed_forward": 15,
    "weight_grads": 17,
    "second_projection": 18,
    "middle_back": 13,
    "attend_backward": 11,
    "attention_grads": 14,
    "layer_output": 13,
    "first_norm_terms": 9,
    "add_stage": 8,
    "token_grads": 9,
    "last_stage": 8,
    "last_far_stage": 8,
    "wait_for": 1,
    "add_far_stage": 16,
}
COST = 2300000000
COSTS = {"middle_back_1": 46000000000, "wait_for": 16100000000, "token_grads_0": 13800000000}


def dot_nn(a, b):
    return lax.dot_general(a, b, (((1,), (0,)), ((), ())), preferred_element_type=F32)


def dot_nt(a, b):
    return lax.dot_general(a, b, (((1,), (1,)), ((), ())), preferred_element_type=F32)


def dot_tn(a, b):
    return lax.dot_general(a, b, (((0,), (0,)), ((), ())), preferred_element_type=F32)


def norm_parts(values):
    average = jnp.mean(values, axis=-1, keepdims=True)
    centered = values - average
    inverse = lax.rsqrt(jnp.mean(centered * centered, axis=-1, keepdims=True) + EPS)
    return centered * inverse, inverse


def norm_back(grad_norm, scaled, inverse, gain):
    grad_hat = grad_norm * gain
    first_mean = jnp.mean(grad_hat, axis=-1, keepdims=True)
    second_mean = jnp.mean(grad_hat * scaled, axis=-1, keepdims=True)
    return inverse * (grad_hat - first_mean - scaled * second_mean)


def col_sum(values):
    return jnp.sum(values, axis=0, keepdims=True)


def call(kernel, name, in_specs, out_specs, out_shape, args, after=None, scratch=(), vmem=VMEM_MIB, alias=None, bring=(), late=False, ties=()):
    single = not isinstance(out_shape, list)
    if single:
        out_specs, out_shape = [out_specs], [out_shape]
    n_in, n_out, n_bring = len(args), len(out_shape), len(bring)
    after = list(ties) if after is None else [after, *ties]
    n_after = len(after)
    args = [
        pltpu.with_memory_space_constraint(arg, pltpu.VMEM if spec is VMEM else pltpu.HBM)
        if spec is VMEM or spec is ANY
        else arg
        for arg, spec in zip(args, in_specs)
    ]
    args += [pltpu.with_memory_space_constraint(arg, pltpu.HBM) for arg in bring]
    out_shape = [
        pltpu.VMEM(o.shape, o.dtype) if spec is VMEM else o for o, spec in zip(out_shape, out_specs)
    ]

    def ordered(*refs):
        ins, refs = refs[:n_in], refs[n_in:]
        bring_hbm, refs = refs[:n_bring], refs[n_bring + n_after :]
        outs, refs = refs[:n_out], refs[n_out:]
        bring_refs, done, refs = refs[:n_bring], refs[n_bring], refs[n_bring + 1 :]
        done[...] = jnp.zeros_like(done)
        loads = []
        if n_bring:
            refs, sems = refs[:-1], refs[-1]

        def begin():
            for i in range(n_bring):
                loads.append(pltpu.make_async_copy(bring_hbm[i], bring_refs[i], sems.at[i]))
                loads[-1].start()

        if late:
            kernel(begin, *ins, *outs, *refs)
        else:
            begin()
            kernel(*ins, *outs, *refs)
        for load in loads:
            load.wait()

    out = pl.pallas_call(
        ordered,
        in_specs=list(in_specs) + [ANY] * (n_bring + n_after),
        out_specs=list(out_specs) + [VMEM] * (n_bring + 1),
        out_shape=list(out_shape) + [pltpu.VMEM(a.shape, a.dtype) for a in bring] + [pltpu.VMEM((8, 128), F32)],
        scratch_shapes=list(scratch) + ([pltpu.SemaphoreType.DMA((n_bring,))] if n_bring else []),
        input_output_aliases=alias or {},
        compiler_params=pltpu.CompilerParams(vmem_limit_bytes=(LIMITS.get(name.rstrip("_0123456789"), vmem) + SPARE) * MIB),
        cost_estimate=pl.CostEstimate(flops=COSTS.get(name, COST), bytes_accessed=COST, transcendentals=0),
        name=name,
    )(*args, *after)
    return (out[0] if single and not n_bring else out[:-1]), out[-1]


class Copies:
    def __init__(self, sems):
        self.sems = sems
        self.used = 0

    def start(self, source, target):
        copy = pltpu.make_async_copy(source, target, self.sems.at[self.used])
        self.used += 1
        copy.start()
        return copy


def shape(dims, dtype):
    return jax.ShapeDtypeStruct(dims, dtype)


SMEM = pl.BlockSpec(memory_space=pltpu.SMEM)
VMEM = pl.BlockSpec(memory_space=pltpu.VMEM)
ANY = pl.BlockSpec(memory_space=pl.ANY)
COPIED = pl.BlockSpec(memory_space=pltpu.VMEM)

GAIN1, SHIFT1, GAIN2, SHIFT2, PROJ_BIAS, SCALE_ATTN, FC2_BIAS, SCALE_MLP = range(8)


def row_total(lengths_ref):
    total = jnp.int32(0)
    for slot in range(lengths_ref.shape[1]):
        total = total + lengths_ref[0, slot]
    return total


def valid_rows(lengths_ref, first, rows):
    places = lax.broadcasted_iota(jnp.int32, (rows, 1), 0) + first
    return (places < row_total(lengths_ref)).astype(F32)


def item_counts(lengths_ref):
    globals_ = jnp.int32(0)
    locals_ = jnp.int32(0)
    for slot in range(lengths_ref.shape[1]):
        value = lengths_ref[0, slot]
        globals_ = globals_ + jnp.where(value == GLOBAL_LEN, 1, 0)
        locals_ = locals_ + jnp.where(value == LOCAL_LEN, 1, 0)
    return globals_, locals_


def item_place(item, globals_, locals_, count):
    is_global = item < globals_
    group = item - globals_
    start = jnp.where(
        is_global, item * GLOBAL_LEN, globals_ * GLOBAL_LEN + group * (GROUP * LOCAL_LEN)
    )
    length = jnp.where(
        is_global, GLOBAL_LEN, jnp.minimum(locals_ - group * GROUP, GROUP) * LOCAL_LEN
    )
    crop = jnp.where(is_global, GLOBAL_LEN, LOCAL_LEN)
    first = jnp.minimum((start // 16) * 16, count - WINDOW)
    return pl.multiple_of(first, 16), start - first, length, crop


def crop_of(places, offset, length, crop, outside):
    inside = (places >= offset) & (places < offset + length)
    index = places - offset
    label = jnp.zeros_like(places)
    for step in range(1, GROUP):
        label = label + jnp.where(index >= step * crop, 1, 0)
    return jnp.where(inside, label, outside)


def item_total(globals_, locals_):
    return globals_ + (locals_ + GROUP - 1) // GROUP


def attend_items(first_item, last_item, q_ref, k_ref, v_ref, out_ref, skipped, lengths_ref):
    count, local = q_ref.shape
    pair = 128
    pairs = local // pair
    globals_, locals_ = item_counts(lengths_ref)
    low_half = lax.broadcasted_iota(jnp.int32, (1, pair), 1) < pair // 2

    def step(item, carry):
        first, offset, length, crop = item_place(item, globals_, locals_, count)
        window = pl.ds(first, WINDOW)
        placed = pl.ds(pl.multiple_of(first - skipped, 16), WINDOW)
        by_key = lax.broadcasted_iota(jnp.int32, (WINDOW, 1), 0)
        by_query = lax.broadcasted_iota(jnp.int32, (1, WINDOW), 1)
        query_crop = crop_of(by_query, offset, length, crop, -2)
        key_crop = crop_of(by_key, offset, length, crop, -1)
        mask = jnp.where(query_crop == key_crop, 0.0, NEGATIVE)
        inside = key_crop >= 0

        def products(index):
            columns = slice(index * pair, (index + 1) * pair)
            return dot_nt(heads_apart(k_ref[window, columns], low_half), q_ref[window, columns])

        now = products(0)
        for index in range(pairs):
            columns = slice(index * pair, (index + 1) * pair)
            later = products(index + 1) if index + 1 < pairs else None
            scores = now.reshape(2, WINDOW, WINDOW) + mask
            weights = jnp.exp(scores - jnp.max(scores, axis=1, keepdims=True))
            total = jnp.sum(weights, axis=1, keepdims=True)
            low = (weights * (1.0 / total)).astype(BF16).reshape(2 * WINDOW, WINDOW)
            out = dot_tn(low, heads_apart(v_ref[window, columns], low_half))
            now = later
            kept = out_ref[placed, columns].astype(F32)
            out_ref[placed, columns] = jnp.where(inside, out, kept).astype(BF16)
        return carry

    lax.fori_loop(first_item, jnp.minimum(last_item, item_total(globals_, locals_)), step, 0)


def attend_forward(tokens, lengths, vectors, weight, qv_bias, scale, rows, later):
    count, width = tokens.shape
    local = weight.shape[2]
    head = 64
    block = 256
    blocks = count // block
    n_vec, n_later = len(vectors), len(later)

    def kernel(x_hbm, w_hbm, *refs):
        later_hbm, refs = refs[:n_later], refs[n_later:]
        vec_hbm, refs = refs[:n_vec], refs[n_vec:]
        qv_hbm, lengths_ref, refs = refs[0], refs[1], refs[2:]
        q_hbm, k_hbm, v_hbm, n_hbm, q_ref, k_ref, v_ref, table_ref, refs = *refs[:8], refs[8:]
        later_refs, (first_ref, rest_ref), refs = refs[:n_later], refs[n_later : n_later + 2], refs[n_later + 2 :]
        vec_refs, refs = refs[:n_vec], refs[n_vec:]
        heads_ref, x_ref, w_ref, n_ref, out_ref, sems = refs
        copies = Copies(sems)

        def part(ref, index):
            return ref.at[pl.ds(index * block, block)]

        loads = [copies.start(part(x_hbm, 0), part(x_ref, 0))]
        small_loads = [copies.start(hbm, ref) for hbm, ref in zip(vec_hbm[:2], vec_refs[:2])]
        weight_loads = [copies.start(w_hbm.at[0], w_ref.at[0])]
        small_loads.append(copies.start(qv_hbm, heads_ref))
        weight_loads += [copies.start(w_hbm.at[i], w_ref.at[i]) for i in range(1, 3)]
        loads += [copies.start(part(x_hbm, i), part(x_ref, i)) for i in range(1, blocks)]
        table_loads = [copies.start(hbm, ref) for hbm, ref in zip(vec_hbm[2:], vec_refs[2:])]
        later_loads = [copies.start(hbm, ref) for hbm, ref in zip(later_hbm, later_refs)]

        def scaled_of(i):
            loads[i].wait()
            return norm_parts(x_ref[i * block : (i + 1) * block].astype(F32))[0]

        def normed_of(i):
            return (scaled_of(i) * vec_refs[GAIN1][...] + vec_refs[SHIFT1][...]).astype(BF16)

        scaled = scaled_of(0)
        for load in small_loads:
            load.wait()
        qv = [
            jnp.concatenate([heads_ref[i, h : h + 1] for h in range(local // head)], axis=1)
            for i in range(2)
        ]
        now = (scaled * vec_refs[GAIN1][...] + vec_refs[SHIFT1][...]).astype(BF16)
        for i in range(blocks):
            rows_i = slice(i * block, (i + 1) * block)
            after = normed_of(i + 1) if i + 1 < blocks else None
            n_ref[rows_i] = now
            if i == 0:
                weight_loads[0].wait()
            queries = (dot_nn(now, w_ref[0]) + qv[0]).astype(BF16)
            q_ref[rows_i] = queries * BF16(scale)
            if i == 0:
                weight_loads[1].wait()
            k_ref[rows_i] = dot_nn(now, w_ref[1]).astype(BF16)
            if i == 0:
                weight_loads[2].wait()
            v_ref[rows_i] = (dot_nn(now, w_ref[2]) + qv[1]).astype(BF16)
            now = after
        stores = [
            copies.start(ref, hbm)
            for ref, hbm in ((q_ref, q_hbm), (k_ref, k_hbm), (v_ref, v_hbm), (n_ref, n_hbm))
        ]
        average = col_sum(v_ref[...].astype(F32)) * (1.0 / count)
        out_ref[...] = jnp.broadcast_to(average, (count, local)).astype(BF16)
        attend_items(0, first_items(rows), q_ref, k_ref, v_ref, out_ref, 0, lengths_ref)
        first_ref[...] = out_ref[:rows]
        rest_ref[...] = out_ref[rows:]
        for load in table_loads:
            load.wait()
        for i in range(n_vec):
            table_ref[i : i + 1] = vec_refs[i][...]
        for copy in later_loads + stores:
            copy.wait()

    part = pltpu.HBM((count, local), BF16)
    near = shape((count, local), BF16)
    outs = [part, part, part, pltpu.HBM((count, width), BF16), near, near, near, shape((n_vec, width), F32)]
    outs += [shape(a.shape, a.dtype) for a in later] + [shape((rows, local), BF16), shape((count - rows, local), BF16)]
    args = (tokens, weight, *later, *vectors, qv_bias, lengths)
    return call(
        kernel,
        "attend_forward",
        [ANY] * (len(args) - 1) + [SMEM],
        [ANY] * 4 + [VMEM] * (len(outs) - 4),
        outs,
        args,
        scratch=[pltpu.VMEM((1, width), F32)] * n_vec
        + [
            pltpu.VMEM(qv_bias.shape, F32),
            pltpu.VMEM((count, width), BF16),
            pltpu.VMEM(weight.shape, BF16),
            pltpu.VMEM((count, width), BF16),
            pltpu.VMEM((count, local), BF16),
            pltpu.SemaphoreType.DMA((blocks + 8 + n_later + n_vec,)),
        ],
    )


def first_items(rows):
    return -(-rows // (GROUP * LOCAL_LEN))


def attend_rest(queries, keys, values, rest, lengths, after):
    rows = queries.shape[0] - rest.shape[0]

    def kernel(q_ref, k_ref, v_ref, rest_ref, lengths_ref, out_ref):
        out_ref[...] = rest_ref[...]
        attend_items(first_items(rows), 1 << 20, q_ref, k_ref, v_ref, out_ref, rows, lengths_ref)

    return call(
        kernel,
        "attend_rest",
        [VMEM] * 4 + [SMEM],
        VMEM,
        shape(rest.shape, BF16),
        (queries, keys, values, rest, lengths),
        after,
    )


def heads_apart(both, low_half):
    return jnp.concatenate([jnp.where(low_half, both, BF16(0)), jnp.where(low_half, BF16(0), both)], axis=0)


def heads_together(apart, low_half):
    return jnp.where(low_half, apart[:WINDOW], apart[WINDOW:])


def attend_backward(queries, keys, values, grad_mixed, lengths, scale, after, bring):
    count, local = queries.shape
    head = 64
    pair = 2 * head

    chunks = len(grad_mixed)
    rows = count // chunks

    def kernel(q_ref, k_ref, v_ref, *refs):
        chunk_refs, refs = refs[:chunks], refs[chunks:]
        lengths_ref, out_ref, bias_ref, acc_ref, g_ref = refs
        for chunk in range(chunks):
            g_ref[chunk * rows : (chunk + 1) * rows] = chunk_refs[chunk][...]
        globals_, locals_ = item_counts(lengths_ref)
        acc_ref[...] = jnp.zeros_like(acc_ref)
        low_half = lax.broadcasted_iota(jnp.int32, (1, pair), 1) < head

        def step(item, carry):
            first, offset, length, crop = item_place(item, globals_, locals_, count)
            window = pl.ds(first, WINDOW)
            by_key = lax.broadcasted_iota(jnp.int32, (WINDOW, 1), 0)
            by_query = lax.broadcasted_iota(jnp.int32, (1, WINDOW), 1)
            query_crop = crop_of(by_query, offset, length, crop, -2)
            key_crop = crop_of(by_key, offset, length, crop, -1)
            mask = jnp.where(query_crop == key_crop, 0.0, NEGATIVE)
            inside = key_crop >= 0
            def products(index):
                columns = slice(index * pair, (index + 1) * pair)
                q2 = q_ref[window, columns]
                g2 = jnp.where(inside, g_ref[window, columns], BF16(0))
                both_k = heads_apart(k_ref[window, columns], low_half)
                both_v = heads_apart(v_ref[window, columns], low_half)
                return q2, g2, both_k, dot_nt(both_k, q2), dot_nt(both_v, g2)

            pairs = local // pair
            now = products(0)
            for index in range(pairs):
                columns = slice(index * pair, (index + 1) * pair)
                later = products(index + 1) if index + 1 < pairs else None
                q2, g2, both_k, scores, grad_probability = now
                now = later
                scores = scores.reshape(2, WINDOW, WINDOW) + mask
                weights = jnp.exp(scores - jnp.max(scores, axis=1, keepdims=True))
                total = jnp.sum(weights, axis=1, keepdims=True)
                probability = weights * (1.0 / total)
                grad_probability = grad_probability.reshape(2, WINDOW, WINDOW)
                delta = jnp.sum(probability * grad_probability, axis=1, keepdims=True)
                grad_scores = (probability * (grad_probability - delta)).astype(BF16)
                grad_scores = grad_scores.reshape(2 * WINDOW, WINDOW)
                low = probability.astype(BF16).reshape(2 * WINDOW, WINDOW)
                grad_v = heads_together(dot_nn(low, g2), low_half)
                grad_k = heads_together(dot_nn(grad_scores, q2), low_half)
                grad_q = dot_tn(grad_scores, both_k)
                acc_ref[0, window, columns] += grad_q * scale
                acc_ref[1, window, columns] += grad_k
                acc_ref[2, window, columns] += grad_v
            return carry

        lax.fori_loop(0, item_total(globals_, locals_), step, 0)
        for part in range(3):
            out_ref[:, part * local : (part + 1) * local] = acc_ref[part].astype(BF16)
            bias_ref[part : part + 1] = col_sum(acc_ref[part])

    return call(
        kernel,
        "attend_backward",
        [VMEM, VMEM, VMEM] + [VMEM] * chunks + [SMEM],
        [VMEM, VMEM],
        [shape((count, 3 * local), BF16), shape((3, local), F32)],
        (queries, keys, values, *grad_mixed, lengths),
        after,
        scratch=[pltpu.VMEM((3, count, local), F32), pltpu.VMEM((count, local), BF16)],
        bring=bring,
    )


def gelu_parts(value):
    size = jnp.abs(value)
    bell = jnp.exp(value * value * -0.5)
    t = 1.0 / (1.0 + size * (0.3275911 * 0.7071067811865476))
    poly = t * (
        0.254829592
        + t * (-0.284496736 + t * (1.421413741 + t * (-1.453152027 + t * 1.061405429)))
    )
    tail = 0.5 * poly * bell
    share = jnp.where(value >= 0, 1.0 - tail, tail)
    return value * share, share + value * (bell * 0.3989422804014327)


def hidden_cotangent(cotangent, lengths, table, fc2, halves, chunks, after):
    count, width = cotangent.shape
    units = fc2.shape[0]
    rows = count // chunks
    n_half = len(halves)

    def kernel(c_ref, w_ref, table_ref, lengths_ref, *refs):
        half_refs, refs = refs[:n_half], refs[n_half:]
        gm_hbm, ga_refs, on_refs = refs[0], refs[1 : 1 + chunks], refs[1 + chunks : 1 + chunks + n_half]
        gm_ref, sems = refs[1 + chunks + n_half :]
        copies = Copies(sems)
        stores = []
        for half_ref, on_ref in zip(half_refs, on_refs):
            on_ref[...] = half_ref[...]
        for chunk in range(chunks):
            place = chunk * rows
            grad = c_ref[place : place + rows].astype(F32) * valid_rows(lengths_ref, place, rows)
            low = (grad * table_ref[SCALE_MLP : SCALE_MLP + 1]).astype(BF16)
            gm_ref[place : place + rows] = low
            own = pl.ds(place, rows)
            stores.append(copies.start(gm_ref.at[own], gm_hbm.at[own]))
            ga_refs[chunk][...] = dot_nt(low, w_ref[...]).astype(BF16)
        for copy in stores:
            copy.wait()

    return call(
        kernel,
        "hidden_cotangent",
        [VMEM, VMEM, VMEM, SMEM] + [VMEM] * n_half,
        [ANY] + [VMEM] * (chunks + n_half),
        [pltpu.HBM((count, width), BF16)]
        + [shape((rows, units), BF16)] * chunks
        + [shape(half.shape, BF16) for half in halves],
        (cotangent, fc2, table, lengths, *halves),
        after,
        scratch=[pltpu.VMEM((count, width), BF16), pltpu.SemaphoreType.DMA((chunks,))],
    )


def feed_forward(chunk, rows, mixed, proj, halves, place, tokens, grad_act, table, fc1, fc1_bias, after):
    width = tokens.shape[1]
    units = fc1.shape[1]
    step_units = min(512, units)
    steps = units // step_units
    parts = len(mixed)
    n_half = len(halves)
    depth = proj.shape[0] // 2

    def kernel(*refs):
        mixed_refs, p_ref, half_refs, refs = refs[:parts], refs[parts], refs[parts + 1 : parts + 1 + n_half], refs[parts + 1 + n_half :]
        place_ref, x_hbm, ga_ref, table_ref, fc1_ref, fb_ref = refs[:6]
        mid_hbm, n2_hbm, act_hbm, gh_hbm, fbg_ref, terms_ref, vec_ref, refs = *refs[6:13], refs[13:]
        mid_ref, n2_ref, act_ref, gh_ref, x_ref, sems = refs
        copies = Copies(sems)
        load = copies.start(x_hbm.at[pl.ds(chunk * rows, rows)], x_ref)

        def vector(row):
            return table_ref[row : row + 1]

        attn = vector(PROJ_BIAS) + dot_nn(mixed_refs[0][...], p_ref[...]).astype(BF16).astype(F32)
        for peer in range(parts - 1):
            m_ref = mixed_refs[peer + 1]
            if n_half == parts - 1:
                term = dot_nn(m_ref[...], half_refs[peer][...])
            else:
                first = pl.ds(pl.multiple_of(place_ref[0] * depth, depth), depth)
                other = pl.ds(pl.multiple_of((1 - place_ref[0]) * depth, depth), depth)
                term = dot_nn(m_ref[:, first], half_refs[2 * peer][...])
                term = term + dot_nn(m_ref[:, other], half_refs[2 * peer + 1][...])
            attn = attn + term.astype(BF16).astype(F32)
        load.wait()
        middle = x_ref[...].astype(F32) + vector(SCALE_ATTN) * attn
        mid_ref[...] = middle
        stores = [copies.start(mid_ref, mid_hbm)]
        scaled, _ = norm_parts(middle)
        n2_ref[...] = (scaled * vector(GAIN2) + vector(SHIFT2)).astype(BF16)
        stores.append(copies.start(n2_ref, n2_hbm))

        def hidden_of(j):
            units_j = slice(j * step_units, (j + 1) * step_units)
            return dot_nn(n2_ref[...], fc1_ref[:, units_j]) + fb_ref[:, units_j]

        total = None
        hidden = hidden_of(0)
        for j in range(steps):
            units_j = slice(j * step_units, (j + 1) * step_units)
            later = hidden_of(j + 1) if j + 1 < steps else None
            activated, slope = gelu_parts(hidden)
            own = pl.ds(j * step_units, step_units)
            act_ref[:, units_j] = activated.astype(BF16)
            stores.append(copies.start(act_ref.at[:, own], act_hbm.at[:, own]))
            grad_hidden = ga_ref[:, units_j].astype(F32) * slope
            fbg_ref[:, units_j] = col_sum(grad_hidden)
            low = grad_hidden.astype(BF16)
            gh_ref[:, units_j] = low
            stores.append(copies.start(gh_ref.at[:, own], gh_hbm.at[:, own]))
            term = dot_nt(low, fc1_ref[:, units_j])
            total = term if total is None else total + term
            hidden = later
        low_terms = total.astype(BF16)
        terms_ref[...] = low_terms
        wide = low_terms.astype(F32)
        scaled, _ = norm_parts(mid_ref[...])
        vec_ref[0:1] = col_sum(wide * scaled)
        vec_ref[1:2] = col_sum(wide)
        for copy in stores:
            copy.wait()

    args = (*mixed, proj, *halves, place, tokens, grad_act, table, fc1, fc1_bias)
    return call(
        kernel,
        "feed_forward",
        [VMEM] * (parts + 1 + n_half) + [SMEM, ANY] + [VMEM] * 3 + [COPIED],
        [ANY] * 4 + [VMEM] * 3,
        [
            pltpu.HBM((rows, width), F32),
            pltpu.HBM((rows, width), BF16),
            pltpu.HBM((rows, units), BF16),
            pltpu.HBM((rows, units), BF16),
            shape((1, units), F32),
            shape((rows, width), BF16),
            shape((2, width), F32),
        ],
        args,
        after,
        scratch=[
            pltpu.VMEM((rows, width), F32),
            pltpu.VMEM((rows, width), BF16),
            pltpu.VMEM((rows, units), BF16),
            pltpu.VMEM((rows, units), BF16),
            pltpu.VMEM((rows, width), BF16),
            pltpu.SemaphoreType.DMA((3 + 2 * steps,)),
        ],
    )


def second_projection(activated, fc2, cotangent, lengths, after, bring):
    units, width = fc2.shape
    chunks = len(activated)
    rows = activated[0].shape[0]
    block = min(512, units)
    steps = units // block

    def kernel(begin, *refs):
        a_hbm, refs = refs[:chunks], refs[chunks:]
        w_hbm, c_hbm, lengths_ref, refs = refs[0], refs[1], refs[2], refs[3:]
        out_hbm, vec_ref, refs = refs[:chunks], refs[chunks], refs[chunks + 1 :]
        a_refs, (w_ref, c_ref, out_ref, sems) = refs[:chunks], refs[chunks:]
        stores = []
        copies = Copies(sems)
        loads = []
        for j in range(steps):
            own = pl.ds(j * block, block)
            loads.append([copies.start(w_hbm.at[own], w_ref.at[own])])
            loads[j].append(copies.start(a_hbm[0].at[:, own], a_refs[0].at[:, own]))
        late = [copies.start(hbm, ref) for hbm, ref in zip(a_hbm[1:], a_refs[1:])]
        late.append(copies.start(c_hbm, c_ref))
        begin()
        for chunk in range(chunks):
            total = None
            if chunk == 0:
                for j in range(steps):
                    for load in loads[j]:
                        load.wait()
                    place = slice(j * block, (j + 1) * block)
                    term = dot_nn(a_refs[0][:, place], w_ref[place])
                    total = term if total is None else total + term
                for load in late:
                    load.wait()
            else:
                total = dot_nn(a_refs[chunk][...], w_ref[...])
            terms = total.astype(BF16)
            place = slice(chunk * rows, (chunk + 1) * rows)
            out_ref[place] = terms
            stores.append(copies.start(out_ref.at[pl.ds(chunk * rows, rows)], out_hbm[chunk]))
            grad = c_ref[place].astype(F32) * valid_rows(lengths_ref, chunk * rows, rows)
            first, second = col_sum(grad * terms.astype(F32)), col_sum(grad)
            vec_ref[0:1] = first if chunk == 0 else vec_ref[0:1] + first
            vec_ref[1:2] = second if chunk == 0 else vec_ref[1:2] + second
        for copy in stores:
            copy.wait()

    return call(
        kernel,
        "second_projection",
        [ANY] * (chunks + 2) + [SMEM],
        [ANY] * chunks + [VMEM],
        [pltpu.HBM((rows, width), BF16)] * chunks + [shape((2, width), F32)],
        (*activated, fc2, cotangent, lengths),
        after,
        scratch=[pltpu.VMEM((rows, units), BF16)] * chunks
        + [
            pltpu.VMEM(fc2.shape, BF16),
            pltpu.VMEM(cotangent.shape, BF16),
            pltpu.VMEM(cotangent.shape, BF16),
            pltpu.SemaphoreType.DMA((2 * steps + 2 * chunks,)),
        ],
        bring=bring,
        late=True,
    )


def weight_grads(normed, grad_hidden, grad_mlp, activated, place, radix, shard, after):
    width = normed[0].shape[1]
    chunks = len(normed)
    rows = normed[0].shape[0]
    units = activated[0].shape[1]
    block = min(512, units)
    slots = 2
    steps = 2 * units // block
    half = steps // 2
    groups = width // (radix * shard)

    def kernel(*refs):
        n_hbm, h_hbm, a_hbm = refs[:chunks], refs[chunks : 2 * chunks], refs[2 * chunks : 3 * chunks]
        g_hbm, place_ref, refs = refs[3 * chunks], refs[3 * chunks + 1], refs[3 * chunks + 2 :]
        out_hbm, (n_ref, g_ref, right_ref, hold_ref, sems) = refs[:radix], refs[radix:]
        copies = Copies(sems)

        def rows_of(chunk):
            return pl.ds(chunk * rows, rows)

        loads = [[] for _ in range(steps)]
        for c in range(chunks):
            loads[0].append(copies.start(n_hbm[c], n_ref.at[rows_of(c)]))
        for step in range(steps):
            own = pl.ds(step % half * block, block)
            if step == half:
                loads[step].append(copies.start(g_hbm, g_ref))
            for c in range(chunks):
                source = (h_hbm if step < half else a_hbm)[c].at[:, own]
                loads[step].append(copies.start(source, right_ref.at[step, rows_of(c)]))
        flying = [[] for _ in range(slots)]
        for step in range(steps):
            for load in loads[step]:
                load.wait()
            total = dot_tn((n_ref if step < half else g_ref)[...], right_ref[step])
            slot = step % slots
            for copy in flying[slot]:
                copy.wait()
            hold_ref[slot] = total.astype(BF16).reshape(groups, radix, shard, block)
            columns = pl.ds(step * block, block)
            flying[slot] = [
                copies.start(
                    hold_ref.at[slot, :, lax.rem(place_ref[0] + part, radix)], out_hbm[part].at[:, :, columns]
                )
                for part in range(radix)
            ]
        for group in flying:
            for copy in group:
                copy.wait()

    return call(
        kernel,
        "weight_grads",
        [ANY] * (3 * chunks + 1) + [SMEM],
        [ANY] * radix,
        [pltpu.HBM((groups, shard, 2 * units), BF16)] * radix,
        (*normed, *grad_hidden, *activated, grad_mlp, place),
        after,
        scratch=[
            pltpu.VMEM((chunks * rows, width), BF16),
            pltpu.VMEM((chunks * rows, width), BF16),
            pltpu.VMEM((steps, chunks * rows, block), BF16),
            pltpu.VMEM((slots, groups, radix, shard, block), BF16),
            pltpu.SemaphoreType.DMA((chunks + 1 + (chunks + radix) * steps,)),
        ],
    )


def attention_grads(normed, grads, grad_attn, mixed, weight, sums, table, raw, share, place, radix, shard, after, ties, bring):
    count, width = normed.shape
    block = max(256, radix * shard)
    wide, local = grads.shape[1], mixed[0].shape[1]
    extra = 128
    total = wide + local + extra
    groups = block // (radix * shard)
    chunks = len(mixed)
    head = 64
    flat_raw = [part for group in raw for part in group]
    n_raw = len(flat_raw)
    units = raw[3][0].shape[1]

    def kernel(n_ref, g_ref, *refs):
        a_refs, m_refs, refs = refs[:chunks], refs[chunks : 2 * chunks], refs[2 * chunks :]
        raw_refs, refs = refs[:n_raw], refs[n_raw:]
        w_ref, s_ref, table_ref, place_ref = refs[:4]
        out_hbm, (hold_ref, v_ref, sems) = refs[4 : 4 + radix], refs[4 + radix :]
        copies = Copies(sems)
        stores = []

        def vector(row):
            return table_ref[row : row + 1]

        def both(group):
            first = sum(len(g) for g in raw[:group])
            return sum(ref[...] for ref in raw_refs[first : first + len(raw[group])])

        middle, norm2, result, hidden = both(0), both(1), both(2), both(3)
        v_ref[...] = jnp.zeros_like(v_ref)
        v_ref[0:1] = vector(GAIN1)
        v_ref[1:2] = vector(SHIFT1)
        v_ref[2:3] = middle[0:1] / vector(SCALE_ATTN) * share
        v_ref[3:4] = middle[1:2] * vector(SCALE_ATTN) * share
        v_ref[4:6] = norm2
        v_ref[6:7] = result[0:1] + result[1:2] * vector(FC2_BIAS) * share
        v_ref[7:8] = result[1:2] * vector(SCALE_MLP) * share

        def spread(flats, first):
            stack = [f[:, i * head : (i + 1) * head] for f in flats for i in range(f.shape[1] // head)]
            stack = jnp.concatenate(stack, axis=0)
            for group in range(head // shard):
                piece = stack[:, group * shard : (group + 1) * shard]
                repeat = max(1, 128 // shard)
                piece = jnp.concatenate([piece] * repeat, axis=1)
                piece = jnp.concatenate([piece] * (width // (repeat * shard)), axis=1)
                v_ref[first : first + stack.shape[0]] = piece
                first += stack.shape[0]
            return first

        spread([hidden], spread([s_ref[0:1], s_ref[2:3]], 8))
        lane = lax.broadcasted_iota(jnp.int32, (block, extra), 1)
        for i in range(width // block):
            blk = slice(i * block, (i + 1) * block)
            columns = v_ref[:, blk].T
            first = second = None
            product = dot_tn(n_ref[:, blk], g_ref[...])
            for part in range(3):
                piece = product[:, part * local : (part + 1) * local]
                w = w_ref[part, blk].astype(F32)
                one = jnp.sum(w * piece, axis=1, keepdims=True)
                two = jnp.sum(w * s_ref[part : part + 1], axis=1, keepdims=True)
                first = one if first is None else first + one
                second = two if second is None else second + two
            gain_grad = (first - columns[:, 1:2] * second) / columns[:, 0:1]
            small = jnp.where(lane == 0, gain_grad, jnp.where(lane == 1, second, columns))
            product_p = None
            for c in range(chunks):
                term = dot_tn(a_refs[c][:, blk], m_refs[c][...])
                product_p = term if product_p is None else product_p + term
            for copy in stores[(i - 2) * radix : (i - 1) * radix] if i >= 2 else ():
                copy.wait()
            hold_ref[i % 2, :, :, :, :wide] = product.astype(BF16).reshape(groups, radix, shard, wide)
            hold_ref[i % 2, :, :, :, wide : wide + local] = product_p.astype(BF16).reshape(groups, radix, shard, local)
            hold_ref[i % 2, :, :, :, wide + local :] = small.astype(BF16).reshape(groups, radix, shard, extra)
            for step in range(radix):
                source = hold_ref.at[i % 2, :, lax.rem(place_ref[0] + step, radix)]
                stores.append(copies.start(source, out_hbm[step].at[pl.ds(i * groups, groups)]))
        for copy in stores[-2 * radix :]:
            copy.wait()

    return call(
        kernel,
        "attention_grads",
        [VMEM, VMEM] + [VMEM] * (2 * chunks + n_raw) + [VMEM, VMEM, VMEM, SMEM],
        [ANY] * radix,
        [pltpu.HBM((width // (radix * shard), shard, total), BF16)] * radix,
        (normed, grads, *grad_attn, *mixed, *flat_raw, weight, sums, table, place),
        after,
        scratch=[
            pltpu.VMEM((2, groups, radix, shard, total), BF16),
            pltpu.VMEM((extra, width), F32),
            pltpu.SemaphoreType.DMA((width // block * radix,)),
        ],
        ties=ties,
        bring=bring,
    )


def add_far_stage(ways, after, name, ties=()):
    sizes = [(len(way[0]), *way[0][0].shape[:2], way[2], way[3]) for way in ways]
    n_out = sum(size[4] for size in sizes)
    n_ways = len(ways)
    kept = [way[0][0] for way in ways]
    arrived = []
    for way in ways:
        arrived += [array for array in way[0][1:] if not any(array is other for other in arrived)]

    def kernel(*refs):
        hbm, refs = refs[:n_ways], refs[n_ways:]
        arrived_refs, place_refs, refs = refs[: len(arrived)], refs[len(arrived) :][:n_ways], refs[len(arrived) + n_ways :]
        out_hbm, refs = refs[:n_out], refs[n_out:]
        in_refs, out_refs, sems = refs[:n_ways], refs[n_ways : 2 * n_ways], refs[2 * n_ways]
        copies = Copies(sems)
        loads = []
        for w, (_, left, _, columns, radix) in enumerate(sizes):
            _, first, _, _, _, below = ways[w]
            span = radix * below
            loads.append(
                [
                    copies.start(
                        hbm[w].at[pl.ds(high * span, span), :, pl.ds(first, columns)],
                        in_refs[w].at[pl.ds(high * span, span)],
                    )
                    for high in range(left // span)
                ]
            )
        stores = []
        given = 0
        for w, (_, left, _, columns, radix) in enumerate(sizes):
            arrays, first, _, _, _, below = ways[w]
            others = [
                arrived_refs[next(i for i, other in enumerate(arrived) if other is array)] for array in arrays[1:]
            ]
            for group in range(left // radix):
                high, low = divmod(group, below)
                if low == 0:
                    loads[w][high].wait()
                for step in range(radix):
                    digit = lax.rem(place_refs[w][0] + step, radix)
                    source = (high * radix + digit) * below + low
                    total = in_refs[w][source].astype(F32)
                    for ref in others:
                        total = total + ref[source, :, first : first + columns].astype(F32)
                    out_refs[w][step, group] = total.astype(BF16)
                    stores.append(copies.start(out_refs[w].at[step, group], out_hbm[given + step].at[group]))
            given += radix
        for copy in stores:
            copy.wait()

    count = sum(left // (radix * way[5]) + left for (_, left, _, _, radix), way in zip(sizes, ways))
    out, done = call(
        kernel,
        name,
        [ANY] * n_ways + [VMEM] * len(arrived) + [SMEM] * n_ways,
        [ANY] * n_out,
        [pltpu.HBM((left // radix, rows, columns), BF16) for _, left, rows, columns, radix in sizes for _ in range(radix)],
        (*kept, *arrived, *[way[4] for way in ways]),
        after,
        scratch=[pltpu.VMEM((left, rows, columns), BF16) for _, left, rows, columns, _ in sizes]
        + [pltpu.VMEM((radix, left // radix, rows, columns), BF16) for _, left, rows, columns, radix in sizes]
        + [pltpu.SemaphoreType.DMA((count,))],
        ties=ties,
    )
    split = []
    for size in sizes:
        split.append(out[: size[4]])
        out = out[size[4] :]
    return split, done


def total_of(refs):
    total = None
    for ref in refs:
        term = ref[0].astype(F32)
        total = term if total is None else total + term
    return total


def last_stage(parts, local, after):
    _, shard, columns = parts[0].shape

    def kernel(*refs):
        part_refs, (qkv_ref, proj_ref, small_ref) = refs[:-3], refs[-3:]
        total = total_of(part_refs)
        for part in range(3):
            qkv_ref[part] = total[:, part * local : (part + 1) * local]
        proj_ref[...] = total[:, 3 * local : 4 * local]
        small_ref[...] = total[:, 4 * local :].T

    return call(
        kernel,
        "last_stage",
        [COPIED] + [VMEM] * (len(parts) - 1),
        [COPIED, COPIED, VMEM],
        [shape((3, shard, local), F32), shape((shard, local), F32), shape((columns - 4 * local, shard), F32)],
        tuple(parts),
        after,
    )


def last_far_stage(firsts, seconds, after):
    _, shard, units = firsts[0].shape
    n_second = len(seconds)

    def kernel(*refs):
        first_ref, second_ref = refs[-2:]
        first_ref[...] = total_of(refs[n_second:-2])
        second_ref[...] = total_of(refs[:n_second])

    return call(
        kernel,
        "last_far_stage",
        [COPIED] + [VMEM] * (n_second - 1) + [COPIED] + [VMEM] * (len(firsts) - 1),
        [COPIED] * 2,
        [shape((shard, units), F32), shape((shard, units), F32)],
        (*seconds, *firsts),
        after,
    )


def wait_for(arrays, after):
    def kernel():
        pass

    _, done = call(kernel, "wait_for", [], [], [], (), after, ties=arrays)
    return done


def middle_back(chunk, rows, terms, middle, tokens, cotangent, lengths, table, proj, after, bring):
    width = middle.shape[1]
    local = proj.shape[0]
    parts = len(terms)

    def kernel(*refs):
        term_refs, refs = refs[:parts], refs[parts:]
        mid_ref, x_hbm, c_hbm, lengths_ref, table_ref, p_ref = refs[:6]
        gmid_hbm, low_ref, gmix_ref, vec_ref, gmid_ref, x_ref, c_ref, sems = refs[6:]
        copies = Copies(sems)
        own = pl.ds(chunk * rows, rows)
        loads = [copies.start(c_hbm.at[own], c_ref), copies.start(x_hbm.at[own], x_ref)]
        grad_norm = None
        for ref in term_refs:
            term = ref[...].astype(F32)
            grad_norm = term if grad_norm is None else grad_norm + term
        middle = mid_ref[...]
        scaled, inverse = norm_parts(middle)
        back = norm_back(grad_norm, scaled, inverse, table_ref[GAIN2 : GAIN2 + 1])
        loads[0].wait()
        grad = c_ref[...].astype(F32) * valid_rows(lengths_ref, chunk * rows, rows) + back
        gmid_ref[...] = grad
        store = copies.start(gmid_ref, gmid_hbm)
        low = (table_ref[SCALE_ATTN : SCALE_ATTN + 1] * grad).astype(BF16)
        low_ref[...] = low
        gmix_ref[...] = dot_nt(low, p_ref[...]).astype(BF16)
        loads[1].wait()
        vec_ref[0:1] = col_sum(grad * (middle - x_ref[...].astype(F32)))
        vec_ref[1:2] = col_sum(grad)
        store.wait()

    return call(
        kernel,
        f"middle_back_{chunk}",
        [VMEM] * parts + [VMEM, ANY, ANY, SMEM, VMEM, VMEM],
        [ANY] + [VMEM] * 3,
        [
            pltpu.HBM((rows, width), F32),
            shape((rows, width), BF16),
            shape((rows, local), BF16),
            shape((2, width), F32),
        ],
        (*terms, middle, tokens, cotangent, lengths, table, proj),
        after,
        scratch=[
            pltpu.VMEM((rows, width), F32),
            pltpu.VMEM((rows, width), BF16),
            pltpu.VMEM((rows, width), BF16),
            pltpu.SemaphoreType.DMA((3,)),
        ],
        bring=bring,
    )


def first_norm_terms(chunks, grads, weight, after):
    width, local = weight.shape[1:]
    rows = grads.shape[0] // chunks

    def kernel(g_ref, w_hbm, *refs):
        out_refs, (w_ref, sems) = refs[:chunks], refs[chunks:]
        copies = Copies(sems)
        loads = [copies.start(w_hbm.at[part], w_ref.at[part]) for part in range(3)]
        for chunk in range(chunks):
            place = slice(chunk * rows, (chunk + 1) * rows)
            total = None
            for part in range(3):
                if chunk == 0:
                    loads[part].wait()
                term = dot_nt(g_ref[place, part * local : (part + 1) * local], w_ref[part])
                total = term if total is None else total + term
            out_refs[chunk][...] = total.astype(BF16)

    return call(
        kernel,
        "first_norm_terms",
        [VMEM, ANY],
        [VMEM] * chunks,
        [shape((rows, width), BF16)] * chunks,
        (grads, weight),
        after,
        scratch=[pltpu.VMEM(weight.shape, BF16), pltpu.SemaphoreType.DMA((3,))],
    )


def to_rows(chunk, rows, compute, args, specs, dims, kept, after, name, sources=(), ties=()):
    extra = 0 if kept is None else 1
    blocks = 2
    block = rows // blocks
    n_args = len(args)
    n_source = len(sources)
    args, specs = args + tuple(array for array, _ in sources), specs + [ANY] * n_source

    def kernel(*refs):
        ins, refs = refs[:n_args], refs[n_args:]
        source_hbm, refs = refs[:n_source], refs[n_source:]
        out_hbm, hold_ref, sems = refs[extra : extra + 3]
        source_refs = refs[extra + 3 :]
        copies = Copies(sems)
        loads = [
            [
                copies.start(hbm.at[pl.ds(first + i * block, block)], ref.at[i])
                for hbm, ref, (_, first) in zip(source_hbm, source_refs, sources)
            ]
            for i in range(blocks)
        ]
        stores = []
        for i in range(blocks):
            for load in loads[i]:
                load.wait()
            hold_ref[i] = compute(i * block, block, *[ref[i] for ref in source_refs], *ins).astype(BF16)
            place = pl.ds(chunk * rows + i * block, block)
            stores.append(copies.start(hold_ref.at[i], out_hbm.at[place]))
        for copy in stores:
            copy.wait()

    alias = None
    if extra:
        alias = {len(args): 0}
        args = args + (kept,)
    scratch = [
        pltpu.VMEM((blocks, block, dims[1]), BF16),
        pltpu.SemaphoreType.DMA(((1 + n_source) * blocks,)),
        *[pltpu.VMEM((blocks, block, dims[1]), array.dtype) for array, _ in sources],
    ]
    return call(
        kernel,
        name,
        specs + [ANY] * extra,
        ANY,
        pltpu.HBM(dims, BF16),
        args,
        after,
        scratch=scratch,
        alias=alias,
        ties=ties,
    )


def token_grads(chunk, rows, terms, grad_middle, tokens, table, kept, after):
    parts = len(terms)

    def compute(first, block, x, grad, *refs):
        table_ref = refs[parts]
        place = slice(first, first + block)
        grad_norm = None
        for ref in refs[:parts]:
            term = ref[place].astype(F32)
            grad_norm = term if grad_norm is None else grad_norm + term
        scaled, inverse = norm_parts(x.astype(F32))
        return grad + norm_back(grad_norm, scaled, inverse, table_ref[GAIN1 : GAIN1 + 1])

    args = (*terms, table)
    specs = [VMEM] * (parts + 1)
    sources = ((tokens, chunk * rows), (grad_middle, 0))
    return to_rows(chunk, rows, compute, args, specs, tokens.shape, kept, after, f"token_grads_{chunk}", sources)


def layer_output(chunk, rows, terms, middle, lengths, table, dims, kept, after):
    parts = len(terms)

    def compute(first, block, mid, *refs):
        lengths_ref, table_ref = refs[parts:]
        mlp = table_ref[FC2_BIAS : FC2_BIAS + 1]
        for term in refs[:parts]:
            mlp = mlp + term.astype(F32)
        valid = valid_rows(lengths_ref, chunk * rows + first, block)
        return valid * (mid + table_ref[SCALE_MLP : SCALE_MLP + 1] * mlp)

    sources = ((middle, 0), *((term, 0) for term in terms))
    name = f"layer_output_{chunk}"
    return to_rows(chunk, rows, compute, (lengths, table), [SMEM, VMEM], dims, kept, after, name, sources)


def from_peers(array):
    size = lax.axis_size("tensor")
    return [
        lax.ppermute(array, "tensor", [(i, (i + step) % size) for i in range(size)])
        for step in range(1, size)
    ]


def other_of_pair(array):
    return lax.ppermute(array, "dp", [(i, i ^ 1) for i in range(lax.axis_size("dp"))])


def radices(size):
    found = []
    if size % 2 == 0:
        found.append(2)
        size //= 2
    while size > 1:
        step = 2 if size % 4 and size % 2 == 0 or size == 8 else next((r for r in (4, 3) if size % r == 0), size)
        found.append(step)
        size //= step
    return found


def small_digits(size, stride):
    digits = []
    while stride < size:
        left = size // stride
        radix = next(r for r in (2, 3, 5, left) if left % r == 0)
        digits.append((stride, radix))
        stride *= radix
    return digits


def exchange(parts, stride, radix):
    size = lax.axis_size("dp")
    arrived = []
    for step in range(1, radix):
        moves = []
        for i in range(size):
            at = (i // stride) % radix
            moves.append((i, i + ((at + step) % radix - at) * stride))
        arrived.append(lax.ppermute(parts[step], "dp", moves))
    return [parts[0]] + arrived


def body(
    tokens,
    lengths,
    norm1_gain,
    norm1_bias,
    qkv_weight,
    qv_bias,
    proj_weight,
    proj_bias,
    scale_attn,
    norm2_gain,
    norm2_bias,
    fc1_weight,
    fc1_bias,
    fc2_weight,
    fc2_bias,
    scale_mlp,
    cotangent,
):
    count, width = tokens.shape
    heads, head_size = qv_bias.shape[1:]
    local = heads * head_size
    units = fc1_weight.shape[1]
    tensor = lax.axis_size("tensor")
    dp = lax.axis_size("dp")
    chunks = 2
    rows = count // chunks
    scale = head_size**-0.5

    def flat(vector):
        return vector.reshape(1, -1)

    index = lax.axis_index("dp")
    steps = radices(dp)
    strides = [1]
    for step in steps:
        strides.append(strides[-1] * step)
    places = [((index // stride) % step).reshape(1) for stride, step in zip(strides, steps)]

    half_rows = local // 2
    paired = dp % 2 == 0 and half_rows % 128 == 0
    half_place = (index % 2).reshape(1)
    half = proj_weight
    if paired:
        half = lax.dynamic_slice_in_dim(proj_weight, half_place[0] * half_rows, half_rows, 0)
    halves = from_peers(half)
    vectors = (norm1_gain, norm1_bias, norm2_gain, norm2_bias, proj_bias, scale_attn, fc2_bias, scale_mlp)
    out, done = attend_forward(
        tokens,
        lengths,
        [flat(vector) for vector in vectors],
        qkv_weight,
        qv_bias,
        scale,
        rows,
        (cotangent, fc2_weight, proj_weight, fc1_weight),
    )
    queries, keys, values, normed1, *near, table, cotangent_near, fc2_near, proj_weight, fc1_weight = out[:12]
    first, rest = out[12:]
    mixed_parts = [[first] + from_peers(first)]
    rest, done = attend_rest(*near, rest, lengths, done)
    mixed_parts.append([rest] + from_peers(rest))
    mixed = [first, rest]
    out, done = hidden_cotangent(cotangent_near, lengths, table, fc2_near, halves, chunks, done)
    grad_mlp, grad_act, halves = out[0], out[1 : 1 + chunks], out[1 + chunks :]
    if paired:
        halves = [part for half in halves for part in (half, other_of_pair(half))]

    middle, normed2, activated, grad_hidden, norm2_parts = [], [], [], [], []
    raw = [[], [], [], []]
    for chunk in range(chunks):
        out, done = feed_forward(
            chunk,
            rows,
            mixed_parts[chunk],
            proj_weight,
            halves,
            half_place,
            tokens,
            grad_act[chunk],
            table,
            fc1_weight,
            flat(fc1_bias),
            done,
        )
        for group, part in zip((middle, normed2, activated, grad_hidden), out[:4]):
            group.append(part)
        raw[3].append(out[4])
        raw[1].append(out[6])
        norm2_parts.append([out[5]] + from_peers(out[5]))

    shard = width // dp
    fc_parts, done = weight_grads(
        normed2, grad_hidden, grad_mlp, activated, places[0], steps[0], shard, done
    )
    fc_parts = exchange(fc_parts, 1, steps[0])

    def near_stage(parts, stage, done):
        way = (parts, 0, parts[0].shape[2], steps[stage], places[stage], 1)
        (parts,), done = add_far_stage([way], done, f"add_stage_{stage}")
        return exchange(parts, strides[stage], steps[stage]), done

    out, done = second_projection(activated, fc2_weight, cotangent, lengths, done, middle)
    mlp_parts = [[terms] + from_peers(terms) for terms in out[:chunks]]
    raw[2].append(out[chunks])
    middle_near = out[chunks + 1 :]

    grad_middle, grad_attn, grad_mixed = [], [], []
    for chunk in range(chunks):
        out, done = middle_back(
            chunk,
            rows,
            norm2_parts[chunk],
            middle_near[chunk],
            tokens,
            cotangent,
            lengths,
            table,
            proj_weight,
            done,
            (queries, keys, values) if chunk == 0 else (),
        )
        if chunk == 0:
            queries, keys, values = out[4:]
        for group, part in zip((grad_middle, grad_attn, grad_mixed), out[:3]):
            group.append(part)
        raw[0].append(out[3])
    stages = len(steps)
    digits = small_digits(dp, strides[1])
    orders = [digits, digits[1:] + digits[:1]]

    def far_stage(at, firsts, seconds, start, done, ties=()):
        ways = []
        for arrays, first, order in ((firsts, 0, orders[0]), (seconds, start, orders[1])):
            stride, radix = order[at]
            below = 1
            for other_stride, other_radix in order[at:]:
                below *= other_radix if other_stride < stride else 1
            place = ((index // stride) % radix).reshape(1)
            ways.append((arrays, first, units, radix, place, below))
        split, done = add_far_stage(ways, done, f"add_far_stage_{at}", ties)
        return [exchange(parts, *order[at]) for parts, order in zip(split, orders)], done

    (firsts, seconds), done = far_stage(0, fc_parts, fc_parts, units, done)
    (grads, grad_sums, qkv_near, normed1), done = attend_backward(
        queries, keys, values, grad_mixed, lengths, scale, done, (qkv_weight, normed1)
    )
    parts, done = attention_grads(
        normed1,
        grads,
        grad_attn,
        mixed,
        qkv_near,
        grad_sums,
        table,
        raw,
        1.0 / tensor,
        places[0],
        steps[0],
        shard,
        done,
        mlp_parts[0][1:],
        (),
    )
    parts = exchange(parts, 1, steps[0])
    if len(digits) > 1:
        (firsts, seconds), done = far_stage(1, firsts, seconds, 0, done)
    terms, done = first_norm_terms(chunks, grads, qkv_weight, done)
    norm1_parts = [[part] + from_peers(part) for part in terms]
    done = wait_for([part for group in mlp_parts[1:] for part in group[1:]], done)
    if stages > 1:
        parts, done = near_stage(parts, 1, done)
    output = None
    for chunk in range(chunks):
        output, done = layer_output(
            chunk, rows, mlp_parts[chunk], middle[chunk], lengths, table, tokens.shape, output, done
        )
    for at in range(2, len(digits)):
        (firsts, seconds), done = far_stage(at, firsts, seconds, 0, done)
    grad_tokens = None
    for chunk in range(chunks - 1):
        grad_tokens, done = token_grads(
            chunk, rows, norm1_parts[chunk], grad_middle[chunk], tokens, table, grad_tokens, done
        )
    for stage in range(2, stages):
        parts, done = near_stage(parts, stage, done)
    (fc1_grad, fc2_grad), done = last_far_stage(firsts, seconds, done)
    grad_tokens, done = token_grads(
        chunks - 1, rows, norm1_parts[-1], grad_middle[-1], tokens, table, grad_tokens, done
    )
    (qkv_grad, proj_grad, small), done = last_stage(parts, local, done)

    vector_share = small[:8]
    for other in from_peers(vector_share):
        vector_share = vector_share + other
    own = shard // tensor
    vector_share = lax.dynamic_slice_in_dim(vector_share, lax.axis_index("tensor") * own, own, 1)

    def columns_of(first, heads_in):
        groups = head_size // shard
        pieces = [small[first + i * heads_in : first + (i + 1) * heads_in] for i in range(groups)]
        every = pieces[0] if groups == 1 else jnp.concatenate(pieces, axis=1)
        return lax.dynamic_slice_in_dim(every, index * (head_size // dp), head_size // dp, 1)

    bias_share = columns_of(8, 2 * heads).reshape(2, heads, -1)
    fc1_share = columns_of(8 + 2 * heads * (head_size // shard), units // head_size)

    return (
        output,
        grad_tokens,
        vector_share[0],
        vector_share[1],
        qkv_grad,
        bias_share,
        proj_grad.T,
        vector_share[3],
        vector_share[2],
        vector_share[4],
        vector_share[5],
        fc1_grad,
        fc1_share,
        fc2_grad.T,
        vector_share[7],
        vector_share[6],
    )


def solution(mesh):
    in_specs = (
        P("dp", None),
        P("dp", None),
        P(),
        P(),
        P(None, None, "tensor"),
        P(None, "tensor", None),
        P("tensor", None),
        P(),
        P(),
        P(),
        P(),
        P(None, "tensor"),
        P("tensor"),
        P("tensor", None),
        P(),
        P(),
        P("dp", None),
    )
    out_specs = (
        P("dp", None),
        P("dp", None),
        P(("dp", "tensor")),
        P(("dp", "tensor")),
        P(None, "dp", "tensor"),
        P(None, "tensor", "dp"),
        P("tensor", "dp"),
        P(("dp", "tensor")),
        P(("dp", "tensor")),
        P(("dp", "tensor")),
        P(("dp", "tensor")),
        P("dp", "tensor"),
        P("tensor", "dp"),
        P("tensor", "dp"),
        P(("dp", "tensor")),
        P(("dp", "tensor")),
    )
    return jax.shard_map(body, mesh=mesh, in_specs=in_specs, out_specs=out_specs, check_vma=False)
```

```python
from functools import partial

import jax
import jax.numpy as jnp
from jax import lax
from jax.experimental import pallas as pl
from jax.experimental.pallas import tpu as pltpu
from jax.sharding import PartitionSpec as P

EPS = 1e-06
NEGATIVE = -1e30
GLOBAL_LEN = 197
LOCAL_LEN = 37
GROUP = GLOBAL_LEN // LOCAL_LEN
WINDOW = 224
BF16 = jnp.bfloat16
F32 = jnp.float32
MIB = 1 << 20
VMEM_MIB = 16
SPARE = 6
LIMITS = {
    "attend_forward": 14,
    "attend_rest": 6,
    "hidden_cotangent": 6,
    "feed_forward": 15,
    "weight_grads": 17,
    "second_projection": 18,
    "middle_back": 15,
    "attend_backward": 11,
    "attention_grads": 14,
    "layer_output": 13,
    "first_norm_terms": 9,
    "add_stage": 8,
    "token_grads": 9,
    "last_stage": 8,
    "last_far_stage": 8,
    "wait_for": 1,
    "add_far_stage": 16,
}
COST = 2300000000
COSTS = {"middle_back_1": 46000000000, "wait_for": 16100000000, "token_grads_0": 13800000000}


def dot_nn(a, b):
    return lax.dot_general(a, b, (((1,), (0,)), ((), ())), preferred_element_type=F32)


def dot_nt(a, b):
    return lax.dot_general(a, b, (((1,), (1,)), ((), ())), preferred_element_type=F32)


def dot_tn(a, b):
    return lax.dot_general(a, b, (((0,), (0,)), ((), ())), preferred_element_type=F32)


def norm_parts(values):
    average = jnp.mean(values, axis=-1, keepdims=True)
    centered = values - average
    inverse = lax.rsqrt(jnp.mean(centered * centered, axis=-1, keepdims=True) + EPS)
    return centered * inverse, inverse


def norm_back(grad_norm, scaled, inverse, gain):
    grad_hat = grad_norm * gain
    first_mean = jnp.mean(grad_hat, axis=-1, keepdims=True)
    second_mean = jnp.mean(grad_hat * scaled, axis=-1, keepdims=True)
    return inverse * (grad_hat - first_mean - scaled * second_mean)


def col_sum(values):
    return jnp.sum(values, axis=0, keepdims=True)


def call(kernel, name, in_specs, out_specs, out_shape, args, after=None, scratch=(), vmem=VMEM_MIB, alias=None, bring=(), late=False, ties=()):
    single = not isinstance(out_shape, list)
    if single:
        out_specs, out_shape = [out_specs], [out_shape]
    n_in, n_out, n_bring = len(args), len(out_shape), len(bring)
    after = list(ties) if after is None else [after, *ties]
    n_after = len(after)
    args = [
        pltpu.with_memory_space_constraint(arg, pltpu.VMEM if spec is VMEM else pltpu.HBM)
        if spec is VMEM or spec is ANY
        else arg
        for arg, spec in zip(args, in_specs)
    ]
    args += [pltpu.with_memory_space_constraint(arg, pltpu.HBM) for arg in bring]
    out_shape = [
        pltpu.VMEM(o.shape, o.dtype) if spec is VMEM else o for o, spec in zip(out_shape, out_specs)
    ]

    def ordered(*refs):
        ins, refs = refs[:n_in], refs[n_in:]
        bring_hbm, refs = refs[:n_bring], refs[n_bring + n_after :]
        outs, refs = refs[:n_out], refs[n_out:]
        bring_refs, done, refs = refs[:n_bring], refs[n_bring], refs[n_bring + 1 :]
        done[...] = jnp.zeros_like(done)
        loads = []
        if n_bring:
            refs, sems = refs[:-1], refs[-1]

        def begin():
            for i in range(n_bring):
                loads.append(pltpu.make_async_copy(bring_hbm[i], bring_refs[i], sems.at[i]))
                loads[-1].start()

        if late:
            kernel(begin, *ins, *outs, *refs)
        else:
            begin()
            kernel(*ins, *outs, *refs)
        for load in loads:
            load.wait()

    out = pl.pallas_call(
        ordered,
        in_specs=list(in_specs) + [ANY] * (n_bring + n_after),
        out_specs=list(out_specs) + [VMEM] * (n_bring + 1),
        out_shape=list(out_shape) + [pltpu.VMEM(a.shape, a.dtype) for a in bring] + [pltpu.VMEM((8, 128), F32)],
        scratch_shapes=list(scratch) + ([pltpu.SemaphoreType.DMA((n_bring,))] if n_bring else []),
        input_output_aliases=alias or {},
        compiler_params=pltpu.CompilerParams(vmem_limit_bytes=(LIMITS.get(name.rstrip("_0123456789"), vmem) + SPARE) * MIB),
        cost_estimate=pl.CostEstimate(flops=COSTS.get(name, COST), bytes_accessed=COST, transcendentals=0),
        name=name,
    )(*args, *after)
    return (out[0] if single and not n_bring else out[:-1]), out[-1]


class Copies:
    def __init__(self, sems):
        self.sems = sems
        self.used = 0

    def start(self, source, target):
        copy = pltpu.make_async_copy(source, target, self.sems.at[self.used])
        self.used += 1
        copy.start()
        return copy


def shape(dims, dtype):
    return jax.ShapeDtypeStruct(dims, dtype)


SMEM = pl.BlockSpec(memory_space=pltpu.SMEM)
VMEM = pl.BlockSpec(memory_space=pltpu.VMEM)
ANY = pl.BlockSpec(memory_space=pl.ANY)
COPIED = pl.BlockSpec(memory_space=pltpu.VMEM)

GAIN1, SHIFT1, GAIN2, SHIFT2, PROJ_BIAS, SCALE_ATTN, FC2_BIAS, SCALE_MLP = range(8)


def row_total(lengths_ref):
    total = jnp.int32(0)
    for slot in range(lengths_ref.shape[1]):
        total = total + lengths_ref[0, slot]
    return total


def valid_rows(lengths_ref, first, rows):
    places = lax.broadcasted_iota(jnp.int32, (rows, 1), 0) + first
    return (places < row_total(lengths_ref)).astype(F32)


def item_counts(lengths_ref):
    globals_ = jnp.int32(0)
    locals_ = jnp.int32(0)
    for slot in range(lengths_ref.shape[1]):
        value = lengths_ref[0, slot]
        globals_ = globals_ + jnp.where(value == GLOBAL_LEN, 1, 0)
        locals_ = locals_ + jnp.where(value == LOCAL_LEN, 1, 0)
    return globals_, locals_


def item_place(item, globals_, locals_, count):
    is_global = item < globals_
    group = item - globals_
    start = jnp.where(
        is_global, item * GLOBAL_LEN, globals_ * GLOBAL_LEN + group * (GROUP * LOCAL_LEN)
    )
    length = jnp.where(
        is_global, GLOBAL_LEN, jnp.minimum(locals_ - group * GROUP, GROUP) * LOCAL_LEN
    )
    crop = jnp.where(is_global, GLOBAL_LEN, LOCAL_LEN)
    first = jnp.minimum((start // 16) * 16, count - WINDOW)
    return pl.multiple_of(first, 16), start - first, length, crop


def crop_of(places, offset, length, crop, outside):
    inside = (places >= offset) & (places < offset + length)
    index = places - offset
    label = jnp.zeros_like(places)
    for step in range(1, GROUP):
        label = label + jnp.where(index >= step * crop, 1, 0)
    return jnp.where(inside, label, outside)


def item_total(globals_, locals_):
    return globals_ + (locals_ + GROUP - 1) // GROUP


def attend_items(first_item, last_item, q_ref, k_ref, v_ref, out_ref, skipped, lengths_ref):
    count, local = q_ref.shape
    pair = 128
    pairs = local // pair
    globals_, locals_ = item_counts(lengths_ref)
    low_half = lax.broadcasted_iota(jnp.int32, (1, pair), 1) < pair // 2

    def step(item, carry):
        first, offset, length, crop = item_place(item, globals_, locals_, count)
        window = pl.ds(first, WINDOW)
        placed = pl.ds(pl.multiple_of(first - skipped, 16), WINDOW)
        by_key = lax.broadcasted_iota(jnp.int32, (WINDOW, 1), 0)
        by_query = lax.broadcasted_iota(jnp.int32, (1, WINDOW), 1)
        query_crop = crop_of(by_query, offset, length, crop, -2)
        key_crop = crop_of(by_key, offset, length, crop, -1)
        mask = jnp.where(query_crop == key_crop, 0.0, NEGATIVE)
        inside = key_crop >= 0

        def products(index):
            columns = slice(index * pair, (index + 1) * pair)
            return dot_nt(heads_apart(k_ref[window, columns], low_half), q_ref[window, columns])

        now = products(0)
        for index in range(pairs):
            columns = slice(index * pair, (index + 1) * pair)
            later = products(index + 1) if index + 1 < pairs else None
            scores = now.reshape(2, WINDOW, WINDOW) + mask
            weights = jnp.exp(scores - jnp.max(scores, axis=1, keepdims=True))
            total = jnp.sum(weights, axis=1, keepdims=True)
            low = (weights * (1.0 / total)).astype(BF16).reshape(2 * WINDOW, WINDOW)
            out = dot_tn(low, heads_apart(v_ref[window, columns], low_half))
            now = later
            kept = out_ref[placed, columns].astype(F32)
            out_ref[placed, columns] = jnp.where(inside, out, kept).astype(BF16)
        return carry

    lax.fori_loop(first_item, jnp.minimum(last_item, item_total(globals_, locals_)), step, 0)


def attend_forward(tokens, lengths, vectors, weight, qv_bias, scale, rows, later):
    count, width = tokens.shape
    local = weight.shape[2]
    head = 64
    block = 256
    blocks = count // block
    n_vec, n_later = len(vectors), len(later)

    def kernel(x_hbm, w_hbm, *refs):
        later_hbm, refs = refs[:n_later], refs[n_later:]
        vec_hbm, refs = refs[:n_vec], refs[n_vec:]
        qv_hbm, lengths_ref, refs = refs[0], refs[1], refs[2:]
        q_hbm, k_hbm, v_hbm, n_hbm, q_ref, k_ref, v_ref, table_ref, refs = *refs[:8], refs[8:]
        later_refs, (first_ref, rest_ref), refs = refs[:n_later], refs[n_later : n_later + 2], refs[n_later + 2 :]
        vec_refs, refs = refs[:n_vec], refs[n_vec:]
        heads_ref, x_ref, w_ref, n_ref, out_ref, sems = refs
        copies = Copies(sems)

        def part(ref, index):
            return ref.at[pl.ds(index * block, block)]

        loads = [copies.start(part(x_hbm, 0), part(x_ref, 0))]
        small_loads = [copies.start(hbm, ref) for hbm, ref in zip(vec_hbm[:2], vec_refs[:2])]
        weight_loads = [copies.start(w_hbm.at[0], w_ref.at[0])]
        small_loads.append(copies.start(qv_hbm, heads_ref))
        weight_loads += [copies.start(w_hbm.at[i], w_ref.at[i]) for i in range(1, 3)]
        loads += [copies.start(part(x_hbm, i), part(x_ref, i)) for i in range(1, blocks)]
        table_loads = [copies.start(hbm, ref) for hbm, ref in zip(vec_hbm[2:], vec_refs[2:])]
        later_loads = [copies.start(hbm, ref) for hbm, ref in zip(later_hbm, later_refs)]

        def scaled_of(i):
            loads[i].wait()
            return norm_parts(x_ref[i * block : (i + 1) * block].astype(F32))[0]

        def normed_of(i):
            return (scaled_of(i) * vec_refs[GAIN1][...] + vec_refs[SHIFT1][...]).astype(BF16)

        scaled = scaled_of(0)
        for load in small_loads:
            load.wait()
        qv = [
            jnp.concatenate([heads_ref[i, h : h + 1] for h in range(local // head)], axis=1)
            for i in range(2)
        ]
        now = (scaled * vec_refs[GAIN1][...] + vec_refs[SHIFT1][...]).astype(BF16)
        for i in range(blocks):
            rows_i = slice(i * block, (i + 1) * block)
            after = normed_of(i + 1) if i + 1 < blocks else None
            n_ref[rows_i] = now
            if i == 0:
                weight_loads[0].wait()
            queries = (dot_nn(now, w_ref[0]) + qv[0]).astype(BF16)
            q_ref[rows_i] = queries * BF16(scale)
            if i == 0:
                weight_loads[1].wait()
            k_ref[rows_i] = dot_nn(now, w_ref[1]).astype(BF16)
            if i == 0:
                weight_loads[2].wait()
            v_ref[rows_i] = (dot_nn(now, w_ref[2]) + qv[1]).astype(BF16)
            now = after
        stores = [
            copies.start(ref, hbm)
            for ref, hbm in ((q_ref, q_hbm), (k_ref, k_hbm), (v_ref, v_hbm), (n_ref, n_hbm))
        ]
        average = col_sum(v_ref[...].astype(F32)) * (1.0 / count)
        out_ref[...] = jnp.broadcast_to(average, (count, local)).astype(BF16)
        attend_items(0, first_items(rows), q_ref, k_ref, v_ref, out_ref, 0, lengths_ref)
        first_ref[...] = out_ref[:rows]
        rest_ref[...] = out_ref[rows:]
        for load in table_loads:
            load.wait()
        for i in range(n_vec):
            table_ref[i : i + 1] = vec_refs[i][...]
        for copy in later_loads + stores:
            copy.wait()

    part = pltpu.HBM((count, local), BF16)
    near = shape((count, local), BF16)
    outs = [part, part, part, pltpu.HBM((count, width), BF16), near, near, near, shape((n_vec, width), F32)]
    outs += [shape(a.shape, a.dtype) for a in later] + [shape((rows, local), BF16), shape((count - rows, local), BF16)]
    args = (tokens, weight, *later, *vectors, qv_bias, lengths)
    return call(
        kernel,
        "attend_forward",
        [ANY] * (len(args) - 1) + [SMEM],
        [ANY] * 4 + [VMEM] * (len(outs) - 4),
        outs,
        args,
        scratch=[pltpu.VMEM((1, width), F32)] * n_vec
        + [
            pltpu.VMEM(qv_bias.shape, F32),
            pltpu.VMEM((count, width), BF16),
            pltpu.VMEM(weight.shape, BF16),
            pltpu.VMEM((count, width), BF16),
            pltpu.VMEM((count, local), BF16),
            pltpu.SemaphoreType.DMA((blocks + 8 + n_later + n_vec,)),
        ],
    )


def first_items(rows):
    return -(-rows // (GROUP * LOCAL_LEN))


def attend_rest(queries, keys, values, rest, lengths, after):
    rows = queries.shape[0] - rest.shape[0]

    def kernel(q_ref, k_ref, v_ref, rest_ref, lengths_ref, out_ref):
        out_ref[...] = rest_ref[...]
        attend_items(first_items(rows), 1 << 20, q_ref, k_ref, v_ref, out_ref, rows, lengths_ref)

    return call(
        kernel,
        "attend_rest",
        [VMEM] * 4 + [SMEM],
        VMEM,
        shape(rest.shape, BF16),
        (queries, keys, values, rest, lengths),
        after,
    )


def heads_apart(both, low_half):
    return jnp.concatenate([jnp.where(low_half, both, BF16(0)), jnp.where(low_half, BF16(0), both)], axis=0)


def heads_together(apart, low_half):
    return jnp.where(low_half, apart[:WINDOW], apart[WINDOW:])


def attend_backward(queries, keys, values, grad_mixed, lengths, scale, after, bring):
    count, local = queries.shape
    head = 64
    pair = 2 * head

    chunks = len(grad_mixed)
    rows = count // chunks

    def kernel(q_ref, k_ref, v_ref, *refs):
        chunk_refs, refs = refs[:chunks], refs[chunks:]
        lengths_ref, out_ref, bias_ref, acc_ref, g_ref = refs
        for chunk in range(chunks):
            g_ref[chunk * rows : (chunk + 1) * rows] = chunk_refs[chunk][...]
        globals_, locals_ = item_counts(lengths_ref)
        acc_ref[...] = jnp.zeros_like(acc_ref)
        low_half = lax.broadcasted_iota(jnp.int32, (1, pair), 1) < head

        def step(item, carry):
            first, offset, length, crop = item_place(item, globals_, locals_, count)
            window = pl.ds(first, WINDOW)
            by_key = lax.broadcasted_iota(jnp.int32, (WINDOW, 1), 0)
            by_query = lax.broadcasted_iota(jnp.int32, (1, WINDOW), 1)
            query_crop = crop_of(by_query, offset, length, crop, -2)
            key_crop = crop_of(by_key, offset, length, crop, -1)
            mask = jnp.where(query_crop == key_crop, 0.0, NEGATIVE)
            inside = key_crop >= 0
            def products(index):
                columns = slice(index * pair, (index + 1) * pair)
                q2 = q_ref[window, columns]
                g2 = jnp.where(inside, g_ref[window, columns], BF16(0))
                both_k = heads_apart(k_ref[window, columns], low_half)
                both_v = heads_apart(v_ref[window, columns], low_half)
                return q2, g2, both_k, dot_nt(both_k, q2), dot_nt(both_v, g2)

            pairs = local // pair
            now = products(0)
            for index in range(pairs):
                columns = slice(index * pair, (index + 1) * pair)
                later = products(index + 1) if index + 1 < pairs else None
                q2, g2, both_k, scores, grad_probability = now
                now = later
                scores = scores.reshape(2, WINDOW, WINDOW) + mask
                weights = jnp.exp(scores - jnp.max(scores, axis=1, keepdims=True))
                total = jnp.sum(weights, axis=1, keepdims=True)
                probability = weights * (1.0 / total)
                grad_probability = grad_probability.reshape(2, WINDOW, WINDOW)
                delta = jnp.sum(probability * grad_probability, axis=1, keepdims=True)
                grad_scores = (probability * (grad_probability - delta)).astype(BF16)
                grad_scores = grad_scores.reshape(2 * WINDOW, WINDOW)
                low = probability.astype(BF16).reshape(2 * WINDOW, WINDOW)
                grad_v = heads_together(dot_nn(low, g2), low_half)
                grad_k = heads_together(dot_nn(grad_scores, q2), low_half)
                grad_q = dot_tn(grad_scores, both_k)
                acc_ref[0, window, columns] += grad_q * scale
                acc_ref[1, window, columns] += grad_k
                acc_ref[2, window, columns] += grad_v
            return carry

        lax.fori_loop(0, item_total(globals_, locals_), step, 0)
        for part in range(3):
            out_ref[:, part * local : (part + 1) * local] = acc_ref[part].astype(BF16)
            bias_ref[part : part + 1] = col_sum(acc_ref[part])

    return call(
        kernel,
        "attend_backward",
        [VMEM, VMEM, VMEM] + [VMEM] * chunks + [SMEM],
        [VMEM, VMEM],
        [shape((count, 3 * local), BF16), shape((3, local), F32)],
        (queries, keys, values, *grad_mixed, lengths),
        after,
        scratch=[pltpu.VMEM((3, count, local), F32), pltpu.VMEM((count, local), BF16)],
        bring=bring,
    )


def gelu_parts(value):
    size = jnp.abs(value)
    bell = jnp.exp(value * value * -0.5)
    t = 1.0 / (1.0 + size * (0.3275911 * 0.7071067811865476))
    poly = t * (
        0.254829592
        + t * (-0.284496736 + t * (1.421413741 + t * (-1.453152027 + t * 1.061405429)))
    )
    tail = 0.5 * poly * bell
    share = jnp.where(value >= 0, 1.0 - tail, tail)
    return value * share, share + value * (bell * 0.3989422804014327)


def hidden_cotangent(cotangent, lengths, table, fc2, halves, chunks, after):
    count, width = cotangent.shape
    units = fc2.shape[0]
    rows = count // chunks
    n_half = len(halves)

    def kernel(c_ref, w_ref, table_ref, lengths_ref, *refs):
        half_refs, refs = refs[:n_half], refs[n_half:]
        gm_hbm, ga_refs, on_refs = refs[0], refs[1 : 1 + chunks], refs[1 + chunks : 1 + chunks + n_half]
        gm_ref, sems = refs[1 + chunks + n_half :]
        copies = Copies(sems)
        stores = []
        for half_ref, on_ref in zip(half_refs, on_refs):
            on_ref[...] = half_ref[...]
        for chunk in range(chunks):
            place = chunk * rows
            grad = c_ref[place : place + rows].astype(F32) * valid_rows(lengths_ref, place, rows)
            low = (grad * table_ref[SCALE_MLP : SCALE_MLP + 1]).astype(BF16)
            gm_ref[place : place + rows] = low
            own = pl.ds(place, rows)
            stores.append(copies.start(gm_ref.at[own], gm_hbm.at[own]))
            ga_refs[chunk][...] = dot_nt(low, w_ref[...]).astype(BF16)
        for copy in stores:
            copy.wait()

    return call(
        kernel,
        "hidden_cotangent",
        [VMEM, VMEM, VMEM, SMEM] + [VMEM] * n_half,
        [ANY] + [VMEM] * (chunks + n_half),
        [pltpu.HBM((count, width), BF16)]
        + [shape((rows, units), BF16)] * chunks
        + [shape(half.shape, BF16) for half in halves],
        (cotangent, fc2, table, lengths, *halves),
        after,
        scratch=[pltpu.VMEM((count, width), BF16), pltpu.SemaphoreType.DMA((chunks,))],
    )


def feed_forward(chunk, rows, mixed, proj, halves, place, tokens, grad_act, table, fc1, fc1_bias, after):
    width = tokens.shape[1]
    units = fc1.shape[1]
    step_units = min(512, units)
    steps = units // step_units
    parts = len(mixed)
    n_half = len(halves)
    depth = proj.shape[0] // 2

    def kernel(*refs):
        mixed_refs, p_ref, half_refs, refs = refs[:parts], refs[parts], refs[parts + 1 : parts + 1 + n_half], refs[parts + 1 + n_half :]
        place_ref, x_hbm, ga_ref, table_ref, fc1_ref, fb_ref = refs[:6]
        mid_hbm, n2_hbm, act_hbm, gh_hbm, fbg_ref, terms_ref, refs = *refs[6:12], refs[12:]
        mid_ref, n2_ref, act_ref, gh_ref, x_ref, sems = refs
        copies = Copies(sems)
        load = copies.start(x_hbm.at[pl.ds(chunk * rows, rows)], x_ref)

        def vector(row):
            return table_ref[row : row + 1]

        attn = vector(PROJ_BIAS) + dot_nn(mixed_refs[0][...], p_ref[...]).astype(BF16).astype(F32)
        for peer in range(parts - 1):
            m_ref = mixed_refs[peer + 1]
            if n_half == parts - 1:
                term = dot_nn(m_ref[...], half_refs[peer][...])
            else:
                first = pl.ds(pl.multiple_of(place_ref[0] * depth, depth), depth)
                other = pl.ds(pl.multiple_of((1 - place_ref[0]) * depth, depth), depth)
                term = dot_nn(m_ref[:, first], half_refs[2 * peer][...])
                term = term + dot_nn(m_ref[:, other], half_refs[2 * peer + 1][...])
            attn = attn + term.astype(BF16).astype(F32)
        load.wait()
        middle = x_ref[...].astype(F32) + vector(SCALE_ATTN) * attn
        mid_ref[...] = middle
        stores = [copies.start(mid_ref, mid_hbm)]
        scaled, _ = norm_parts(middle)
        n2_ref[...] = (scaled * vector(GAIN2) + vector(SHIFT2)).astype(BF16)
        stores.append(copies.start(n2_ref, n2_hbm))

        def hidden_of(j):
            units_j = slice(j * step_units, (j + 1) * step_units)
            return dot_nn(n2_ref[...], fc1_ref[:, units_j]) + fb_ref[:, units_j]

        total = None
        hidden = hidden_of(0)
        for j in range(steps):
            units_j = slice(j * step_units, (j + 1) * step_units)
            later = hidden_of(j + 1) if j + 1 < steps else None
            activated, slope = gelu_parts(hidden)
            own = pl.ds(j * step_units, step_units)
            act_ref[:, units_j] = activated.astype(BF16)
            stores.append(copies.start(act_ref.at[:, own], act_hbm.at[:, own]))
            grad_hidden = ga_ref[:, units_j].astype(F32) * slope
            fbg_ref[:, units_j] = col_sum(grad_hidden)
            low = grad_hidden.astype(BF16)
            gh_ref[:, units_j] = low
            stores.append(copies.start(gh_ref.at[:, own], gh_hbm.at[:, own]))
            term = dot_nt(low, fc1_ref[:, units_j])
            total = term if total is None else total + term
            hidden = later
        terms_ref[...] = total.astype(BF16)
        for copy in stores:
            copy.wait()

    args = (*mixed, proj, *halves, place, tokens, grad_act, table, fc1, fc1_bias)
    return call(
        kernel,
        "feed_forward",
        [VMEM] * (parts + 1 + n_half) + [SMEM, ANY] + [VMEM] * 3 + [COPIED],
        [ANY] * 4 + [VMEM] * 2,
        [
            pltpu.HBM((rows, width), F32),
            pltpu.HBM((rows, width), BF16),
            pltpu.HBM((rows, units), BF16),
            pltpu.HBM((rows, units), BF16),
            shape((1, units), F32),
            shape((rows, width), BF16),
        ],
        args,
        after,
        scratch=[
            pltpu.VMEM((rows, width), F32),
            pltpu.VMEM((rows, width), BF16),
            pltpu.VMEM((rows, units), BF16),
            pltpu.VMEM((rows, units), BF16),
            pltpu.VMEM((rows, width), BF16),
            pltpu.SemaphoreType.DMA((3 + 2 * steps,)),
        ],
    )


def second_projection(activated, fc2, cotangent, lengths, after, bring):
    units, width = fc2.shape
    chunks = len(activated)
    rows = activated[0].shape[0]
    block = min(512, units)
    steps = units // block

    def kernel(begin, *refs):
        a_hbm, refs = refs[:chunks], refs[chunks:]
        w_hbm, c_hbm, lengths_ref, refs = refs[0], refs[1], refs[2], refs[3:]
        out_hbm, vec_ref, refs = refs[:chunks], refs[chunks], refs[chunks + 1 :]
        a_refs, (w_ref, c_ref, out_ref, sems) = refs[:chunks], refs[chunks:]
        stores = []
        copies = Copies(sems)
        loads = []
        for j in range(steps):
            own = pl.ds(j * block, block)
            loads.append([copies.start(w_hbm.at[own], w_ref.at[own])])
            loads[j].append(copies.start(a_hbm[0].at[:, own], a_refs[0].at[:, own]))
        late = [copies.start(hbm, ref) for hbm, ref in zip(a_hbm[1:], a_refs[1:])]
        late.append(copies.start(c_hbm, c_ref))
        begin()
        for chunk in range(chunks):
            total = None
            if chunk == 0:
                for j in range(steps):
                    for load in loads[j]:
                        load.wait()
                    place = slice(j * block, (j + 1) * block)
                    term = dot_nn(a_refs[0][:, place], w_ref[place])
                    total = term if total is None else total + term
                for load in late:
                    load.wait()
            else:
                total = dot_nn(a_refs[chunk][...], w_ref[...])
            terms = total.astype(BF16)
            place = slice(chunk * rows, (chunk + 1) * rows)
            out_ref[place] = terms
            stores.append(copies.start(out_ref.at[pl.ds(chunk * rows, rows)], out_hbm[chunk]))
            grad = c_ref[place].astype(F32) * valid_rows(lengths_ref, chunk * rows, rows)
            first, second = col_sum(grad * terms.astype(F32)), col_sum(grad)
            vec_ref[0:1] = first if chunk == 0 else vec_ref[0:1] + first
            vec_ref[1:2] = second if chunk == 0 else vec_ref[1:2] + second
        for copy in stores:
            copy.wait()

    return call(
        kernel,
        "second_projection",
        [ANY] * (chunks + 2) + [SMEM],
        [ANY] * chunks + [VMEM],
        [pltpu.HBM((rows, width), BF16)] * chunks + [shape((2, width), F32)],
        (*activated, fc2, cotangent, lengths),
        after,
        scratch=[pltpu.VMEM((rows, units), BF16)] * chunks
        + [
            pltpu.VMEM(fc2.shape, BF16),
            pltpu.VMEM(cotangent.shape, BF16),
            pltpu.VMEM(cotangent.shape, BF16),
            pltpu.SemaphoreType.DMA((2 * steps + 2 * chunks,)),
        ],
        bring=bring,
        late=True,
    )


def weight_grads(normed, grad_hidden, grad_mlp, activated, place, radix, shard, after):
    width = normed[0].shape[1]
    chunks = len(normed)
    rows = normed[0].shape[0]
    units = activated[0].shape[1]
    block = min(512, units)
    slots = 2
    steps = 2 * units // block
    half = steps // 2
    groups = width // (radix * shard)

    def kernel(*refs):
        n_hbm, h_hbm, a_hbm = refs[:chunks], refs[chunks : 2 * chunks], refs[2 * chunks : 3 * chunks]
        g_hbm, place_ref, refs = refs[3 * chunks], refs[3 * chunks + 1], refs[3 * chunks + 2 :]
        out_hbm, (n_ref, g_ref, right_ref, hold_ref, sems) = refs[:radix], refs[radix:]
        copies = Copies(sems)

        def rows_of(chunk):
            return pl.ds(chunk * rows, rows)

        loads = [[] for _ in range(steps)]
        for c in range(chunks):
            loads[0].append(copies.start(n_hbm[c], n_ref.at[rows_of(c)]))
        for step in range(steps):
            own = pl.ds(step % half * block, block)
            if step == half:
                loads[step].append(copies.start(g_hbm, g_ref))
            for c in range(chunks):
                source = (h_hbm if step < half else a_hbm)[c].at[:, own]
                loads[step].append(copies.start(source, right_ref.at[step, rows_of(c)]))
        flying = [[] for _ in range(slots)]
        for step in range(steps):
            for load in loads[step]:
                load.wait()
            total = dot_tn((n_ref if step < half else g_ref)[...], right_ref[step])
            slot = step % slots
            for copy in flying[slot]:
                copy.wait()
            hold_ref[slot] = total.astype(BF16).reshape(groups, radix, shard, block)
            columns = pl.ds(step * block, block)
            flying[slot] = [
                copies.start(
                    hold_ref.at[slot, :, lax.rem(place_ref[0] + part, radix)], out_hbm[part].at[:, :, columns]
                )
                for part in range(radix)
            ]
        for group in flying:
            for copy in group:
                copy.wait()

    return call(
        kernel,
        "weight_grads",
        [ANY] * (3 * chunks + 1) + [SMEM],
        [ANY] * radix,
        [pltpu.HBM((groups, shard, 2 * units), BF16)] * radix,
        (*normed, *grad_hidden, *activated, grad_mlp, place),
        after,
        scratch=[
            pltpu.VMEM((chunks * rows, width), BF16),
            pltpu.VMEM((chunks * rows, width), BF16),
            pltpu.VMEM((steps, chunks * rows, block), BF16),
            pltpu.VMEM((slots, groups, radix, shard, block), BF16),
            pltpu.SemaphoreType.DMA((chunks + 1 + (chunks + radix) * steps,)),
        ],
    )


def attention_grads(normed, grads, grad_attn, mixed, weight, sums, table, raw, share, place, radix, shard, after, ties, bring):
    count, width = normed.shape
    block = max(256, radix * shard)
    wide, local = grads.shape[1], mixed[0].shape[1]
    extra = 128
    total = wide + local + extra
    groups = block // (radix * shard)
    chunks = len(mixed)
    head = 64
    flat_raw = [part for group in raw for part in group]
    n_raw = len(flat_raw)

    def kernel(n_ref, g_ref, *refs):
        a_refs, m_refs, refs = refs[:chunks], refs[chunks : 2 * chunks], refs[2 * chunks :]
        raw_refs, refs = refs[:n_raw], refs[n_raw:]
        w_ref, s_ref, table_ref, place_ref = refs[:4]
        out_hbm, (hold_ref, v_ref, sems) = refs[4 : 4 + radix], refs[4 + radix :]
        copies = Copies(sems)
        stores = []

        def vector(row):
            return table_ref[row : row + 1]

        def both(group):
            first = sum(len(g) for g in raw[:group])
            return sum(ref[...] for ref in raw_refs[first : first + len(raw[group])])

        middle, result, hidden = both(0), both(1), both(2)
        v_ref[...] = jnp.zeros_like(v_ref)
        v_ref[0:1] = vector(GAIN1)
        v_ref[1:2] = vector(SHIFT1)
        v_ref[2:3] = middle[0:1] / vector(SCALE_ATTN) * share
        v_ref[3:4] = middle[1:2] * vector(SCALE_ATTN) * share
        v_ref[4:6] = middle[2:4]
        v_ref[6:7] = result[0:1] + result[1:2] * vector(FC2_BIAS) * share
        v_ref[7:8] = result[1:2] * vector(SCALE_MLP) * share

        def spread(flats, first):
            stack = [f[:, i * head : (i + 1) * head] for f in flats for i in range(f.shape[1] // head)]
            stack = jnp.concatenate(stack, axis=0)
            for group in range(head // shard):
                piece = stack[:, group * shard : (group + 1) * shard]
                repeat = max(1, 128 // shard)
                piece = jnp.concatenate([piece] * repeat, axis=1)
                piece = jnp.concatenate([piece] * (width // (repeat * shard)), axis=1)
                v_ref[first : first + stack.shape[0]] = piece
                first += stack.shape[0]
            return first

        spread([hidden], spread([s_ref[0:1], s_ref[2:3]], 8))
        lane = lax.broadcasted_iota(jnp.int32, (block, extra), 1)
        for i in range(width // block):
            blk = slice(i * block, (i + 1) * block)
            columns = v_ref[:, blk].T
            first = second = None
            product = dot_tn(n_ref[:, blk], g_ref[...])
            for part in range(3):
                piece = product[:, part * local : (part + 1) * local]
                w = w_ref[part, blk].astype(F32)
                one = jnp.sum(w * piece, axis=1, keepdims=True)
                two = jnp.sum(w * s_ref[part : part + 1], axis=1, keepdims=True)
                first = one if first is None else first + one
                second = two if second is None else second + two
            gain_grad = (first - columns[:, 1:2] * second) / columns[:, 0:1]
            small = jnp.where(lane == 0, gain_grad, jnp.where(lane == 1, second, columns))
            product_p = None
            for c in range(chunks):
                term = dot_tn(a_refs[c][:, blk], m_refs[c][...])
                product_p = term if product_p is None else product_p + term
            for copy in stores[(i - 2) * radix : (i - 1) * radix] if i >= 2 else ():
                copy.wait()
            hold_ref[i % 2, :, :, :, :wide] = product.astype(BF16).reshape(groups, radix, shard, wide)
            hold_ref[i % 2, :, :, :, wide : wide + local] = product_p.astype(BF16).reshape(groups, radix, shard, local)
            hold_ref[i % 2, :, :, :, wide + local :] = small.astype(BF16).reshape(groups, radix, shard, extra)
            for step in range(radix):
                source = hold_ref.at[i % 2, :, lax.rem(place_ref[0] + step, radix)]
                stores.append(copies.start(source, out_hbm[step].at[pl.ds(i * groups, groups)]))
        for copy in stores[-2 * radix :]:
            copy.wait()

    return call(
        kernel,
        "attention_grads",
        [VMEM, VMEM] + [VMEM] * (2 * chunks + n_raw) + [VMEM, VMEM, VMEM, SMEM],
        [ANY] * radix,
        [pltpu.HBM((width // (radix * shard), shard, total), BF16)] * radix,
        (normed, grads, *grad_attn, *mixed, *flat_raw, weight, sums, table, place),
        after,
        scratch=[
            pltpu.VMEM((2, groups, radix, shard, total), BF16),
            pltpu.VMEM((extra, width), F32),
            pltpu.SemaphoreType.DMA((width // block * radix,)),
        ],
        ties=ties,
        bring=bring,
    )


def add_far_stage(ways, after, name, ties=()):
    sizes = [(len(way[0]), *way[0][0].shape[:2], way[2], way[3]) for way in ways]
    n_out = sum(size[4] for size in sizes)
    n_ways = len(ways)
    kept = [way[0][0] for way in ways]
    arrived = []
    for way in ways:
        arrived += [array for array in way[0][1:] if not any(array is other for other in arrived)]

    def kernel(*refs):
        hbm, refs = refs[:n_ways], refs[n_ways:]
        arrived_refs, place_refs, refs = refs[: len(arrived)], refs[len(arrived) :][:n_ways], refs[len(arrived) + n_ways :]
        out_hbm, refs = refs[:n_out], refs[n_out:]
        in_refs, out_refs, sems = refs[:n_ways], refs[n_ways : 2 * n_ways], refs[2 * n_ways]
        copies = Copies(sems)
        loads = []
        for w, (_, left, _, columns, radix) in enumerate(sizes):
            _, first, _, _, _, below = ways[w]
            span = radix * below
            loads.append(
                [
                    copies.start(
                        hbm[w].at[pl.ds(high * span, span), :, pl.ds(first, columns)],
                        in_refs[w].at[pl.ds(high * span, span)],
                    )
                    for high in range(left // span)
                ]
            )
        stores = []
        given = 0
        for w, (_, left, _, columns, radix) in enumerate(sizes):
            arrays, first, _, _, _, below = ways[w]
            others = [
                arrived_refs[next(i for i, other in enumerate(arrived) if other is array)] for array in arrays[1:]
            ]
            for group in range(left // radix):
                high, low = divmod(group, below)
                if low == 0:
                    loads[w][high].wait()
                for step in range(radix):
                    digit = lax.rem(place_refs[w][0] + step, radix)
                    source = (high * radix + digit) * below + low
                    total = in_refs[w][source].astype(F32)
                    for ref in others:
                        total = total + ref[source, :, first : first + columns].astype(F32)
                    out_refs[w][step, group] = total.astype(BF16)
                    stores.append(copies.start(out_refs[w].at[step, group], out_hbm[given + step].at[group]))
            given += radix
        for copy in stores:
            copy.wait()

    count = sum(left // (radix * way[5]) + left for (_, left, _, _, radix), way in zip(sizes, ways))
    out, done = call(
        kernel,
        name,
        [ANY] * n_ways + [VMEM] * len(arrived) + [SMEM] * n_ways,
        [ANY] * n_out,
        [pltpu.HBM((left // radix, rows, columns), BF16) for _, left, rows, columns, radix in sizes for _ in range(radix)],
        (*kept, *arrived, *[way[4] for way in ways]),
        after,
        scratch=[pltpu.VMEM((left, rows, columns), BF16) for _, left, rows, columns, _ in sizes]
        + [pltpu.VMEM((radix, left // radix, rows, columns), BF16) for _, left, rows, columns, radix in sizes]
        + [pltpu.SemaphoreType.DMA((count,))],
        ties=ties,
    )
    split = []
    for size in sizes:
        split.append(out[: size[4]])
        out = out[size[4] :]
    return split, done


def total_of(refs):
    total = None
    for ref in refs:
        term = ref[0].astype(F32)
        total = term if total is None else total + term
    return total


def last_stage(parts, local, after):
    _, shard, columns = parts[0].shape

    def kernel(*refs):
        part_refs, (qkv_ref, proj_ref, small_ref) = refs[:-3], refs[-3:]
        total = total_of(part_refs)
        for part in range(3):
            qkv_ref[part] = total[:, part * local : (part + 1) * local]
        proj_ref[...] = total[:, 3 * local : 4 * local]
        small_ref[...] = total[:, 4 * local :].T

    return call(
        kernel,
        "last_stage",
        [COPIED] + [VMEM] * (len(parts) - 1),
        [COPIED, COPIED, VMEM],
        [shape((3, shard, local), F32), shape((shard, local), F32), shape((columns - 4 * local, shard), F32)],
        tuple(parts),
        after,
    )


def last_far_stage(firsts, seconds, after):
    _, shard, units = firsts[0].shape
    n_second = len(seconds)

    def kernel(*refs):
        first_ref, second_ref = refs[-2:]
        first_ref[...] = total_of(refs[n_second:-2])
        second_ref[...] = total_of(refs[:n_second])

    return call(
        kernel,
        "last_far_stage",
        [COPIED] + [VMEM] * (n_second - 1) + [COPIED] + [VMEM] * (len(firsts) - 1),
        [COPIED] * 2,
        [shape((shard, units), F32), shape((shard, units), F32)],
        (*seconds, *firsts),
        after,
    )


def wait_for(arrays, after):
    def kernel():
        pass

    _, done = call(kernel, "wait_for", [], [], [], (), after, ties=arrays)
    return done


def middle_back(chunk, rows, terms, middle, tokens, cotangent, lengths, table, proj, after, bring):
    width = middle.shape[1]
    local = proj.shape[0]
    parts = len(terms)

    def kernel(*refs):
        term_refs, refs = refs[:parts], refs[parts:]
        mid_ref, x_hbm, c_hbm, lengths_ref, table_ref, p_ref = refs[:6]
        gmid_hbm, low_ref, gmix_ref, vec_ref, gmid_ref, x_ref, c_ref, sems = refs[6:]
        copies = Copies(sems)
        own = pl.ds(chunk * rows, rows)
        loads = [copies.start(c_hbm.at[own], c_ref), copies.start(x_hbm.at[own], x_ref)]
        grad_norm = None
        for ref in term_refs:
            term = ref[...].astype(F32)
            grad_norm = term if grad_norm is None else grad_norm + term
        middle = mid_ref[...]
        scaled, inverse = norm_parts(middle)
        back = norm_back(grad_norm, scaled, inverse, table_ref[GAIN2 : GAIN2 + 1])
        loads[0].wait()
        grad = c_ref[...].astype(F32) * valid_rows(lengths_ref, chunk * rows, rows) + back
        gmid_ref[...] = grad
        store = copies.start(gmid_ref, gmid_hbm)
        low = (table_ref[SCALE_ATTN : SCALE_ATTN + 1] * grad).astype(BF16)
        low_ref[...] = low
        gmix_ref[...] = dot_nt(low, p_ref[...]).astype(BF16)
        loads[1].wait()
        vec_ref[0:1] = col_sum(grad * (middle - x_ref[...].astype(F32)))
        vec_ref[1:2] = col_sum(grad)
        own = term_refs[0][...].astype(F32)
        vec_ref[2:3] = col_sum(own * scaled)
        vec_ref[3:4] = col_sum(own)
        store.wait()

    return call(
        kernel,
        f"middle_back_{chunk}",
        [VMEM] * parts + [VMEM, ANY, ANY, SMEM, VMEM, VMEM],
        [ANY] + [VMEM] * 3,
        [
            pltpu.HBM((rows, width), F32),
            shape((rows, width), BF16),
            shape((rows, local), BF16),
            shape((4, width), F32),
        ],
        (*terms, middle, tokens, cotangent, lengths, table, proj),
        after,
        scratch=[
            pltpu.VMEM((rows, width), F32),
            pltpu.VMEM((rows, width), BF16),
            pltpu.VMEM((rows, width), BF16),
            pltpu.SemaphoreType.DMA((3,)),
        ],
        bring=bring,
    )


def first_norm_terms(chunks, grads, weight, after):
    width, local = weight.shape[1:]
    rows = grads.shape[0] // chunks

    def kernel(g_ref, w_hbm, *refs):
        out_refs, (w_ref, sems) = refs[:chunks], refs[chunks:]
        copies = Copies(sems)
        loads = [copies.start(w_hbm.at[part], w_ref.at[part]) for part in range(3)]
        for chunk in range(chunks):
            place = slice(chunk * rows, (chunk + 1) * rows)
            total = None
            for part in range(3):
                if chunk == 0:
                    loads[part].wait()
                term = dot_nt(g_ref[place, part * local : (part + 1) * local], w_ref[part])
                total = term if total is None else total + term
            out_refs[chunk][...] = total.astype(BF16)

    return call(
        kernel,
        "first_norm_terms",
        [VMEM, ANY],
        [VMEM] * chunks,
        [shape((rows, width), BF16)] * chunks,
        (grads, weight),
        after,
        scratch=[pltpu.VMEM(weight.shape, BF16), pltpu.SemaphoreType.DMA((3,))],
    )


def to_rows(chunk, rows, compute, args, specs, dims, kept, after, name, sources=(), ties=()):
    extra = 0 if kept is None else 1
    blocks = 2
    block = rows // blocks
    n_args = len(args)
    n_source = len(sources)
    args, specs = args + tuple(array for array, _ in sources), specs + [ANY] * n_source

    def kernel(*refs):
        ins, refs = refs[:n_args], refs[n_args:]
        source_hbm, refs = refs[:n_source], refs[n_source:]
        out_hbm, hold_ref, sems = refs[extra : extra + 3]
        source_refs = refs[extra + 3 :]
        copies = Copies(sems)
        loads = [
            [
                copies.start(hbm.at[pl.ds(first + i * block, block)], ref.at[i])
                for hbm, ref, (_, first) in zip(source_hbm, source_refs, sources)
            ]
            for i in range(blocks)
        ]
        stores = []
        for i in range(blocks):
            for load in loads[i]:
                load.wait()
            hold_ref[i] = compute(i * block, block, *[ref[i] for ref in source_refs], *ins).astype(BF16)
            place = pl.ds(chunk * rows + i * block, block)
            stores.append(copies.start(hold_ref.at[i], out_hbm.at[place]))
        for copy in stores:
            copy.wait()

    alias = None
    if extra:
        alias = {len(args): 0}
        args = args + (kept,)
    scratch = [
        pltpu.VMEM((blocks, block, dims[1]), BF16),
        pltpu.SemaphoreType.DMA(((1 + n_source) * blocks,)),
        *[pltpu.VMEM((blocks, block, dims[1]), array.dtype) for array, _ in sources],
    ]
    return call(
        kernel,
        name,
        specs + [ANY] * extra,
        ANY,
        pltpu.HBM(dims, BF16),
        args,
        after,
        scratch=scratch,
        alias=alias,
        ties=ties,
    )


def token_grads(chunk, rows, terms, grad_middle, tokens, table, kept, after):
    parts = len(terms)

    def compute(first, block, x, grad, *refs):
        table_ref = refs[parts]
        place = slice(first, first + block)
        grad_norm = None
        for ref in refs[:parts]:
            term = ref[place].astype(F32)
            grad_norm = term if grad_norm is None else grad_norm + term
        scaled, inverse = norm_parts(x.astype(F32))
        return grad + norm_back(grad_norm, scaled, inverse, table_ref[GAIN1 : GAIN1 + 1])

    args = (*terms, table)
    specs = [VMEM] * (parts + 1)
    sources = ((tokens, chunk * rows), (grad_middle, 0))
    return to_rows(chunk, rows, compute, args, specs, tokens.shape, kept, after, f"token_grads_{chunk}", sources)


def layer_output(chunk, rows, terms, middle, lengths, table, dims, kept, after):
    parts = len(terms)

    def compute(first, block, mid, *refs):
        lengths_ref, table_ref = refs[parts:]
        mlp = table_ref[FC2_BIAS : FC2_BIAS + 1]
        for term in refs[:parts]:
            mlp = mlp + term.astype(F32)
        valid = valid_rows(lengths_ref, chunk * rows + first, block)
        return valid * (mid + table_ref[SCALE_MLP : SCALE_MLP + 1] * mlp)

    sources = ((middle, 0), *((term, 0) for term in terms))
    name = f"layer_output_{chunk}"
    return to_rows(chunk, rows, compute, (lengths, table), [SMEM, VMEM], dims, kept, after, name, sources)


def from_peers(array):
    size = lax.axis_size("tensor")
    return [
        lax.ppermute(array, "tensor", [(i, (i + step) % size) for i in range(size)])
        for step in range(1, size)
    ]


def other_of_pair(array):
    return lax.ppermute(array, "dp", [(i, i ^ 1) for i in range(lax.axis_size("dp"))])


def radices(size):
    found = []
    if size % 2 == 0:
        found.append(2)
        size //= 2
    while size > 1:
        step = 2 if size % 4 and size % 2 == 0 or size == 8 else next((r for r in (4, 3) if size % r == 0), size)
        found.append(step)
        size //= step
    return found


def small_digits(size, stride):
    digits = []
    while stride < size:
        left = size // stride
        radix = next(r for r in (2, 3, 5, left) if left % r == 0)
        digits.append((stride, radix))
        stride *= radix
    return digits


def exchange(parts, stride, radix):
    size = lax.axis_size("dp")
    arrived = []
    for step in range(1, radix):
        moves = []
        for i in range(size):
            at = (i // stride) % radix
            moves.append((i, i + ((at + step) % radix - at) * stride))
        arrived.append(lax.ppermute(parts[step], "dp", moves))
    return [parts[0]] + arrived


def body(
    tokens,
    lengths,
    norm1_gain,
    norm1_bias,
    qkv_weight,
    qv_bias,
    proj_weight,
    proj_bias,
    scale_attn,
    norm2_gain,
    norm2_bias,
    fc1_weight,
    fc1_bias,
    fc2_weight,
    fc2_bias,
    scale_mlp,
    cotangent,
):
    count, width = tokens.shape
    heads, head_size = qv_bias.shape[1:]
    local = heads * head_size
    units = fc1_weight.shape[1]
    tensor = lax.axis_size("tensor")
    dp = lax.axis_size("dp")
    chunks = 2
    rows = count // chunks
    scale = head_size**-0.5

    def flat(vector):
        return vector.reshape(1, -1)

    index = lax.axis_index("dp")
    steps = radices(dp)
    strides = [1]
    for step in steps:
        strides.append(strides[-1] * step)
    places = [((index // stride) % step).reshape(1) for stride, step in zip(strides, steps)]

    half_rows = local // 2
    paired = dp % 2 == 0 and half_rows % 128 == 0
    half_place = (index % 2).reshape(1)
    half = proj_weight
    if paired:
        half = lax.dynamic_slice_in_dim(proj_weight, half_place[0] * half_rows, half_rows, 0)
    halves = from_peers(half)
    vectors = (norm1_gain, norm1_bias, norm2_gain, norm2_bias, proj_bias, scale_attn, fc2_bias, scale_mlp)
    out, done = attend_forward(
        tokens,
        lengths,
        [flat(vector) for vector in vectors],
        qkv_weight,
        qv_bias,
        scale,
        rows,
        (cotangent, fc2_weight, proj_weight, fc1_weight),
    )
    queries, keys, values, normed1, *near, table, cotangent_near, fc2_near, proj_weight, fc1_weight = out[:12]
    first, rest = out[12:]
    mixed_parts = [[first] + from_peers(first)]
    rest, done = attend_rest(*near, rest, lengths, done)
    mixed_parts.append([rest] + from_peers(rest))
    mixed = [first, rest]
    out, done = hidden_cotangent(cotangent_near, lengths, table, fc2_near, halves, chunks, done)
    grad_mlp, grad_act, halves = out[0], out[1 : 1 + chunks], out[1 + chunks :]
    if paired:
        halves = [part for half in halves for part in (half, other_of_pair(half))]

    middle, normed2, activated, grad_hidden, norm2_parts = [], [], [], [], []
    raw = [[], [], []]
    for chunk in range(chunks):
        out, done = feed_forward(
            chunk,
            rows,
            mixed_parts[chunk],
            proj_weight,
            halves,
            half_place,
            tokens,
            grad_act[chunk],
            table,
            fc1_weight,
            flat(fc1_bias),
            done,
        )
        for group, part in zip((middle, normed2, activated, grad_hidden), out[:4]):
            group.append(part)
        raw[2].append(out[4])
        norm2_parts.append([out[5]] + from_peers(out[5]))

    shard = width // dp
    fc_parts, done = weight_grads(
        normed2, grad_hidden, grad_mlp, activated, places[0], steps[0], shard, done
    )
    fc_parts = exchange(fc_parts, 1, steps[0])

    def near_stage(parts, stage, done):
        way = (parts, 0, parts[0].shape[2], steps[stage], places[stage], 1)
        (parts,), done = add_far_stage([way], done, f"add_stage_{stage}")
        return exchange(parts, strides[stage], steps[stage]), done

    out, done = second_projection(activated, fc2_weight, cotangent, lengths, done, middle)
    mlp_parts = [[terms] + from_peers(terms) for terms in out[:chunks]]
    raw[1].append(out[chunks])
    middle_near = out[chunks + 1 :]

    grad_middle, grad_attn, grad_mixed = [], [], []
    for chunk in range(chunks):
        out, done = middle_back(
            chunk,
            rows,
            norm2_parts[chunk],
            middle_near[chunk],
            tokens,
            cotangent,
            lengths,
            table,
            proj_weight,
            done,
            (queries, keys, values) if chunk == 0 else (),
        )
        if chunk == 0:
            queries, keys, values = out[4:]
        for group, part in zip((grad_middle, grad_attn, grad_mixed), out[:3]):
            group.append(part)
        raw[0].append(out[3])
    stages = len(steps)
    digits = small_digits(dp, strides[1])
    orders = [digits, digits[1:] + digits[:1]]

    def far_stage(at, firsts, seconds, start, done, ties=()):
        ways = []
        for arrays, first, order in ((firsts, 0, orders[0]), (seconds, start, orders[1])):
            stride, radix = order[at]
            below = 1
            for other_stride, other_radix in order[at:]:
                below *= other_radix if other_stride < stride else 1
            place = ((index // stride) % radix).reshape(1)
            ways.append((arrays, first, units, radix, place, below))
        split, done = add_far_stage(ways, done, f"add_far_stage_{at}", ties)
        return [exchange(parts, *order[at]) for parts, order in zip(split, orders)], done

    (firsts, seconds), done = far_stage(0, fc_parts, fc_parts, units, done)
    (grads, grad_sums, qkv_near, normed1), done = attend_backward(
        queries, keys, values, grad_mixed, lengths, scale, done, (qkv_weight, normed1)
    )
    parts, done = attention_grads(
        normed1,
        grads,
        grad_attn,
        mixed,
        qkv_near,
        grad_sums,
        table,
        raw,
        1.0 / tensor,
        places[0],
        steps[0],
        shard,
        done,
        mlp_parts[0][1:],
        (),
    )
    parts = exchange(parts, 1, steps[0])
    if len(digits) > 1:
        (firsts, seconds), done = far_stage(1, firsts, seconds, 0, done)
    terms, done = first_norm_terms(chunks, grads, qkv_weight, done)
    norm1_parts = [[part] + from_peers(part) for part in terms]
    done = wait_for([part for group in mlp_parts[1:] for part in group[1:]], done)
    if stages > 1:
        parts, done = near_stage(parts, 1, done)
    output = None
    for chunk in range(chunks):
        output, done = layer_output(
            chunk, rows, mlp_parts[chunk], middle[chunk], lengths, table, tokens.shape, output, done
        )
    for at in range(2, len(digits)):
        (firsts, seconds), done = far_stage(at, firsts, seconds, 0, done)
    grad_tokens = None
    for chunk in range(chunks - 1):
        grad_tokens, done = token_grads(
            chunk, rows, norm1_parts[chunk], grad_middle[chunk], tokens, table, grad_tokens, done
        )
    for stage in range(2, stages):
        parts, done = near_stage(parts, stage, done)
    (fc1_grad, fc2_grad), done = last_far_stage(firsts, seconds, done)
    grad_tokens, done = token_grads(
        chunks - 1, rows, norm1_parts[-1], grad_middle[-1], tokens, table, grad_tokens, done
    )
    (qkv_grad, proj_grad, small), done = last_stage(parts, local, done)

    vector_share = small[:8]
    for other in from_peers(vector_share):
        vector_share = vector_share + other
    own = shard // tensor
    vector_share = lax.dynamic_slice_in_dim(vector_share, lax.axis_index("tensor") * own, own, 1)

    def columns_of(first, heads_in):
        groups = head_size // shard
        pieces = [small[first + i * heads_in : first + (i + 1) * heads_in] for i in range(groups)]
        every = pieces[0] if groups == 1 else jnp.concatenate(pieces, axis=1)
        return lax.dynamic_slice_in_dim(every, index * (head_size // dp), head_size // dp, 1)

    bias_share = columns_of(8, 2 * heads).reshape(2, heads, -1)
    fc1_share = columns_of(8 + 2 * heads * (head_size // shard), units // head_size)

    return (
        output,
        grad_tokens,
        vector_share[0],
        vector_share[1],
        qkv_grad,
        bias_share,
        proj_grad.T,
        vector_share[3],
        vector_share[2],
        vector_share[4],
        vector_share[5],
        fc1_grad,
        fc1_share,
        fc2_grad.T,
        vector_share[7],
        vector_share[6],
    )


def solution(mesh):
    in_specs = (
        P("dp", None),
        P("dp", None),
        P(),
        P(),
        P(None, None, "tensor"),
        P(None, "tensor", None),
        P("tensor", None),
        P(),
        P(),
        P(),
        P(),
        P(None, "tensor"),
        P("tensor"),
        P("tensor", None),
        P(),
        P(),
        P("dp", None),
    )
    out_specs = (
        P("dp", None),
        P("dp", None),
        P(("dp", "tensor")),
        P(("dp", "tensor")),
        P(None, "dp", "tensor"),
        P(None, "tensor", "dp"),
        P("tensor", "dp"),
        P(("dp", "tensor")),
        P(("dp", "tensor")),
        P(("dp", "tensor")),
        P(("dp", "tensor")),
        P("dp", "tensor"),
        P("tensor", "dp"),
        P("tensor", "dp"),
        P(("dp", "tensor")),
        P(("dp", "tensor")),
    )
    return jax.shard_map(body, mesh=mesh, in_specs=in_specs, out_specs=out_specs, check_vma=False)
```

```python
from functools import partial

import jax
import jax.numpy as jnp
from jax import lax
from jax.experimental import pallas as pl
from jax.experimental.pallas import tpu as pltpu
from jax.sharding import PartitionSpec as P

EPS = 1e-06
NEGATIVE = -1e30
GLOBAL_LEN = 197
LOCAL_LEN = 37
GROUP = GLOBAL_LEN // LOCAL_LEN
WINDOW = 224
BF16 = jnp.bfloat16
F32 = jnp.float32
MIB = 1 << 20
VMEM_MIB = 16
SPARE = 6
LIMITS = {
    "attend_forward": 14,
    "attend_rest": 6,
    "hidden_cotangent": 6,
    "feed_forward": 15,
    "weight_grads": 17,
    "second_projection": 18,
    "middle_back": 15,
    "attend_backward": 11,
    "attention_grads": 14,
    "layer_output": 13,
    "first_norm_terms": 9,
    "add_stage": 8,
    "token_grads": 9,
    "last_stage": 8,
    "last_far_stage": 8,
    "wait_for": 1,
    "add_far_stage": 16,
}
COST = 2300000000
COSTS = {"middle_back_1": 46000000000, "wait_for": 16100000000, "token_grads_0": 13800000000}


def dot_nn(a, b):
    return lax.dot_general(a, b, (((1,), (0,)), ((), ())), preferred_element_type=F32)


def dot_nt(a, b):
    return lax.dot_general(a, b, (((1,), (1,)), ((), ())), preferred_element_type=F32)


def dot_tn(a, b):
    return lax.dot_general(a, b, (((0,), (0,)), ((), ())), preferred_element_type=F32)


def norm_parts(values):
    average = jnp.mean(values, axis=-1, keepdims=True)
    centered = values - average
    inverse = lax.rsqrt(jnp.mean(centered * centered, axis=-1, keepdims=True) + EPS)
    return centered * inverse, inverse


def norm_back(grad_norm, scaled, inverse, gain):
    grad_hat = grad_norm * gain
    first_mean = jnp.mean(grad_hat, axis=-1, keepdims=True)
    second_mean = jnp.mean(grad_hat * scaled, axis=-1, keepdims=True)
    return inverse * (grad_hat - first_mean - scaled * second_mean)


def col_sum(values):
    return jnp.sum(values, axis=0, keepdims=True)


def call(kernel, name, in_specs, out_specs, out_shape, args, after=None, scratch=(), vmem=VMEM_MIB, alias=None, bring=(), late=False, ties=()):
    single = not isinstance(out_shape, list)
    if single:
        out_specs, out_shape = [out_specs], [out_shape]
    n_in, n_out, n_bring = len(args), len(out_shape), len(bring)
    after = list(ties) if after is None else [after, *ties]
    n_after = len(after)
    args = [
        pltpu.with_memory_space_constraint(arg, pltpu.VMEM if spec is VMEM else pltpu.HBM)
        if spec is VMEM or spec is ANY
        else arg
        for arg, spec in zip(args, in_specs)
    ]
    args += [pltpu.with_memory_space_constraint(arg, pltpu.HBM) for arg in bring]
    out_shape = [
        pltpu.VMEM(o.shape, o.dtype) if spec is VMEM else o for o, spec in zip(out_shape, out_specs)
    ]

    def ordered(*refs):
        ins, refs = refs[:n_in], refs[n_in:]
        bring_hbm, refs = refs[:n_bring], refs[n_bring + n_after :]
        outs, refs = refs[:n_out], refs[n_out:]
        bring_refs, done, refs = refs[:n_bring], refs[n_bring], refs[n_bring + 1 :]
        done[...] = jnp.zeros_like(done)
        loads = []
        if n_bring:
            refs, sems = refs[:-1], refs[-1]

        def begin():
            for i in range(n_bring):
                loads.append(pltpu.make_async_copy(bring_hbm[i], bring_refs[i], sems.at[i]))
                loads[-1].start()

        if late:
            kernel(begin, *ins, *outs, *refs)
        else:
            begin()
            kernel(*ins, *outs, *refs)
        for load in loads:
            load.wait()

    out = pl.pallas_call(
        ordered,
        in_specs=list(in_specs) + [ANY] * (n_bring + n_after),
        out_specs=list(out_specs) + [VMEM] * (n_bring + 1),
        out_shape=list(out_shape) + [pltpu.VMEM(a.shape, a.dtype) for a in bring] + [pltpu.VMEM((8, 128), F32)],
        scratch_shapes=list(scratch) + ([pltpu.SemaphoreType.DMA((n_bring,))] if n_bring else []),
        input_output_aliases=alias or {},
        compiler_params=pltpu.CompilerParams(vmem_limit_bytes=(LIMITS.get(name.rstrip("_0123456789"), vmem) + SPARE) * MIB),
        cost_estimate=pl.CostEstimate(flops=COSTS.get(name, COST), bytes_accessed=COST, transcendentals=0),
        name=name,
    )(*args, *after)
    return (out[0] if single and not n_bring else out[:-1]), out[-1]


class Copies:
    def __init__(self, sems):
        self.sems = sems
        self.used = 0

    def start(self, source, target):
        copy = pltpu.make_async_copy(source, target, self.sems.at[self.used])
        self.used += 1
        copy.start()
        return copy


def shape(dims, dtype):
    return jax.ShapeDtypeStruct(dims, dtype)


SMEM = pl.BlockSpec(memory_space=pltpu.SMEM)
VMEM = pl.BlockSpec(memory_space=pltpu.VMEM)
ANY = pl.BlockSpec(memory_space=pl.ANY)
COPIED = pl.BlockSpec(memory_space=pltpu.VMEM)

GAIN1, SHIFT1, GAIN2, SHIFT2, PROJ_BIAS, SCALE_ATTN, FC2_BIAS, SCALE_MLP = range(8)


def row_total(lengths_ref):
    total = jnp.int32(0)
    for slot in range(lengths_ref.shape[1]):
        total = total + lengths_ref[0, slot]
    return total


def valid_rows(lengths_ref, first, rows):
    places = lax.broadcasted_iota(jnp.int32, (rows, 1), 0) + first
    return (places < row_total(lengths_ref)).astype(F32)


def item_counts(lengths_ref):
    globals_ = jnp.int32(0)
    locals_ = jnp.int32(0)
    for slot in range(lengths_ref.shape[1]):
        value = lengths_ref[0, slot]
        globals_ = globals_ + jnp.where(value == GLOBAL_LEN, 1, 0)
        locals_ = locals_ + jnp.where(value == LOCAL_LEN, 1, 0)
    return globals_, locals_


def item_place(item, globals_, locals_, count):
    is_global = item < globals_
    group = item - globals_
    start = jnp.where(
        is_global, item * GLOBAL_LEN, globals_ * GLOBAL_LEN + group * (GROUP * LOCAL_LEN)
    )
    length = jnp.where(
        is_global, GLOBAL_LEN, jnp.minimum(locals_ - group * GROUP, GROUP) * LOCAL_LEN
    )
    crop = jnp.where(is_global, GLOBAL_LEN, LOCAL_LEN)
    first = jnp.minimum((start // 16) * 16, count - WINDOW)
    return pl.multiple_of(first, 16), start - first, length, crop


def crop_of(places, offset, length, crop, outside):
    inside = (places >= offset) & (places < offset + length)
    index = places - offset
    label = jnp.zeros_like(places)
    for step in range(1, GROUP):
        label = label + jnp.where(index >= step * crop, 1, 0)
    return jnp.where(inside, label, outside)


def item_total(globals_, locals_):
    return globals_ + (locals_ + GROUP - 1) // GROUP


def attend_items(first_item, last_item, q_ref, k_ref, v_ref, out_ref, skipped, lengths_ref):
    count, local = q_ref.shape
    pair = 128
    pairs = local // pair
    globals_, locals_ = item_counts(lengths_ref)
    low_half = lax.broadcasted_iota(jnp.int32, (1, pair), 1) < pair // 2

    def step(item, carry):
        first, offset, length, crop = item_place(item, globals_, locals_, count)
        window = pl.ds(first, WINDOW)
        placed = pl.ds(pl.multiple_of(first - skipped, 16), WINDOW)
        by_key = lax.broadcasted_iota(jnp.int32, (WINDOW, 1), 0)
        by_query = lax.broadcasted_iota(jnp.int32, (1, WINDOW), 1)
        query_crop = crop_of(by_query, offset, length, crop, -2)
        key_crop = crop_of(by_key, offset, length, crop, -1)
        mask = jnp.where(query_crop == key_crop, 0.0, NEGATIVE)
        inside = key_crop >= 0

        def products(index):
            columns = slice(index * pair, (index + 1) * pair)
            return dot_nt(heads_apart(k_ref[window, columns], low_half), q_ref[window, columns])

        now = products(0)
        for index in range(pairs):
            columns = slice(index * pair, (index + 1) * pair)
            later = products(index + 1) if index + 1 < pairs else None
            scores = now.reshape(2, WINDOW, WINDOW) + mask
            weights = jnp.exp(scores - jnp.max(scores, axis=1, keepdims=True))
            total = jnp.sum(weights, axis=1, keepdims=True)
            low = (weights * (1.0 / total)).astype(BF16).reshape(2 * WINDOW, WINDOW)
            out = dot_tn(low, heads_apart(v_ref[window, columns], low_half))
            now = later
            kept = out_ref[placed, columns].astype(F32)
            out_ref[placed, columns] = jnp.where(inside, out, kept).astype(BF16)
        return carry

    lax.fori_loop(first_item, jnp.minimum(last_item, item_total(globals_, locals_)), step, 0)


def attend_forward(tokens, lengths, vectors, weight, qv_bias, scale, rows, later):
    count, width = tokens.shape
    local = weight.shape[2]
    head = 64
    block = 256
    blocks = count // block
    n_vec, n_later = len(vectors), len(later)

    def kernel(x_hbm, w_hbm, *refs):
        later_hbm, refs = refs[:n_later], refs[n_later:]
        vec_hbm, refs = refs[:n_vec], refs[n_vec:]
        qv_hbm, lengths_ref, refs = refs[0], refs[1], refs[2:]
        q_hbm, k_hbm, v_hbm, n_hbm, q_ref, k_ref, v_ref, table_ref, refs = *refs[:8], refs[8:]
        later_refs, (first_ref, rest_ref), refs = refs[:n_later], refs[n_later : n_later + 2], refs[n_later + 2 :]
        vec_refs, refs = refs[:n_vec], refs[n_vec:]
        heads_ref, x_ref, w_ref, n_ref, out_ref, sems = refs
        copies = Copies(sems)

        def part(ref, index):
            return ref.at[pl.ds(index * block, block)]

        loads = [copies.start(part(x_hbm, 0), part(x_ref, 0))]
        small_loads = [copies.start(hbm, ref) for hbm, ref in zip(vec_hbm[:2], vec_refs[:2])]
        weight_loads = [copies.start(w_hbm.at[0], w_ref.at[0])]
        small_loads.append(copies.start(qv_hbm, heads_ref))
        weight_loads += [copies.start(w_hbm.at[i], w_ref.at[i]) for i in range(1, 3)]
        loads += [copies.start(part(x_hbm, i), part(x_ref, i)) for i in range(1, blocks)]
        table_loads = [copies.start(hbm, ref) for hbm, ref in zip(vec_hbm[2:], vec_refs[2:])]
        later_loads = []

        def scaled_of(i):
            loads[i].wait()
            return norm_parts(x_ref[i * block : (i + 1) * block].astype(F32))[0]

        def normed_of(i):
            return (scaled_of(i) * vec_refs[GAIN1][...] + vec_refs[SHIFT1][...]).astype(BF16)

        scaled = scaled_of(0)
        for load in small_loads:
            load.wait()
        qv = [
            jnp.concatenate([heads_ref[i, h : h + 1] for h in range(local // head)], axis=1)
            for i in range(2)
        ]
        now = (scaled * vec_refs[GAIN1][...] + vec_refs[SHIFT1][...]).astype(BF16)
        for i in range(blocks):
            rows_i = slice(i * block, (i + 1) * block)
            after = normed_of(i + 1) if i + 1 < blocks else None
            n_ref[rows_i] = now
            if i == 0:
                weight_loads[0].wait()
            queries = (dot_nn(now, w_ref[0]) + qv[0]).astype(BF16)
            q_ref[rows_i] = queries * BF16(scale)
            if i == 0:
                weight_loads[1].wait()
            k_ref[rows_i] = dot_nn(now, w_ref[1]).astype(BF16)
            if i == 0:
                weight_loads[2].wait()
            v_ref[rows_i] = (dot_nn(now, w_ref[2]) + qv[1]).astype(BF16)
            now = after
            if i == 0:
                later_loads += [copies.start(hbm, ref) for hbm, ref in zip(later_hbm, later_refs)]
        stores = [
            copies.start(ref, hbm)
            for ref, hbm in ((q_ref, q_hbm), (k_ref, k_hbm), (v_ref, v_hbm), (n_ref, n_hbm))
        ]
        average = col_sum(v_ref[...].astype(F32)) * (1.0 / count)
        out_ref[...] = jnp.broadcast_to(average, (count, local)).astype(BF16)
        attend_items(0, first_items(rows), q_ref, k_ref, v_ref, out_ref, 0, lengths_ref)
        first_ref[...] = out_ref[:rows]
        rest_ref[...] = out_ref[rows:]
        for load in table_loads:
            load.wait()
        for i in range(n_vec):
            table_ref[i : i + 1] = vec_refs[i][...]
        for copy in later_loads + stores:
            copy.wait()

    part = pltpu.HBM((count, local), BF16)
    near = shape((count, local), BF16)
    outs = [part, part, part, pltpu.HBM((count, width), BF16), near, near, near, shape((n_vec, width), F32)]
    outs += [shape(a.shape, a.dtype) for a in later] + [shape((rows, local), BF16), shape((count - rows, local), BF16)]
    args = (tokens, weight, *later, *vectors, qv_bias, lengths)
    return call(
        kernel,
        "attend_forward",
        [ANY] * (len(args) - 1) + [SMEM],
        [ANY] * 4 + [VMEM] * (len(outs) - 4),
        outs,
        args,
        scratch=[pltpu.VMEM((1, width), F32)] * n_vec
        + [
            pltpu.VMEM(qv_bias.shape, F32),
            pltpu.VMEM((count, width), BF16),
            pltpu.VMEM(weight.shape, BF16),
            pltpu.VMEM((count, width), BF16),
            pltpu.VMEM((count, local), BF16),
            pltpu.SemaphoreType.DMA((blocks + 8 + n_later + n_vec,)),
        ],
    )


def first_items(rows):
    return -(-rows // (GROUP * LOCAL_LEN))


def attend_rest(queries, keys, values, rest, lengths, after):
    rows = queries.shape[0] - rest.shape[0]

    def kernel(q_ref, k_ref, v_ref, rest_ref, lengths_ref, out_ref):
        out_ref[...] = rest_ref[...]
        attend_items(first_items(rows), 1 << 20, q_ref, k_ref, v_ref, out_ref, rows, lengths_ref)

    return call(
        kernel,
        "attend_rest",
        [VMEM] * 4 + [SMEM],
        VMEM,
        shape(rest.shape, BF16),
        (queries, keys, values, rest, lengths),
        after,
    )


def heads_apart(both, low_half):
    return jnp.concatenate([jnp.where(low_half, both, BF16(0)), jnp.where(low_half, BF16(0), both)], axis=0)


def heads_together(apart, low_half):
    return jnp.where(low_half, apart[:WINDOW], apart[WINDOW:])


def attend_backward(queries, keys, values, grad_mixed, lengths, scale, after, bring):
    count, local = queries.shape
    head = 64
    pair = 2 * head

    chunks = len(grad_mixed)
    rows = count // chunks

    def kernel(q_ref, k_ref, v_ref, *refs):
        chunk_refs, refs = refs[:chunks], refs[chunks:]
        lengths_ref, out_ref, bias_ref, acc_ref, g_ref = refs
        for chunk in range(chunks):
            g_ref[chunk * rows : (chunk + 1) * rows] = chunk_refs[chunk][...]
        globals_, locals_ = item_counts(lengths_ref)
        acc_ref[...] = jnp.zeros_like(acc_ref)
        low_half = lax.broadcasted_iota(jnp.int32, (1, pair), 1) < head

        def step(item, carry):
            first, offset, length, crop = item_place(item, globals_, locals_, count)
            window = pl.ds(first, WINDOW)
            by_key = lax.broadcasted_iota(jnp.int32, (WINDOW, 1), 0)
            by_query = lax.broadcasted_iota(jnp.int32, (1, WINDOW), 1)
            query_crop = crop_of(by_query, offset, length, crop, -2)
            key_crop = crop_of(by_key, offset, length, crop, -1)
            mask = jnp.where(query_crop == key_crop, 0.0, NEGATIVE)
            inside = key_crop >= 0
            def products(index):
                columns = slice(index * pair, (index + 1) * pair)
                q2 = q_ref[window, columns]
                g2 = jnp.where(inside, g_ref[window, columns], BF16(0))
                both_k = heads_apart(k_ref[window, columns], low_half)
                both_v = heads_apart(v_ref[window, columns], low_half)
                return q2, g2, both_k, dot_nt(both_k, q2), dot_nt(both_v, g2)

            pairs = local // pair
            now = products(0)
            for index in range(pairs):
                columns = slice(index * pair, (index + 1) * pair)
                later = products(index + 1) if index + 1 < pairs else None
                q2, g2, both_k, scores, grad_probability = now
                now = later
                scores = scores.reshape(2, WINDOW, WINDOW) + mask
                weights = jnp.exp(scores - jnp.max(scores, axis=1, keepdims=True))
                total = jnp.sum(weights, axis=1, keepdims=True)
                probability = weights * (1.0 / total)
                grad_probability = grad_probability.reshape(2, WINDOW, WINDOW)
                delta = jnp.sum(probability * grad_probability, axis=1, keepdims=True)
                grad_scores = (probability * (grad_probability - delta)).astype(BF16)
                grad_scores = grad_scores.reshape(2 * WINDOW, WINDOW)
                low = probability.astype(BF16).reshape(2 * WINDOW, WINDOW)
                grad_v = heads_together(dot_nn(low, g2), low_half)
                grad_k = heads_together(dot_nn(grad_scores, q2), low_half)
                grad_q = dot_tn(grad_scores, both_k)
                acc_ref[0, window, columns] += grad_q * scale
                acc_ref[1, window, columns] += grad_k
                acc_ref[2, window, columns] += grad_v
            return carry

        lax.fori_loop(0, item_total(globals_, locals_), step, 0)
        for part in range(3):
            out_ref[:, part * local : (part + 1) * local] = acc_ref[part].astype(BF16)
            bias_ref[part : part + 1] = col_sum(acc_ref[part])

    return call(
        kernel,
        "attend_backward",
        [VMEM, VMEM, VMEM] + [VMEM] * chunks + [SMEM],
        [VMEM, VMEM],
        [shape((count, 3 * local), BF16), shape((3, local), F32)],
        (queries, keys, values, *grad_mixed, lengths),
        after,
        scratch=[pltpu.VMEM((3, count, local), F32), pltpu.VMEM((count, local), BF16)],
        bring=bring,
    )


def gelu_parts(value):
    size = jnp.abs(value)
    bell = jnp.exp(value * value * -0.5)
    t = 1.0 / (1.0 + size * (0.3275911 * 0.7071067811865476))
    poly = t * (
        0.254829592
        + t * (-0.284496736 + t * (1.421413741 + t * (-1.453152027 + t * 1.061405429)))
    )
    tail = 0.5 * poly * bell
    share = jnp.where(value >= 0, 1.0 - tail, tail)
    return value * share, share + value * (bell * 0.3989422804014327)


def hidden_cotangent(cotangent, lengths, table, fc2, halves, chunks, after):
    count, width = cotangent.shape
    units = fc2.shape[0]
    rows = count // chunks
    n_half = len(halves)

    def kernel(c_ref, w_ref, table_ref, lengths_ref, *refs):
        half_refs, refs = refs[:n_half], refs[n_half:]
        gm_hbm, ga_refs, on_refs = refs[0], refs[1 : 1 + chunks], refs[1 + chunks : 1 + chunks + n_half]
        gm_ref, sems = refs[1 + chunks + n_half :]
        copies = Copies(sems)
        stores = []
        for half_ref, on_ref in zip(half_refs, on_refs):
            on_ref[...] = half_ref[...]
        for chunk in range(chunks):
            place = chunk * rows
            grad = c_ref[place : place + rows].astype(F32) * valid_rows(lengths_ref, place, rows)
            low = (grad * table_ref[SCALE_MLP : SCALE_MLP + 1]).astype(BF16)
            gm_ref[place : place + rows] = low
            own = pl.ds(place, rows)
            stores.append(copies.start(gm_ref.at[own], gm_hbm.at[own]))
            ga_refs[chunk][...] = dot_nt(low, w_ref[...]).astype(BF16)
        for copy in stores:
            copy.wait()

    return call(
        kernel,
        "hidden_cotangent",
        [VMEM, VMEM, VMEM, SMEM] + [VMEM] * n_half,
        [ANY] + [VMEM] * (chunks + n_half),
        [pltpu.HBM((count, width), BF16)]
        + [shape((rows, units), BF16)] * chunks
        + [shape(half.shape, BF16) for half in halves],
        (cotangent, fc2, table, lengths, *halves),
        after,
        scratch=[pltpu.VMEM((count, width), BF16), pltpu.SemaphoreType.DMA((chunks,))],
    )


def feed_forward(chunk, rows, mixed, proj, halves, place, tokens, grad_act, table, fc1, fc1_bias, after):
    width = tokens.shape[1]
    units = fc1.shape[1]
    step_units = min(512, units)
    steps = units // step_units
    parts = len(mixed)
    n_half = len(halves)
    depth = proj.shape[0] // 2

    def kernel(*refs):
        mixed_refs, p_ref, half_refs, refs = refs[:parts], refs[parts], refs[parts + 1 : parts + 1 + n_half], refs[parts + 1 + n_half :]
        place_ref, x_hbm, ga_ref, table_ref, fc1_ref, fb_ref = refs[:6]
        mid_hbm, n2_hbm, act_hbm, gh_hbm, fbg_ref, terms_ref, refs = *refs[6:12], refs[12:]
        mid_ref, n2_ref, act_ref, gh_ref, x_ref, sems = refs
        copies = Copies(sems)
        load = copies.start(x_hbm.at[pl.ds(chunk * rows, rows)], x_ref)

        def vector(row):
            return table_ref[row : row + 1]

        attn = vector(PROJ_BIAS) + dot_nn(mixed_refs[0][...], p_ref[...]).astype(BF16).astype(F32)
        for peer in range(parts - 1):
            m_ref = mixed_refs[peer + 1]
            if n_half == parts - 1:
                term = dot_nn(m_ref[...], half_refs[peer][...])
            else:
                first = pl.ds(pl.multiple_of(place_ref[0] * depth, depth), depth)
                other = pl.ds(pl.multiple_of((1 - place_ref[0]) * depth, depth), depth)
                term = dot_nn(m_ref[:, first], half_refs[2 * peer][...])
                term = term + dot_nn(m_ref[:, other], half_refs[2 * peer + 1][...])
            attn = attn + term.astype(BF16).astype(F32)
        load.wait()
        middle = x_ref[...].astype(F32) + vector(SCALE_ATTN) * attn
        mid_ref[...] = middle
        stores = [copies.start(mid_ref, mid_hbm)]
        scaled, _ = norm_parts(middle)
        n2_ref[...] = (scaled * vector(GAIN2) + vector(SHIFT2)).astype(BF16)
        stores.append(copies.start(n2_ref, n2_hbm))

        def hidden_of(j):
            units_j = slice(j * step_units, (j + 1) * step_units)
            return dot_nn(n2_ref[...], fc1_ref[:, units_j]) + fb_ref[:, units_j]

        total = None
        hidden = hidden_of(0)
        for j in range(steps):
            units_j = slice(j * step_units, (j + 1) * step_units)
            later = hidden_of(j + 1) if j + 1 < steps else None
            activated, slope = gelu_parts(hidden)
            own = pl.ds(j * step_units, step_units)
            act_ref[:, units_j] = activated.astype(BF16)
            stores.append(copies.start(act_ref.at[:, own], act_hbm.at[:, own]))
            grad_hidden = ga_ref[:, units_j].astype(F32) * slope
            fbg_ref[:, units_j] = col_sum(grad_hidden)
            low = grad_hidden.astype(BF16)
            gh_ref[:, units_j] = low
            stores.append(copies.start(gh_ref.at[:, own], gh_hbm.at[:, own]))
            term = dot_nt(low, fc1_ref[:, units_j])
            total = term if total is None else total + term
            hidden = later
        terms_ref[...] = total.astype(BF16)
        for copy in stores:
            copy.wait()

    args = (*mixed, proj, *halves, place, tokens, grad_act, table, fc1, fc1_bias)
    return call(
        kernel,
        "feed_forward",
        [VMEM] * (parts + 1 + n_half) + [SMEM, ANY] + [VMEM] * 3 + [COPIED],
        [ANY] * 4 + [VMEM] * 2,
        [
            pltpu.HBM((rows, width), F32),
            pltpu.HBM((rows, width), BF16),
            pltpu.HBM((rows, units), BF16),
            pltpu.HBM((rows, units), BF16),
            shape((1, units), F32),
            shape((rows, width), BF16),
        ],
        args,
        after,
        scratch=[
            pltpu.VMEM((rows, width), F32),
            pltpu.VMEM((rows, width), BF16),
            pltpu.VMEM((rows, units), BF16),
            pltpu.VMEM((rows, units), BF16),
            pltpu.VMEM((rows, width), BF16),
            pltpu.SemaphoreType.DMA((3 + 2 * steps,)),
        ],
    )


def second_projection(activated, fc2, cotangent, lengths, after, bring):
    units, width = fc2.shape
    chunks = len(activated)
    rows = activated[0].shape[0]
    block = min(512, units)
    steps = units // block

    def kernel(begin, *refs):
        a_hbm, refs = refs[:chunks], refs[chunks:]
        w_hbm, c_hbm, lengths_ref, refs = refs[0], refs[1], refs[2], refs[3:]
        out_hbm, vec_ref, refs = refs[:chunks], refs[chunks], refs[chunks + 1 :]
        a_refs, (w_ref, c_ref, out_ref, sems) = refs[:chunks], refs[chunks:]
        stores = []
        copies = Copies(sems)
        loads = []
        for j in range(steps):
            own = pl.ds(j * block, block)
            loads.append([copies.start(w_hbm.at[own], w_ref.at[own])])
            loads[j].append(copies.start(a_hbm[0].at[:, own], a_refs[0].at[:, own]))
        late = [copies.start(hbm, ref) for hbm, ref in zip(a_hbm[1:], a_refs[1:])]
        late.append(copies.start(c_hbm, c_ref))
        begin()
        for chunk in range(chunks):
            total = None
            if chunk == 0:
                for j in range(steps):
                    for load in loads[j]:
                        load.wait()
                    place = slice(j * block, (j + 1) * block)
                    term = dot_nn(a_refs[0][:, place], w_ref[place])
                    total = term if total is None else total + term
                for load in late:
                    load.wait()
            else:
                total = dot_nn(a_refs[chunk][...], w_ref[...])
            terms = total.astype(BF16)
            place = slice(chunk * rows, (chunk + 1) * rows)
            out_ref[place] = terms
            stores.append(copies.start(out_ref.at[pl.ds(chunk * rows, rows)], out_hbm[chunk]))
            grad = c_ref[place].astype(F32) * valid_rows(lengths_ref, chunk * rows, rows)
            first, second = col_sum(grad * terms.astype(F32)), col_sum(grad)
            vec_ref[0:1] = first if chunk == 0 else vec_ref[0:1] + first
            vec_ref[1:2] = second if chunk == 0 else vec_ref[1:2] + second
        for copy in stores:
            copy.wait()

    return call(
        kernel,
        "second_projection",
        [ANY] * (chunks + 2) + [SMEM],
        [ANY] * chunks + [VMEM],
        [pltpu.HBM((rows, width), BF16)] * chunks + [shape((2, width), F32)],
        (*activated, fc2, cotangent, lengths),
        after,
        scratch=[pltpu.VMEM((rows, units), BF16)] * chunks
        + [
            pltpu.VMEM(fc2.shape, BF16),
            pltpu.VMEM(cotangent.shape, BF16),
            pltpu.VMEM(cotangent.shape, BF16),
            pltpu.SemaphoreType.DMA((2 * steps + 2 * chunks,)),
        ],
        bring=bring,
        late=True,
    )


def weight_grads(normed, grad_hidden, grad_mlp, activated, place, radix, shard, after):
    width = normed[0].shape[1]
    chunks = len(normed)
    rows = normed[0].shape[0]
    units = activated[0].shape[1]
    block = min(512, units)
    slots = 2
    steps = 2 * units // block
    half = steps // 2
    groups = width // (radix * shard)

    def kernel(*refs):
        n_hbm, h_hbm, a_hbm = refs[:chunks], refs[chunks : 2 * chunks], refs[2 * chunks : 3 * chunks]
        g_hbm, place_ref, refs = refs[3 * chunks], refs[3 * chunks + 1], refs[3 * chunks + 2 :]
        out_hbm, (n_ref, g_ref, right_ref, hold_ref, sems) = refs[:radix], refs[radix:]
        copies = Copies(sems)

        def rows_of(chunk):
            return pl.ds(chunk * rows, rows)

        loads = [[] for _ in range(steps)]
        for c in range(chunks):
            loads[0].append(copies.start(n_hbm[c], n_ref.at[rows_of(c)]))
        for step in range(steps):
            own = pl.ds(step % half * block, block)
            if step == half:
                loads[step].append(copies.start(g_hbm, g_ref))
            for c in range(chunks):
                source = (h_hbm if step < half else a_hbm)[c].at[:, own]
                loads[step].append(copies.start(source, right_ref.at[step, rows_of(c)]))
        flying = [[] for _ in range(slots)]
        for step in range(steps):
            for load in loads[step]:
                load.wait()
            total = dot_tn((n_ref if step < half else g_ref)[...], right_ref[step])
            slot = step % slots
            for copy in flying[slot]:
                copy.wait()
            hold_ref[slot] = total.astype(BF16).reshape(groups, radix, shard, block)
            columns = pl.ds(step * block, block)
            flying[slot] = [
                copies.start(
                    hold_ref.at[slot, :, lax.rem(place_ref[0] + part, radix)], out_hbm[part].at[:, :, columns]
                )
                for part in range(radix)
            ]
        for group in flying:
            for copy in group:
                copy.wait()

    return call(
        kernel,
        "weight_grads",
        [ANY] * (3 * chunks + 1) + [SMEM],
        [ANY] * radix,
        [pltpu.HBM((groups, shard, 2 * units), BF16)] * radix,
        (*normed, *grad_hidden, *activated, grad_mlp, place),
        after,
        scratch=[
            pltpu.VMEM((chunks * rows, width), BF16),
            pltpu.VMEM((chunks * rows, width), BF16),
            pltpu.VMEM((steps, chunks * rows, block), BF16),
            pltpu.VMEM((slots, groups, radix, shard, block), BF16),
            pltpu.SemaphoreType.DMA((chunks + 1 + (chunks + radix) * steps,)),
        ],
    )


def attention_grads(normed, grads, grad_attn, mixed, weight, sums, table, raw, share, place, radix, shard, after, ties, bring):
    count, width = normed.shape
    block = max(256, radix * shard)
    wide, local = grads.shape[1], mixed[0].shape[1]
    extra = 128
    total = wide + local + extra
    groups = block // (radix * shard)
    chunks = len(mixed)
    head = 64
    flat_raw = [part for group in raw for part in group]
    n_raw = len(flat_raw)

    def kernel(n_ref, g_ref, *refs):
        a_refs, m_refs, refs = refs[:chunks], refs[chunks : 2 * chunks], refs[2 * chunks :]
        raw_refs, refs = refs[:n_raw], refs[n_raw:]
        w_ref, s_ref, table_ref, place_ref = refs[:4]
        out_hbm, (hold_ref, v_ref, sems) = refs[4 : 4 + radix], refs[4 + radix :]
        copies = Copies(sems)
        stores = []

        def vector(row):
            return table_ref[row : row + 1]

        def both(group):
            first = sum(len(g) for g in raw[:group])
            return sum(ref[...] for ref in raw_refs[first : first + len(raw[group])])

        middle, result, hidden = both(0), both(1), both(2)
        v_ref[...] = jnp.zeros_like(v_ref)
        v_ref[0:1] = vector(GAIN1)
        v_ref[1:2] = vector(SHIFT1)
        v_ref[2:3] = middle[0:1] / vector(SCALE_ATTN) * share
        v_ref[3:4] = middle[1:2] * vector(SCALE_ATTN) * share
        v_ref[4:6] = middle[2:4]
        v_ref[6:7] = result[0:1] + result[1:2] * vector(FC2_BIAS) * share
        v_ref[7:8] = result[1:2] * vector(SCALE_MLP) * share

        def spread(flats, first):
            stack = [f[:, i * head : (i + 1) * head] for f in flats for i in range(f.shape[1] // head)]
            stack = jnp.concatenate(stack, axis=0)
            for group in range(head // shard):
                piece = stack[:, group * shard : (group + 1) * shard]
                repeat = max(1, 128 // shard)
                piece = jnp.concatenate([piece] * repeat, axis=1)
                piece = jnp.concatenate([piece] * (width // (repeat * shard)), axis=1)
                v_ref[first : first + stack.shape[0]] = piece
                first += stack.shape[0]
            return first

        spread([hidden], spread([s_ref[0:1], s_ref[2:3]], 8))
        lane = lax.broadcasted_iota(jnp.int32, (block, extra), 1)
        for i in range(width // block):
            blk = slice(i * block, (i + 1) * block)
            columns = v_ref[:, blk].T
            first = second = None
            product = dot_tn(n_ref[:, blk], g_ref[...])
            for part in range(3):
                piece = product[:, part * local : (part + 1) * local]
                w = w_ref[part, blk].astype(F32)
                one = jnp.sum(w * piece, axis=1, keepdims=True)
                two = jnp.sum(w * s_ref[part : part + 1], axis=1, keepdims=True)
                first = one if first is None else first + one
                second = two if second is None else second + two
            gain_grad = (first - columns[:, 1:2] * second) / columns[:, 0:1]
            small = jnp.where(lane == 0, gain_grad, jnp.where(lane == 1, second, columns))
            product_p = None
            for c in range(chunks):
                term = dot_tn(a_refs[c][:, blk], m_refs[c][...])
                product_p = term if product_p is None else product_p + term
            for copy in stores[(i - 2) * radix : (i - 1) * radix] if i >= 2 else ():
                copy.wait()
            hold_ref[i % 2, :, :, :, :wide] = product.astype(BF16).reshape(groups, radix, shard, wide)
            hold_ref[i % 2, :, :, :, wide : wide + local] = product_p.astype(BF16).reshape(groups, radix, shard, local)
            hold_ref[i % 2, :, :, :, wide + local :] = small.astype(BF16).reshape(groups, radix, shard, extra)
            for step in range(radix):
                source = hold_ref.at[i % 2, :, lax.rem(place_ref[0] + step, radix)]
                stores.append(copies.start(source, out_hbm[step].at[pl.ds(i * groups, groups)]))
        for copy in stores[-2 * radix :]:
            copy.wait()

    return call(
        kernel,
        "attention_grads",
        [VMEM, VMEM] + [VMEM] * (2 * chunks + n_raw) + [VMEM, VMEM, VMEM, SMEM],
        [ANY] * radix,
        [pltpu.HBM((width // (radix * shard), shard, total), BF16)] * radix,
        (normed, grads, *grad_attn, *mixed, *flat_raw, weight, sums, table, place),
        after,
        scratch=[
            pltpu.VMEM((2, groups, radix, shard, total), BF16),
            pltpu.VMEM((extra, width), F32),
            pltpu.SemaphoreType.DMA((width // block * radix,)),
        ],
        ties=ties,
        bring=bring,
    )


def add_far_stage(ways, after, name, ties=()):
    sizes = [(len(way[0]), *way[0][0].shape[:2], way[2], way[3]) for way in ways]
    n_out = sum(size[4] for size in sizes)
    n_ways = len(ways)
    kept = [way[0][0] for way in ways]
    arrived = []
    for way in ways:
        arrived += [array for array in way[0][1:] if not any(array is other for other in arrived)]

    def kernel(*refs):
        hbm, refs = refs[:n_ways], refs[n_ways:]
        arrived_refs, place_refs, refs = refs[: len(arrived)], refs[len(arrived) :][:n_ways], refs[len(arrived) + n_ways :]
        out_hbm, refs = refs[:n_out], refs[n_out:]
        in_refs, out_refs, sems = refs[:n_ways], refs[n_ways : 2 * n_ways], refs[2 * n_ways]
        copies = Copies(sems)
        loads = []
        for w, (_, left, _, columns, radix) in enumerate(sizes):
            _, first, _, _, _, below = ways[w]
            span = radix * below
            loads.append(
                [
                    copies.start(
                        hbm[w].at[pl.ds(high * span, span), :, pl.ds(first, columns)],
                        in_refs[w].at[pl.ds(high * span, span)],
                    )
                    for high in range(left // span)
                ]
            )
        stores = []
        given = 0
        for w, (_, left, _, columns, radix) in enumerate(sizes):
            arrays, first, _, _, _, below = ways[w]
            others = [
                arrived_refs[next(i for i, other in enumerate(arrived) if other is array)] for array in arrays[1:]
            ]
            for group in range(left // radix):
                high, low = divmod(group, below)
                if low == 0:
                    loads[w][high].wait()
                for step in range(radix):
                    digit = lax.rem(place_refs[w][0] + step, radix)
                    source = (high * radix + digit) * below + low
                    total = in_refs[w][source].astype(F32)
                    for ref in others:
                        total = total + ref[source, :, first : first + columns].astype(F32)
                    out_refs[w][step, group] = total.astype(BF16)
                    stores.append(copies.start(out_refs[w].at[step, group], out_hbm[given + step].at[group]))
            given += radix
        for copy in stores:
            copy.wait()

    count = sum(left // (radix * way[5]) + left for (_, left, _, _, radix), way in zip(sizes, ways))
    out, done = call(
        kernel,
        name,
        [ANY] * n_ways + [VMEM] * len(arrived) + [SMEM] * n_ways,
        [ANY] * n_out,
        [pltpu.HBM((left // radix, rows, columns), BF16) for _, left, rows, columns, radix in sizes for _ in range(radix)],
        (*kept, *arrived, *[way[4] for way in ways]),
        after,
        scratch=[pltpu.VMEM((left, rows, columns), BF16) for _, left, rows, columns, _ in sizes]
        + [pltpu.VMEM((radix, left // radix, rows, columns), BF16) for _, left, rows, columns, radix in sizes]
        + [pltpu.SemaphoreType.DMA((count,))],
        ties=ties,
    )
    split = []
    for size in sizes:
        split.append(out[: size[4]])
        out = out[size[4] :]
    return split, done


def total_of(refs):
    total = None
    for ref in refs:
        term = ref[0].astype(F32)
        total = term if total is None else total + term
    return total


def last_stage(parts, local, after):
    _, shard, columns = parts[0].shape

    def kernel(*refs):
        part_refs, (qkv_ref, proj_ref, small_ref) = refs[:-3], refs[-3:]
        total = total_of(part_refs)
        for part in range(3):
            qkv_ref[part] = total[:, part * local : (part + 1) * local]
        proj_ref[...] = total[:, 3 * local : 4 * local]
        small_ref[...] = total[:, 4 * local :].T

    return call(
        kernel,
        "last_stage",
        [COPIED] + [VMEM] * (len(parts) - 1),
        [COPIED, COPIED, VMEM],
        [shape((3, shard, local), F32), shape((shard, local), F32), shape((columns - 4 * local, shard), F32)],
        tuple(parts),
        after,
    )


def last_far_stage(firsts, seconds, after):
    _, shard, units = firsts[0].shape
    n_second = len(seconds)

    def kernel(*refs):
        first_ref, second_ref = refs[-2:]
        first_ref[...] = total_of(refs[n_second:-2])
        second_ref[...] = total_of(refs[:n_second])

    return call(
        kernel,
        "last_far_stage",
        [COPIED] + [VMEM] * (n_second - 1) + [COPIED] + [VMEM] * (len(firsts) - 1),
        [COPIED] * 2,
        [shape((shard, units), F32), shape((shard, units), F32)],
        (*seconds, *firsts),
        after,
    )


def wait_for(arrays, after):
    def kernel():
        pass

    _, done = call(kernel, "wait_for", [], [], [], (), after, ties=arrays)
    return done


def middle_back(chunk, rows, terms, middle, tokens, cotangent, lengths, table, proj, after, bring):
    width = middle.shape[1]
    local = proj.shape[0]
    parts = len(terms)

    def kernel(*refs):
        term_refs, refs = refs[:parts], refs[parts:]
        mid_ref, x_hbm, c_hbm, lengths_ref, table_ref, p_ref = refs[:6]
        gmid_hbm, low_ref, gmix_ref, vec_ref, gmid_ref, x_ref, c_ref, sems = refs[6:]
        copies = Copies(sems)
        own = pl.ds(chunk * rows, rows)
        loads = [copies.start(c_hbm.at[own], c_ref), copies.start(x_hbm.at[own], x_ref)]
        grad_norm = None
        for ref in term_refs:
            term = ref[...].astype(F32)
            grad_norm = term if grad_norm is None else grad_norm + term
        middle = mid_ref[...]
        scaled, inverse = norm_parts(middle)
        back = norm_back(grad_norm, scaled, inverse, table_ref[GAIN2 : GAIN2 + 1])
        loads[0].wait()
        grad = c_ref[...].astype(F32) * valid_rows(lengths_ref, chunk * rows, rows) + back
        gmid_ref[...] = grad
        store = copies.start(gmid_ref, gmid_hbm)
        low = (table_ref[SCALE_ATTN : SCALE_ATTN + 1] * grad).astype(BF16)
        low_ref[...] = low
        gmix_ref[...] = dot_nt(low, p_ref[...]).astype(BF16)
        loads[1].wait()
        vec_ref[0:1] = col_sum(grad * (middle - x_ref[...].astype(F32)))
        vec_ref[1:2] = col_sum(grad)
        own = term_refs[0][...].astype(F32)
        vec_ref[2:3] = col_sum(own * scaled)
        vec_ref[3:4] = col_sum(own)
        store.wait()

    return call(
        kernel,
        f"middle_back_{chunk}",
        [VMEM] * parts + [VMEM, ANY, ANY, SMEM, VMEM, VMEM],
        [ANY] + [VMEM] * 3,
        [
            pltpu.HBM((rows, width), F32),
            shape((rows, width), BF16),
            shape((rows, local), BF16),
            shape((4, width), F32),
        ],
        (*terms, middle, tokens, cotangent, lengths, table, proj),
        after,
        scratch=[
            pltpu.VMEM((rows, width), F32),
            pltpu.VMEM((rows, width), BF16),
            pltpu.VMEM((rows, width), BF16),
            pltpu.SemaphoreType.DMA((3,)),
        ],
        bring=bring,
    )


def first_norm_terms(chunks, grads, weight, after):
    width, local = weight.shape[1:]
    rows = grads.shape[0] // chunks

    def kernel(g_ref, w_hbm, *refs):
        out_refs, (w_ref, sems) = refs[:chunks], refs[chunks:]
        copies = Copies(sems)
        loads = [copies.start(w_hbm.at[part], w_ref.at[part]) for part in range(3)]
        for chunk in range(chunks):
            place = slice(chunk * rows, (chunk + 1) * rows)
            total = None
            for part in range(3):
                if chunk == 0:
                    loads[part].wait()
                term = dot_nt(g_ref[place, part * local : (part + 1) * local], w_ref[part])
                total = term if total is None else total + term
            out_refs[chunk][...] = total.astype(BF16)

    return call(
        kernel,
        "first_norm_terms",
        [VMEM, ANY],
        [VMEM] * chunks,
        [shape((rows, width), BF16)] * chunks,
        (grads, weight),
        after,
        scratch=[pltpu.VMEM(weight.shape, BF16), pltpu.SemaphoreType.DMA((3,))],
    )


def to_rows(chunk, rows, compute, args, specs, dims, kept, after, name, sources=(), ties=()):
    extra = 0 if kept is None else 1
    blocks = 2
    block = rows // blocks
    n_args = len(args)
    n_source = len(sources)
    args, specs = args + tuple(array for array, _ in sources), specs + [ANY] * n_source

    def kernel(*refs):
        ins, refs = refs[:n_args], refs[n_args:]
        source_hbm, refs = refs[:n_source], refs[n_source:]
        out_hbm, hold_ref, sems = refs[extra : extra + 3]
        source_refs = refs[extra + 3 :]
        copies = Copies(sems)
        loads = [
            [
                copies.start(hbm.at[pl.ds(first + i * block, block)], ref.at[i])
                for hbm, ref, (_, first) in zip(source_hbm, source_refs, sources)
            ]
            for i in range(blocks)
        ]
        stores = []
        for i in range(blocks):
            for load in loads[i]:
                load.wait()
            hold_ref[i] = compute(i * block, block, *[ref[i] for ref in source_refs], *ins).astype(BF16)
            place = pl.ds(chunk * rows + i * block, block)
            stores.append(copies.start(hold_ref.at[i], out_hbm.at[place]))
        for copy in stores:
            copy.wait()

    alias = None
    if extra:
        alias = {len(args): 0}
        args = args + (kept,)
    scratch = [
        pltpu.VMEM((blocks, block, dims[1]), BF16),
        pltpu.SemaphoreType.DMA(((1 + n_source) * blocks,)),
        *[pltpu.VMEM((blocks, block, dims[1]), array.dtype) for array, _ in sources],
    ]
    return call(
        kernel,
        name,
        specs + [ANY] * extra,
        ANY,
        pltpu.HBM(dims, BF16),
        args,
        after,
        scratch=scratch,
        alias=alias,
        ties=ties,
    )


def token_grads(chunk, rows, terms, grad_middle, tokens, table, kept, after):
    parts = len(terms)

    def compute(first, block, x, grad, *refs):
        table_ref = refs[parts]
        place = slice(first, first + block)
        grad_norm = None
        for ref in refs[:parts]:
            term = ref[place].astype(F32)
            grad_norm = term if grad_norm is None else grad_norm + term
        scaled, inverse = norm_parts(x.astype(F32))
        return grad + norm_back(grad_norm, scaled, inverse, table_ref[GAIN1 : GAIN1 + 1])

    args = (*terms, table)
    specs = [VMEM] * (parts + 1)
    sources = ((tokens, chunk * rows), (grad_middle, 0))
    return to_rows(chunk, rows, compute, args, specs, tokens.shape, kept, after, f"token_grads_{chunk}", sources)


def layer_output(chunk, rows, terms, middle, lengths, table, dims, kept, after):
    parts = len(terms)

    def compute(first, block, mid, *refs):
        lengths_ref, table_ref = refs[parts:]
        mlp = table_ref[FC2_BIAS : FC2_BIAS + 1]
        for term in refs[:parts]:
            mlp = mlp + term.astype(F32)
        valid = valid_rows(lengths_ref, chunk * rows + first, block)
        return valid * (mid + table_ref[SCALE_MLP : SCALE_MLP + 1] * mlp)

    sources = ((middle, 0), *((term, 0) for term in terms))
    name = f"layer_output_{chunk}"
    return to_rows(chunk, rows, compute, (lengths, table), [SMEM, VMEM], dims, kept, after, name, sources)


def from_peers(array):
    size = lax.axis_size("tensor")
    return [
        lax.ppermute(array, "tensor", [(i, (i + step) % size) for i in range(size)])
        for step in range(1, size)
    ]


def other_of_pair(array):
    return lax.ppermute(array, "dp", [(i, i ^ 1) for i in range(lax.axis_size("dp"))])


def radices(size):
    found = []
    if size % 2 == 0:
        found.append(2)
        size //= 2
    while size > 1:
        step = 2 if size % 4 and size % 2 == 0 or size == 8 else next((r for r in (4, 3) if size % r == 0), size)
        found.append(step)
        size //= step
    return found


def small_digits(size, stride):
    digits = []
    while stride < size:
        left = size // stride
        radix = next(r for r in (2, 3, 5, left) if left % r == 0)
        digits.append((stride, radix))
        stride *= radix
    return digits


def exchange(parts, stride, radix):
    size = lax.axis_size("dp")
    arrived = []
    for step in range(1, radix):
        moves = []
        for i in range(size):
            at = (i // stride) % radix
            moves.append((i, i + ((at + step) % radix - at) * stride))
        arrived.append(lax.ppermute(parts[step], "dp", moves))
    return [parts[0]] + arrived


def body(
    tokens,
    lengths,
    norm1_gain,
    norm1_bias,
    qkv_weight,
    qv_bias,
    proj_weight,
    proj_bias,
    scale_attn,
    norm2_gain,
    norm2_bias,
    fc1_weight,
    fc1_bias,
    fc2_weight,
    fc2_bias,
    scale_mlp,
    cotangent,
):
    count, width = tokens.shape
    heads, head_size = qv_bias.shape[1:]
    local = heads * head_size
    units = fc1_weight.shape[1]
    tensor = lax.axis_size("tensor")
    dp = lax.axis_size("dp")
    chunks = 2
    rows = count // chunks
    scale = head_size**-0.5

    def flat(vector):
        return vector.reshape(1, -1)

    index = lax.axis_index("dp")
    steps = radices(dp)
    strides = [1]
    for step in steps:
        strides.append(strides[-1] * step)
    places = [((index // stride) % step).reshape(1) for stride, step in zip(strides, steps)]

    half_rows = local // 2
    paired = dp % 2 == 0 and half_rows % 128 == 0
    half_place = (index % 2).reshape(1)
    half = proj_weight
    if paired:
        half = lax.dynamic_slice_in_dim(proj_weight, half_place[0] * half_rows, half_rows, 0)
    halves = from_peers(half)
    vectors = (norm1_gain, norm1_bias, norm2_gain, norm2_bias, proj_bias, scale_attn, fc2_bias, scale_mlp)
    out, done = attend_forward(
        tokens,
        lengths,
        [flat(vector) for vector in vectors],
        qkv_weight,
        qv_bias,
        scale,
        rows,
        (cotangent, fc2_weight, proj_weight, fc1_weight),
    )
    queries, keys, values, normed1, *near, table, cotangent_near, fc2_near, proj_weight, fc1_weight = out[:12]
    first, rest = out[12:]
    mixed_parts = [[first] + from_peers(first)]
    rest, done = attend_rest(*near, rest, lengths, done)
    mixed_parts.append([rest] + from_peers(rest))
    mixed = [first, rest]
    out, done = hidden_cotangent(cotangent_near, lengths, table, fc2_near, halves, chunks, done)
    grad_mlp, grad_act, halves = out[0], out[1 : 1 + chunks], out[1 + chunks :]
    if paired:
        halves = [part for half in halves for part in (half, other_of_pair(half))]

    middle, normed2, activated, grad_hidden, norm2_parts = [], [], [], [], []
    raw = [[], [], []]
    for chunk in range(chunks):
        out, done = feed_forward(
            chunk,
            rows,
            mixed_parts[chunk],
            proj_weight,
            halves,
            half_place,
            tokens,
            grad_act[chunk],
            table,
            fc1_weight,
            flat(fc1_bias),
            done,
        )
        for group, part in zip((middle, normed2, activated, grad_hidden), out[:4]):
            group.append(part)
        raw[2].append(out[4])
        norm2_parts.append([out[5]] + from_peers(out[5]))

    shard = width // dp
    fc_parts, done = weight_grads(
        normed2, grad_hidden, grad_mlp, activated, places[0], steps[0], shard, done
    )
    fc_parts = exchange(fc_parts, 1, steps[0])

    def near_stage(parts, stage, done):
        way = (parts, 0, parts[0].shape[2], steps[stage], places[stage], 1)
        (parts,), done = add_far_stage([way], done, f"add_stage_{stage}")
        return exchange(parts, strides[stage], steps[stage]), done

    out, done = second_projection(activated, fc2_weight, cotangent, lengths, done, middle)
    mlp_parts = [[terms] + from_peers(terms) for terms in out[:chunks]]
    raw[1].append(out[chunks])
    middle_near = out[chunks + 1 :]

    grad_middle, grad_attn, grad_mixed = [], [], []
    for chunk in range(chunks):
        out, done = middle_back(
            chunk,
            rows,
            norm2_parts[chunk],
            middle_near[chunk],
            tokens,
            cotangent,
            lengths,
            table,
            proj_weight,
            done,
            (queries, keys, values) if chunk == 0 else (),
        )
        if chunk == 0:
            queries, keys, values = out[4:]
        for group, part in zip((grad_middle, grad_attn, grad_mixed), out[:3]):
            group.append(part)
        raw[0].append(out[3])
    stages = len(steps)
    digits = small_digits(dp, strides[1])
    orders = [digits, digits[1:] + digits[:1]]

    def far_stage(at, firsts, seconds, start, done, ties=()):
        ways = []
        for arrays, first, order in ((firsts, 0, orders[0]), (seconds, start, orders[1])):
            stride, radix = order[at]
            below = 1
            for other_stride, other_radix in order[at:]:
                below *= other_radix if other_stride < stride else 1
            place = ((index // stride) % radix).reshape(1)
            ways.append((arrays, first, units, radix, place, below))
        split, done = add_far_stage(ways, done, f"add_far_stage_{at}", ties)
        return [exchange(parts, *order[at]) for parts, order in zip(split, orders)], done

    (firsts, seconds), done = far_stage(0, fc_parts, fc_parts, units, done)
    (grads, grad_sums, qkv_near, normed1), done = attend_backward(
        queries, keys, values, grad_mixed, lengths, scale, done, (qkv_weight, normed1)
    )
    parts, done = attention_grads(
        normed1,
        grads,
        grad_attn,
        mixed,
        qkv_near,
        grad_sums,
        table,
        raw,
        1.0 / tensor,
        places[0],
        steps[0],
        shard,
        done,
        mlp_parts[0][1:],
        (),
    )
    parts = exchange(parts, 1, steps[0])
    if len(digits) > 1:
        (firsts, seconds), done = far_stage(1, firsts, seconds, 0, done)
    terms, done = first_norm_terms(chunks, grads, qkv_weight, done)
    norm1_parts = [[part] + from_peers(part) for part in terms]
    done = wait_for([part for group in mlp_parts[1:] for part in group[1:]], done)
    if stages > 1:
        parts, done = near_stage(parts, 1, done)
    output = None
    for chunk in range(chunks):
        output, done = layer_output(
            chunk, rows, mlp_parts[chunk], middle[chunk], lengths, table, tokens.shape, output, done
        )
    for at in range(2, len(digits)):
        (firsts, seconds), done = far_stage(at, firsts, seconds, 0, done)
    grad_tokens = None
    for chunk in range(chunks - 1):
        grad_tokens, done = token_grads(
            chunk, rows, norm1_parts[chunk], grad_middle[chunk], tokens, table, grad_tokens, done
        )
    for stage in range(2, stages):
        parts, done = near_stage(parts, stage, done)
    (fc1_grad, fc2_grad), done = last_far_stage(firsts, seconds, done)
    grad_tokens, done = token_grads(
        chunks - 1, rows, norm1_parts[-1], grad_middle[-1], tokens, table, grad_tokens, done
    )
    (qkv_grad, proj_grad, small), done = last_stage(parts, local, done)

    vector_share = small[:8]
    for other in from_peers(vector_share):
        vector_share = vector_share + other
    own = shard // tensor
    vector_share = lax.dynamic_slice_in_dim(vector_share, lax.axis_index("tensor") * own, own, 1)

    def columns_of(first, heads_in):
        groups = head_size // shard
        pieces = [small[first + i * heads_in : first + (i + 1) * heads_in] for i in range(groups)]
        every = pieces[0] if groups == 1 else jnp.concatenate(pieces, axis=1)
        return lax.dynamic_slice_in_dim(every, index * (head_size // dp), head_size // dp, 1)

    bias_share = columns_of(8, 2 * heads).reshape(2, heads, -1)
    fc1_share = columns_of(8 + 2 * heads * (head_size // shard), units // head_size)

    return (
        output,
        grad_tokens,
        vector_share[0],
        vector_share[1],
        qkv_grad,
        bias_share,
        proj_grad.T,
        vector_share[3],
        vector_share[2],
        vector_share[4],
        vector_share[5],
        fc1_grad,
        fc1_share,
        fc2_grad.T,
        vector_share[7],
        vector_share[6],
    )


def solution(mesh):
    in_specs = (
        P("dp", None),
        P("dp", None),
        P(),
        P(),
        P(None, None, "tensor"),
        P(None, "tensor", None),
        P("tensor", None),
        P(),
        P(),
        P(),
        P(),
        P(None, "tensor"),
        P("tensor"),
        P("tensor", None),
        P(),
        P(),
        P("dp", None),
    )
    out_specs = (
        P("dp", None),
        P("dp", None),
        P(("dp", "tensor")),
        P(("dp", "tensor")),
        P(None, "dp", "tensor"),
        P(None, "tensor", "dp"),
        P("tensor", "dp"),
        P(("dp", "tensor")),
        P(("dp", "tensor")),
        P(("dp", "tensor")),
        P(("dp", "tensor")),
        P("dp", "tensor"),
        P("tensor", "dp"),
        P("tensor", "dp"),
        P(("dp", "tensor")),
        P(("dp", "tensor")),
    )
    return jax.shard_map(body, mesh=mesh, in_specs=in_specs, out_specs=out_specs, check_vma=False)
```
